32 devices in a mesh: ctx: 16 (over z, y, x), head: 2 (over core).
Axes of the slice: x: 2, y: 2, z: 4, core: 2. Of those that a mesh axis runs over, the one named last changes fastest.
Arguments:
- hidden_in: bfloat16 [2048, 2304], P('ctx'), may hold values from -6 to 6
- out_cotangent: bfloat16 [2048, 2304], P('ctx'), may hold values from -6 to 6
- block_table: int32 [16, 2], replicated, may hold values from 0 to 31, as said below
- attend_weight: float32 [2304, 4, 4, 256], P('ctx', 'head'), may hold values from -0.1875 to 0.1875
- attend_moment: float32 [2304, 4, 4, 256], P('ctx', 'head'), may hold values from -14.934095 to 14.934095
- attend_square: float32 [2304, 4, 4, 256], P('ctx', 'head'), may hold values from 26.624 to 108.544
- output_weight: float32 [8, 256, 2304], P('head', None, 'ctx'), may hold values from -0.25 to 0.25
- output_moment: float32 [8, 256, 2304], P('head', None, 'ctx'), may hold values from -14.934095 to 14.934095
- output_square: float32 [8, 256, 2304], P('head', None, 'ctx'), may hold values from 26.624 to 108.544
- expand_weight: float32 [2304, 2, 9216], P('ctx', None, 'head'), may hold values from -0.125 to 0.125
- expand_moment: float32 [2304, 2, 9216], P('ctx', None, 'head'), may hold values from -14.934095 to 14.934095
- expand_square: float32 [2304, 2, 9216], P('ctx', None, 'head'), may hold values from 26.624 to 108.544
- shrink_weight: float32 [9216, 2304], P('head', 'ctx'), may hold values from -0.0625 to 0.0625
- shrink_moment: float32 [9216, 2304], P('head', 'ctx'), may hold values from -14.934095 to 14.934095
- shrink_square: float32 [9216, 2304], P('head', 'ctx'), may hold values from 26.624 to 108.544
- gains_weight: float32 [4, 2304], P(None, 'ctx'), may hold values from -0.8 to 0.8
- gains_moment: float32 [4, 2304], P(None, 'ctx'), may hold values from -29.86819 to 29.86819
- gains_square: float32 [4, 2304], P(None, 'ctx'), may hold values from 108.544 to 430.08
Outputs:
- hidden_out: bfloat16 [2048, 2304], P('ctx')
- hidden_grad: float32 [2048, 2304], P('ctx')
- attend_grad: float32 [2304, 4, 4, 256], P('ctx', 'head')
- attend_after: float32 [2304, 4, 4, 256], P('ctx', 'head')
- attend_mean: float32 [2304, 4, 4, 256], P('ctx', 'head')
- attend_power: float32 [2304, 4, 4, 256], P('ctx', 'head')
- output_grad: float32 [8, 256, 2304], P('head', None, 'ctx')
- output_after: float32 [8, 256, 2304], P('head', None, 'ctx')
- output_mean: float32 [8, 256, 2304], P('head', None, 'ctx')
- output_power: float32 [8, 256, 2304], P('head', None, 'ctx')
- expand_grad: float32 [2304, 2, 9216], P('ctx', None, 'head')
- expand_after: float32 [2304, 2, 9216], P('ctx', None, 'head')
- expand_mean: float32 [2304, 2, 9216], P('ctx', None, 'head')
- expand_power: float32 [2304, 2, 9216], P('ctx', None, 'head')
- shrink_grad: float32 [9216, 2304], P('head', 'ctx')
- shrink_after: float32 [9216, 2304], P('head', 'ctx')
- shrink_mean: float32 [9216, 2304], P('head', 'ctx')
- shrink_power: float32 [9216, 2304], P('head', 'ctx')
- gains_grad: float32 [4, 2304], P(None, 'ctx')
- gains_after: float32 [4, 2304], P(None, 'ctx')
- gains_mean: float32 [4, 2304], P(None, 'ctx')
- gains_power: float32 [4, 2304], P(None, 'ctx')
The draws below stay inside these ranges and needn't reach their ends.
Inputs may be any that keep to these rules, and one draw needn't show every extreme that they name: `block_table`: row i lists the two blocks of 64 tokens held by index i of ctx, in the order in which they are laid end to end; the two numbers of a row add up to 31 and every block appears once.
All inputs are finite; a program needn't handle non-finite values.
Results may differ from the reference program's by a relative error of at most 0.02.
The reference program's roundings to bfloat16 on the way count: a program that leaves them out, or rounds other values in their place, can miss the bound.
Values may be sent and summed in bfloat16 or wider, within the bound.
No kernel may reach another device: no remote copies, remote signals or barrier semaphores. Data moves between devices by JAX's collectives and lax.ppermute only.
A program may use at most 256 MiB of HBM per device.

```python
import math
import jax
import jax.numpy as jnp
from jax import lax

D = 2304
FF = 9216
HQ = 8
HK = 4
HD = 256
STEP = 10
BLOCK = 64
SHARDS = 16
SEQ = 2048


def draw_block_table(key, part):
    key = jax.random.fold_in(key, 7)
    order_key, flip_key = jax.random.split(key)
    lower_blocks = jax.random.permutation(order_key, SHARDS).astype(jnp.int32)
    upper_blocks = (2 * SHARDS - 1 - lower_blocks).astype(jnp.int32)
    flip_bits = jax.random.randint(flip_key, (SHARDS,), 0, 2, dtype=jnp.int32)
    leading = jnp.where(flip_bits == 1, upper_blocks, lower_blocks)
    trailing = jnp.where(flip_bits == 1, lower_blocks, upper_blocks)
    return jnp.stack([leading, trailing], axis=1).astype(jnp.int32)


def levels(stream_key, extent, cuts, low, largest):
    def one(dim, blocks):
        steps = jax.random.uniform(jax.random.fold_in(jax.random.fold_in(stream_key, 6), dim), (blocks,), jnp.float32, low / len(cuts), largest / len(cuts))
        return jnp.repeat(jnp.exp(steps), extent[dim] // blocks).reshape((-1,) + (1,) * (len(extent) - dim - 1))

    factor_of = one(*cuts[0])
    for cut in cuts[1:]:
        factor_of = factor_of * one(*cut)
    return factor_of


def bell_draw(key, extent, deviation, most, shards=(), kind=jnp.bfloat16):
    level = levels(key, extent, shards, -0.22, 0.18) if shards else 1.0
    drawn = jax.random.normal(key, extent, jnp.float32) * deviation * level
    return jnp.minimum(jnp.maximum(drawn, -most), most).astype(kind)


def setup_inputs(seed: int = 0) -> dict:
    key_of = jax.random.split(jax.random.key(seed), 19)
    hidden_in = bell_draw(key_of[0], (SEQ, D), 1.0, 6.0, ((0, 16),))
    out_cotangent = bell_draw(key_of[1], (SEQ, D), 1.0, 6.0, ((0, 16),))
    block_table = draw_block_table(jax.random.fold_in(key_of[18], 71), 0)
    attend_weight = bell_draw(key_of[3], (D, HK, HQ // HK + 2, HD), (D // 2) ** -0.5, 0.1875, ((0, 16), (1, 2)), jnp.float32)
    attend_moment = bell_draw(key_of[4], (D, HK, HQ // HK + 2, HD), (0.055 * SEQ ** 0.5), 14.934095, ((0, 16), (1, 2)), jnp.float32)
    attend_square = jnp.clip(jnp.exp(math.log(108.544) - 1.40534252 * jax.random.uniform(key_of[5], (D, HK, HQ // HK + 2, HD), jnp.float32) ** levels(key_of[5], (D, HK, HQ // HK + 2, HD), ((0, 16), (1, 2)), -0.2, 0.2)), 26.624, 108.544)
    output_weight = bell_draw(key_of[6], (HQ, HD, D), (HQ * HD // 4) ** -0.5, 0.25, ((0, 2), (2, 16)), jnp.float32)
    output_moment = bell_draw(key_of[7], (HQ, HD, D), (0.055 * SEQ ** 0.5), 14.934095, ((0, 2), (2, 16)), jnp.float32)
    output_square = jnp.clip(jnp.exp(math.log(108.544) - 1.40534252 * jax.random.uniform(key_of[8], (HQ, HD, D), jnp.float32) ** levels(key_of[8], (HQ, HD, D), ((0, 2), (2, 16)), -0.2, 0.2)), 26.624, 108.544)
    expand_weight = bell_draw(key_of[9], (D, 2, FF), D ** -0.5, 0.125, ((0, 16), (2, 2)), jnp.float32)
    expand_moment = bell_draw(key_of[10], (D, 2, FF), (0.055 * SEQ ** 0.5), 14.934095, ((0, 16), (2, 2)), jnp.float32)
    expand_square = jnp.clip(jnp.exp(math.log(108.544) - 1.40534252 * jax.random.uniform(key_of[11], (D, 2, FF), jnp.float32) ** levels(key_of[11], (D, 2, FF), ((0, 16), (2, 2)), -0.2, 0.2)), 26.624, 108.544)
    shrink_weight = bell_draw(key_of[12], (FF, D), FF ** -0.5, 0.0625, ((0, 2), (1, 16)), jnp.float32)
    shrink_moment = bell_draw(key_of[13], (FF, D), (0.055 * SEQ ** 0.5), 14.934095, ((0, 2), (1, 16)), jnp.float32)
    shrink_square = jnp.clip(jnp.exp(math.log(108.544) - 1.40534252 * jax.random.uniform(key_of[14], (FF, D), jnp.float32) ** levels(key_of[14], (FF, D), ((0, 2), (1, 16)), -0.2, 0.2)), 26.624, 108.544)
    gains_weight = bell_draw(key_of[15], (4, D), 0.2, 0.8, ((1, 16),), jnp.float32)
    gains_moment = bell_draw(key_of[16], (4, D), (0.11 * SEQ ** 0.5), 29.86819, ((1, 16),), jnp.float32)
    gains_square = jnp.clip(jnp.exp(math.log(430.08) - 1.3768156 * jax.random.uniform(key_of[17], (4, D), jnp.float32) ** levels(key_of[17], (4, D), ((1, 16),), -0.2, 0.2)), 108.544, 430.08)
    return dict(hidden_in=hidden_in, out_cotangent=out_cotangent, block_table=block_table, attend_weight=attend_weight, attend_moment=attend_moment, attend_square=attend_square, output_weight=output_weight, output_moment=output_moment, output_square=output_square, expand_weight=expand_weight, expand_moment=expand_moment, expand_square=expand_square, shrink_weight=shrink_weight, shrink_moment=shrink_moment, shrink_square=shrink_square, gains_weight=gains_weight, gains_moment=gains_moment, gains_square=gains_square)


HIGHEST = lax.Precision.HIGHEST
NORM_EPS = 1e-06
SOFT_CAP = 50.0
ROPE_BASE = 10000.0
RATE_MATRIX = 0.02
RATE_GAIN = 0.1
BETA_ONE = 0.9
BETA_TWO = 0.95
ADAM_EPS = 1e-08
DECAY = 0.1

@jax.custom_vjp
def low(v):
    return lax.optimization_barrier(v.astype(jnp.bfloat16)).astype(jnp.float32)

@jax.custom_vjp
def low_back(v):
    return v

def low_keep(v):
    return (low(v), None)

def low_pass(kept, grad):
    return (grad,)

def back_keep(v):
    return (v, None)

def back_low(kept, grad):
    return (low(grad),)
low.defvjp(low_keep, low_pass)
low_back.defvjp(back_keep, back_low)

def token_positions(block_table, block_len):
    offsets = jnp.arange(block_len, dtype=jnp.int32)
    spots = block_table.astype(jnp.int32)[:, :, None] * block_len + offsets[None, None, :]
    return spots.reshape(-1).astype(jnp.int32)

def rope_tables(positions, head_width):
    exponent = jnp.arange(head_width // 2, dtype=jnp.float32) * (2.0 / head_width)
    frequency = ROPE_BASE ** (-exponent)
    angle = positions.astype(jnp.float32)[:, None] * frequency[None, :]
    return (jnp.cos(angle), jnp.sin(angle))

def rotate(values, cosine, sine_table):
    middle = values.shape[-1] // 2
    front_half = values[..., :middle]
    back_half = values[..., middle:]
    return jnp.concatenate([front_half * cosine - back_half * sine_table, back_half * cosine + front_half * sine_table], axis=-1)

def norm_apply(values, norm_gain):
    return values * lax.rsqrt(lax.optimization_barrier(jnp.mean(values * values, axis=-1, keepdims=True)) + NORM_EPS) * (1.0 + norm_gain)

def attention(queries, keys_all, values_all, positions):
    score_scale = queries.shape[-1] ** (-0.5)
    length = queries.shape[0]
    block_rows = min(512, length)
    block_count = length // block_rows

    def one_block(pieces):
        query_part, query_spot = pieces
        raw_score = low_back(jnp.einsum('qgjd,kgd->gjqk', query_part, keys_all, precision=HIGHEST))
        bent_score = jnp.tanh(raw_score * score_scale / SOFT_CAP)
        allowed = positions[None, :] <= query_spot[:, None]
        exp_score = jnp.where(allowed[None, None], jnp.exp(SOFT_CAP * bent_score), 0.0)
        row_total = lax.optimization_barrier(jnp.sum(exp_score, axis=-1))
        summed = low_back(jnp.einsum('gjqk,kgd->qgjd', low(exp_score), values_all, precision=HIGHEST))
        return summed / jnp.transpose(row_total, (2, 0, 1))[..., None]
    shaped = queries.reshape((block_count, block_rows) + queries.shape[1:])
    spots = positions.reshape(block_count, block_rows)
    mixed = lax.map(jax.checkpoint(one_block), (shaped, spots))
    return mixed.reshape(queries.shape)

def apply_layer(hidden, attend_matrix, output_matrix, expand_matrix, shrink_matrix, gains_matrix, positions):
    model_width = hidden.shape[1]
    group_count = attend_matrix.shape[1]
    slot_count = attend_matrix.shape[2]
    head_width = attend_matrix.shape[3]
    hidden_width = expand_matrix.shape[2]
    gains_low = low(gains_matrix)
    normed = low(norm_apply(hidden, gains_low[0]))
    projected = jnp.dot(normed, low(attend_matrix).reshape(model_width, -1), preferred_element_type=jnp.float32, precision=HIGHEST)
    projected = projected.reshape(-1, group_count, slot_count, head_width)
    queries = low_back(projected[:, :, :slot_count - 2])
    keys_pre = low_back(projected[:, :, slot_count - 2])
    values_all = low(low_back(projected[:, :, slot_count - 1]))
    cosine, sine_table = rope_tables(positions, head_width)
    queries = low(rotate(queries, cosine[:, None, None], sine_table[:, None, None]))
    keys_all = low(rotate(keys_pre, cosine[:, None], sine_table[:, None]))
    mixed = low(attention(queries, keys_all, values_all, positions))
    attend_sum = low_back(jnp.dot(mixed.reshape(mixed.shape[0], -1), low(output_matrix).reshape(-1, model_width), preferred_element_type=jnp.float32, precision=HIGHEST))
    first_sum = hidden + norm_apply(attend_sum, gains_low[1])
    normed_two = low(norm_apply(first_sum, gains_low[2]))
    gate_up = low_back(jnp.dot(normed_two, low(expand_matrix).reshape(model_width, -1), preferred_element_type=jnp.float32, precision=HIGHEST))
    gate_up = gate_up.reshape(-1, 2, hidden_width)
    inner_act = low(jax.nn.gelu(gate_up[:, 0], approximate=True) * gate_up[:, 1])
    feed_sum = low_back(jnp.dot(inner_act, low(shrink_matrix), preferred_element_type=jnp.float32, precision=HIGHEST))
    return first_sum + norm_apply(feed_sum, gains_low[3])

def adam_step(weight, moment, square, grad, rate, decay):
    moment_new = BETA_ONE * moment + (1.0 - BETA_ONE) * grad
    square_new = BETA_TWO * square + (1.0 - BETA_TWO) * grad * grad
    mean_hat = moment_new / (1.0 - BETA_ONE ** STEP)
    power_hat = square_new / (1.0 - BETA_TWO ** STEP)
    updated = weight - rate * (mean_hat / (jnp.sqrt(power_hat) + ADAM_EPS) + decay * weight)
    return (updated, moment_new, square_new)

def reference(hidden_in, out_cotangent, block_table, attend_weight, attend_moment, attend_square, output_weight, output_moment, output_square, expand_weight, expand_moment, expand_square, shrink_weight, shrink_moment, shrink_square, gains_weight, gains_moment, gains_square):
    positions = token_positions(block_table, BLOCK)

    def forward(hidden, attend_matrix, output_matrix, expand_matrix, shrink_matrix, gains_matrix):
        return apply_layer(hidden, attend_matrix, output_matrix, expand_matrix, shrink_matrix, gains_matrix, positions)
    result, pull_back = jax.vjp(forward, hidden_in.astype(jnp.float32), attend_weight, output_weight, expand_weight, shrink_weight, gains_weight)
    hidden_grad, attend_grad, output_grad, expand_grad, shrink_grad, gains_grad = pull_back(out_cotangent.astype(jnp.float32))
    attend_after, attend_mean, attend_power = adam_step(attend_weight, attend_moment, attend_square, attend_grad, RATE_MATRIX, DECAY)
    output_after, output_mean, output_power = adam_step(output_weight, output_moment, output_square, output_grad, RATE_MATRIX, DECAY)
    expand_after, expand_mean, expand_power = adam_step(expand_weight, expand_moment, expand_square, expand_grad, RATE_MATRIX, DECAY)
    shrink_after, shrink_mean, shrink_power = adam_step(shrink_weight, shrink_moment, shrink_square, shrink_grad, RATE_MATRIX, DECAY)
    gains_after, gains_mean, gains_power = adam_step(gains_weight, gains_moment, gains_square, gains_grad, RATE_GAIN, 0.0)
    return (result.astype(jnp.bfloat16), hidden_grad, attend_grad, attend_after, attend_mean, attend_power, output_grad, output_after, output_mean, output_power, expand_grad, expand_after, expand_mean, expand_power, shrink_grad, shrink_after, shrink_mean, shrink_power, gains_grad, gains_after, gains_mean, gains_power)
```

```python
import jax
import jax.numpy as jnp
from jax import lax
from jax.sharding import PartitionSpec as P

STEP = 10


NORM_EPS = 1e-06
SOFT_CAP = 50.0
ROPE_BASE = 10000.0
RATE_MATRIX = 0.02
RATE_GAIN = 0.1
BETA_ONE = 0.9
BETA_TWO = 0.95
ADAM_EPS = 1e-08
DECAY = 0.1
ROWS = (((0,), (0,)), ((), ()))
LAST = (((1,), (1,)), ((), ()))
LINES = 4
F32 = jnp.float32
BF16 = jnp.bfloat16


def rope_tables(positions, head_width):
    exponent = jnp.arange(head_width // 2, dtype=F32) * (2.0 / head_width)
    frequency = ROPE_BASE ** (-exponent)
    angle = positions.astype(F32)[:, None] * frequency[None, :]
    return (jnp.cos(angle), jnp.sin(angle))


def rotate(values, cosine, sine_table):
    middle = values.shape[-1] // 2
    front_half = values[..., :middle]
    back_half = values[..., middle:]
    return jnp.concatenate(
        [
            front_half * cosine - back_half * sine_table,
            back_half * cosine + front_half * sine_table,
        ],
        axis=-1,
    )


def norm_factor(values):
    return lax.rsqrt(jnp.mean(values * values, axis=-1, keepdims=True) + NORM_EPS)


def norm_apply(values, norm_gain):
    return values * norm_factor(values) * (1.0 + norm_gain)


def norm_back(values, norm_gain, grad_out):
    factor = norm_factor(values)
    weighted = grad_out * (1.0 + norm_gain)
    grad_in = factor * weighted - values * factor * factor * factor * jnp.mean(
        values * weighted, axis=-1, keepdims=True
    )
    grad_gain = jnp.sum(grad_out * values * factor, axis=0)
    return (grad_in, grad_gain)


def gate_product(gate_act, up_act):
    return jax.nn.gelu(gate_act, approximate=True) * up_act


def adam_step(weight, moment, square, grad, rate, decay):
    moment_new = BETA_ONE * moment + (1.0 - BETA_ONE) * grad
    square_new = BETA_TWO * square + (1.0 - BETA_TWO) * grad * grad
    mean_hat = moment_new / (1.0 - BETA_ONE**STEP)
    power_hat = square_new / (1.0 - BETA_TWO**STEP)
    updated = weight - rate * (mean_hat / (jnp.sqrt(power_hat) + ADAM_EPS) + decay * weight)
    return (updated, moment_new, square_new)


def pick(array, index):
    return lax.dynamic_index_in_dim(array, index, 0, keepdims=False)


def put(array, part, index, dim=0):
    return lax.dynamic_update_slice_in_dim(array, jnp.expand_dims(part, dim), index, dim)


def mirror(number, bits):
    return sum(((number >> i) & 1) << (bits - 1 - i) for i in range(bits))


class Grid:
    def __init__(self):
        self.count = lax.axis_size("ctx")
        self.plane = self.count // LINES
        self.bits = self.plane.bit_length() - 1
        rank = lax.axis_index("ctx")
        self.line = rank // self.plane
        self.place = rank % self.plane
        self.core = lax.axis_index("head")

    def along(self, value, step):
        pairs = [(i, i ^ (step * self.plane)) for i in range(self.count)]
        return lax.ppermute(value, "ctx", pairs)

    def across(self, value):
        return lax.ppermute(value, "head", [(0, 1), (1, 0)])

    def within(self, value, phase):
        pairs = []
        for i in range(self.count):
            for core in range(2):
                bit = phase if core == 0 else self.bits - 1 - phase
                pairs.append((2 * i + core, 2 * (i ^ (1 << bit)) + core))
        return lax.ppermute(value, ("ctx", "head"), pairs)

    def place_of(self, mask):
        return self.place ^ jnp.where(self.core == 0, mask, mirror(mask, self.bits))

    def line_gather(self, value):
        near = self.along(value, 1)
        far = self.along(value, 3)
        middle = self.along(far, 1)
        return jnp.concatenate([value, near, middle, far], axis=0)

    def token_gather(self, value):
        own = self.line_gather(value)
        return jnp.concatenate([own, self.across(own)], axis=0)

    def token_reduce(self, partial):
        half = partial.shape[0] // 2
        got = self.across(partial[half:].astype(BF16))
        mine = partial[:half] + got.astype(F32)
        rows = half // LINES
        block = [mine[k * rows : (k + 1) * rows] for k in range(LINES)]
        passed = self.along(block[2].astype(BF16), 1)
        near = self.along(block[1].astype(BF16), 1)
        far = self.along((block[3] + passed.astype(F32)).astype(BF16), 3)
        return block[0] + near.astype(F32) + far.astype(F32)

    def line_swap(self, blocks):
        result = jnp.zeros(blocks.shape, blocks.dtype)
        result = put(result, pick(blocks, self.line), self.line)
        for step in (3, 2, 1):
            other = self.line ^ step
            result = put(result, self.along(pick(blocks, other), step), other)
        return result

    def plane_gather(self, own):
        parts = {0: own}
        for phase in range(self.bits):
            for mask in range(1 << phase):
                parts[mask | (1 << phase)] = self.within(parts[mask], phase)
        return parts

    def plane_reduce(self, parts):
        parts = dict(parts)
        for phase in reversed(range(self.bits)):
            for mask in reversed(range(1 << phase)):
                got = self.within(parts[mask | (1 << phase)], phase)
                parts[mask] = (parts[mask].astype(F32) + got.astype(F32)).astype(BF16)
        return parts[0]

    def weight_spread(self, blocks):
        own = self.line_swap(blocks)
        parts = self.plane_gather(own)
        full = jnp.zeros((LINES, self.plane) + own.shape[1:], own.dtype)
        for mask, part in parts.items():
            full = put(full, part, self.place_of(mask), 1)
        return full.reshape(-1, own.shape[-1])

    def weight_return(self, full):
        shaped = full.reshape(LINES, self.plane, -1, full.shape[-1])
        parts = {
            mask: lax.dynamic_index_in_dim(shaped, self.place_of(mask), 1, keepdims=False)
            for mask in range(self.plane)
        }
        return self.line_swap(self.plane_reduce(parts))


def body(
    hidden_in,
    out_cotangent,
    block_table,
    attend_weight,
    attend_moment,
    attend_square,
    output_weight,
    output_moment,
    output_square,
    expand_weight,
    expand_moment,
    expand_square,
    shrink_weight,
    shrink_moment,
    shrink_square,
    gains_weight,
    gains_moment,
    gains_square,
):
    grid = Grid()
    core = grid.core
    half_rows = hidden_in.shape[0] // 2
    local_width, group_count, slot_count, head_width = attend_weight.shape
    hidden_width = expand_weight.shape[2]
    model_width = hidden_in.shape[1]
    quarter = hidden_width // LINES
    score_scale = head_width ** (-0.5)

    own_in = lax.dynamic_slice_in_dim(hidden_in, core * half_rows, half_rows)
    own_out = lax.dynamic_slice_in_dim(out_cotangent, core * half_rows, half_rows)
    all_in = grid.token_gather(own_in)

    attend_pack = (
        attend_weight.astype(BF16)
        .reshape(local_width, group_count, 2, 2, head_width)
        .transpose(3, 1, 0, 2, 4)
        .reshape(2, group_count, local_width, 2 * head_width)
    )
    output_pack = (
        output_weight.astype(BF16)
        .reshape(group_count, 2, head_width, local_width)
        .transpose(1, 0, 3, 2)
    )

    def core_swap(pack):
        mine = pick(pack, core)
        got = grid.across(pick(pack, 1 - core))
        return jnp.where(
            core == 0, jnp.concatenate([mine, got]), jnp.concatenate([got, mine])
        )

    def core_return(blocks):
        halves = blocks.reshape((2, group_count) + blocks.shape[1:])
        mine = pick(halves, core)
        got = grid.across(pick(halves, 1 - core))
        return jnp.where(core == 0, jnp.stack([mine, got]), jnp.stack([got, mine]))

    attend_full = grid.weight_spread(core_swap(attend_pack))
    output_full = grid.weight_spread(core_swap(output_pack))
    expand_blocks = (
        expand_weight.astype(BF16)
        .reshape(local_width, 2, LINES, quarter)
        .transpose(2, 0, 1, 3)
        .reshape(LINES, local_width, 2 * quarter)
    )
    shrink_blocks = (
        shrink_weight.T.astype(BF16).reshape(local_width, LINES, quarter).transpose(1, 0, 2)
    )
    expand_full = grid.weight_spread(expand_blocks)
    shrink_full = grid.weight_spread(shrink_blocks)

    gains_own = gains_weight.astype(BF16).astype(F32)
    gains_line = grid.line_gather(gains_own[None])
    gains_lines = jnp.zeros((LINES,) + gains_own.shape, F32)
    for step in range(LINES):
        gains_lines = put(gains_lines, gains_line[step], grid.line ^ step)
    gains_grid = jnp.zeros((LINES, grid.plane) + gains_own.shape, F32)
    for mask, part in grid.plane_gather(gains_lines).items():
        gains_grid = put(gains_grid, part, grid.place_of(mask), 1)
    gains_all = gains_grid.transpose(2, 0, 1, 3).reshape(gains_own.shape[0], model_width)

    lines = grid.line ^ jnp.arange(LINES)
    cores = core ^ jnp.arange(2)
    table = block_table.reshape(LINES, grid.plane, 2)
    offsets = jnp.arange(half_rows, dtype=jnp.int32)
    line_table = jnp.take(jnp.take(table, lines, axis=0), cores, axis=2)
    all_spots = (
        line_table.transpose(1, 2, 0)[..., None] * half_rows + offsets
    ).reshape(grid.plane, -1)
    own_spots = pick(all_spots, grid.place)
    key_spots = all_spots.reshape(-1)
    line_rows = own_spots.shape[0]

    hidden_line = all_in.astype(F32)
    normed_line = norm_apply(hidden_line, gains_all[0]).astype(BF16)
    projected = jnp.dot(normed_line, attend_full, preferred_element_type=F32)
    cosine, sine_table = rope_tables(own_spots, head_width)
    queries_b = rotate(projected[:, :head_width], cosine, sine_table).astype(BF16)
    pair_pre = projected[:, head_width:]
    pair_b = jnp.where(core == 0, rotate(pair_pre, cosine, sine_table), pair_pre).astype(BF16)
    pair_all = jnp.zeros((grid.plane,) + pair_b.shape, BF16)
    for mask, part in grid.plane_gather(pair_b).items():
        pair_all = put(pair_all, part, grid.place_of(mask))

    def flip(values):
        shaped = values.reshape(grid.plane, 2, line_rows // 2, -1)
        return shaped[:, ::-1].reshape(values.shape)

    pair_other = flip(grid.across(pair_all))
    keys_b = jnp.where(core == 0, pair_all, pair_other).reshape(-1, head_width)
    values_b = jnp.where(core == 0, pair_other, pair_all).reshape(-1, head_width)

    raw_score = lax.dot_general(queries_b, keys_b, LAST, preferred_element_type=F32)
    bent_score = jnp.tanh(raw_score * score_scale / SOFT_CAP)
    allowed = key_spots[None, :] <= own_spots[:, None]
    exp_score = jnp.where(allowed, jnp.exp(SOFT_CAP * bent_score), 0.0)
    row_total = jnp.sum(exp_score, axis=-1, keepdims=True)
    exp_score_b = exp_score.astype(BF16)
    summed = jnp.dot(exp_score_b, values_b, preferred_element_type=F32)
    mixed_b = (summed / row_total).astype(BF16)
    attend_part = lax.dot_general(mixed_b, output_full, LAST, preferred_element_type=F32)
    attend_sum = grid.token_reduce(attend_part)

    hidden = own_in.astype(F32)
    first_sum = hidden + norm_apply(attend_sum, gains_all[1])
    normed_two_b = norm_apply(first_sum, gains_all[2]).astype(BF16)
    normed_two_line = grid.token_gather(normed_two_b)
    gate_up = jnp.dot(normed_two_line, expand_full, preferred_element_type=F32)
    gate_act = gate_up[:, :quarter]
    up_act = gate_up[:, quarter:]
    inner_b = gate_product(gate_act, up_act).astype(BF16)
    feed_part = lax.dot_general(inner_b, shrink_full, LAST, preferred_element_type=F32)
    feed_sum = grid.token_reduce(feed_part)
    own_hidden_out = (first_sum + norm_apply(feed_sum, gains_all[3])).astype(BF16)

    grad_out = own_out.astype(F32)
    grad_feed, gain_four = norm_back(feed_sum, gains_all[3], grad_out)
    grad_feed_line = grid.token_gather(grad_feed.astype(BF16))
    grad_inner = jnp.dot(grad_feed_line, shrink_full, preferred_element_type=F32)
    _, pull_back = jax.vjp(gate_product, gate_act, up_act)
    grad_gate, grad_up = pull_back(grad_inner)
    grad_gate_up_b = jnp.concatenate([grad_gate, grad_up], axis=1).astype(BF16)
    grad_two_part = lax.dot_general(grad_gate_up_b, expand_full, LAST, preferred_element_type=F32)
    grad_two = grid.token_reduce(grad_two_part)
    shrink_terms = lax.dot_general(
        grad_feed_line, inner_b, ROWS, preferred_element_type=F32
    ).astype(BF16)
    shrink_back = grid.weight_return(shrink_terms)
    expand_terms = lax.dot_general(
        normed_two_line, grad_gate_up_b, ROWS, preferred_element_type=F32
    ).astype(BF16)
    expand_back = grid.weight_return(expand_terms)

    grad_first_norm, gain_three = norm_back(first_sum, gains_all[2], grad_two)
    grad_first = grad_out + grad_first_norm
    grad_attend, gain_two = norm_back(attend_sum, gains_all[1], grad_first)
    grad_attend_line = grid.token_gather(grad_attend.astype(BF16))
    grad_mixed = jnp.dot(grad_attend_line, output_full, preferred_element_type=F32)
    grad_summed_b = (grad_mixed / row_total).astype(BF16)
    row_delta = jnp.sum(grad_mixed * summed, axis=-1, keepdims=True) / (row_total * row_total)
    grad_exp = (
        lax.dot_general(grad_summed_b, values_b, LAST, preferred_element_type=F32) - row_delta
    )
    grad_raw_b = (
        exp_score * grad_exp * (1.0 - bent_score * bent_score) * score_scale
    ).astype(BF16)
    grad_query = jnp.dot(grad_raw_b, keys_b, preferred_element_type=F32)
    grad_key = lax.dot_general(grad_raw_b, queries_b, ROWS, preferred_element_type=F32)
    grad_value = lax.dot_general(exp_score_b, grad_summed_b, ROWS, preferred_element_type=F32)
    pair_shape = (grid.plane, line_rows, head_width)
    kept = jnp.where(core == 0, grad_key, grad_value).reshape(pair_shape)
    given = jnp.where(core == 0, grad_value, grad_key).reshape(pair_shape)
    pair_terms = kept + flip(grid.across(given.astype(BF16))).astype(F32)
    pair_grad = grid.plane_reduce(
        {m: pick(pair_terms, grid.place_of(m)).astype(BF16) for m in range(grid.plane)}
    ).astype(F32)
    grad_query_pre = rotate(grad_query, cosine, -sine_table)
    grad_pair_pre = jnp.where(core == 0, rotate(pair_grad, cosine, -sine_table), pair_grad)
    grad_proj_b = jnp.concatenate([grad_query_pre, grad_pair_pre], axis=1).astype(BF16)
    grad_normed_part = lax.dot_general(grad_proj_b, attend_full, LAST, preferred_element_type=F32)
    grad_normed = grid.token_reduce(grad_normed_part)
    grad_hidden_norm, gain_one = norm_back(hidden, gains_all[0], grad_normed)
    own_hidden_grad = grad_first + grad_hidden_norm

    output_terms = lax.dot_general(
        grad_attend_line, mixed_b, ROWS, preferred_element_type=F32
    ).astype(BF16)
    output_back = core_return(grid.weight_return(output_terms))
    attend_terms = lax.dot_general(
        normed_line, grad_proj_b, ROWS, preferred_element_type=F32
    ).astype(BF16)
    attend_back = core_return(grid.weight_return(attend_terms))

    def both_halves(value):
        other = grid.across(value)
        return jnp.where(
            core == 0, jnp.concatenate([value, other]), jnp.concatenate([other, value])
        )

    hidden_out = both_halves(own_hidden_out)
    hidden_grad = both_halves(own_hidden_grad)

    gain_terms = jnp.stack([gain_one, gain_two, gain_three, gain_four])
    gain_terms = gain_terms + grid.across(gain_terms)
    gain_terms = gain_terms.reshape(-1, LINES, grid.plane, local_width).transpose(1, 2, 0, 3)
    swept = pick(gain_terms, grid.line)
    for step in (1, 2, 3):
        swept = swept + grid.along(pick(gain_terms, grid.line ^ step), step)
    gain_parts = {m: pick(swept, grid.place_of(m)) for m in range(grid.plane)}
    for phase in reversed(range(grid.bits)):
        for mask in range(1 << phase):
            got = grid.within(gain_parts[mask | (1 << phase)], phase)
            gain_parts[mask] = gain_parts[mask] + got
    gains_grad = gain_parts[0]

    attend_grad = (
        attend_back.reshape(2, group_count, local_width, 2, head_width)
        .transpose(2, 1, 3, 0, 4)
        .reshape(attend_weight.shape)
        .astype(F32)
    )
    output_grad = output_back.transpose(1, 0, 3, 2).reshape(output_weight.shape).astype(F32)
    expand_grad = (
        expand_back.reshape(LINES, local_width, 2, quarter)
        .transpose(1, 2, 0, 3)
        .reshape(expand_weight.shape)
        .astype(F32)
    )
    shrink_grad = shrink_back.transpose(0, 2, 1).reshape(shrink_weight.shape).astype(F32)

    attend_after, attend_mean, attend_power = adam_step(
        attend_weight, attend_moment, attend_square, attend_grad, RATE_MATRIX, DECAY
    )
    output_after, output_mean, output_power = adam_step(
        output_weight, output_moment, output_square, output_grad, RATE_MATRIX, DECAY
    )
    expand_after, expand_mean, expand_power = adam_step(
        expand_weight, expand_moment, expand_square, expand_grad, RATE_MATRIX, DECAY
    )
    shrink_after, shrink_mean, shrink_power = adam_step(
        shrink_weight, shrink_moment, shrink_square, shrink_grad, RATE_MATRIX, DECAY
    )
    gains_after, gains_mean, gains_power = adam_step(
        gains_weight, gains_moment, gains_square, gains_grad, RATE_GAIN, 0.0
    )
    return (
        hidden_out,
        hidden_grad,
        attend_grad,
        attend_after,
        attend_mean,
        attend_power,
        output_grad,
        output_after,
        output_mean,
        output_power,
        expand_grad,
        expand_after,
        expand_mean,
        expand_power,
        shrink_grad,
        shrink_after,
        shrink_mean,
        shrink_power,
        gains_grad,
        gains_after,
        gains_mean,
        gains_power,
    )


def solution(mesh):
    tokens = P("ctx", None)
    attend = P("ctx", "head", None, None)
    output = P("head", None, "ctx")
    expand = P("ctx", None, "head")
    shrink = P("head", "ctx")
    gains = P(None, "ctx")
    in_specs = (tokens, tokens, P()) + sum(
        ((spec,) * 3 for spec in (attend, output, expand, shrink, gains)), ()
    )
    out_specs = (tokens, tokens) + sum(
        ((spec,) * 4 for spec in (attend, output, expand, shrink, gains)), ()
    )
    return jax.shard_map(body, mesh=mesh, in_specs=in_specs, out_specs=out_specs, check_vma=False)
```

```python
import jax
import jax.numpy as jnp
from jax import lax
from jax.experimental import pallas as pl
from jax.experimental.pallas import tpu as pltpu
from jax.sharding import Mesh
from jax.sharding import PartitionSpec as P

STEP = 10


NORM_EPS = 1e-06
SOFT_CAP = 50.0
ROPE_BASE = 10000.0
RATE_MATRIX = 0.02
RATE_GAIN = 0.1
BETA_ONE = 0.9
BETA_TWO = 0.95
ADAM_EPS = 1e-08
DECAY = 0.1
ROWS = (((0,), (0,)), ((), ()))
LAST = (((1,), (1,)), ((), ()))
LINES = 4
F32 = jnp.float32
BF16 = jnp.bfloat16


def rope_tables(positions, head_width):
    exponent = jnp.arange(head_width // 2, dtype=F32) * (2.0 / head_width)
    frequency = ROPE_BASE ** (-exponent)
    angle = positions.astype(F32)[:, None] * frequency[None, :]
    return (jnp.cos(angle), jnp.sin(angle))


def rotate(values, cosine, sine_table):
    middle = values.shape[-1] // 2
    front_half = values[..., :middle]
    back_half = values[..., middle:]
    return jnp.concatenate(
        [
            front_half * cosine - back_half * sine_table,
            back_half * cosine + front_half * sine_table,
        ],
        axis=-1,
    )


def norm_factor(values):
    return lax.rsqrt(jnp.mean(values * values, axis=-1, keepdims=True) + NORM_EPS)


def norm_apply(values, norm_gain):
    return values * norm_factor(values) * (1.0 + norm_gain)


def norm_back(values, norm_gain, grad_out):
    factor = norm_factor(values)
    weighted = grad_out * (1.0 + norm_gain)
    grad_in = factor * weighted - values * factor * factor * factor * jnp.mean(
        values * weighted, axis=-1, keepdims=True
    )
    grad_gain = jnp.sum(grad_out * values * factor, axis=0)
    return (grad_in, grad_gain)


def adam_step(weight, moment, square, grad, rate, decay):
    moment_new = BETA_ONE * moment + (1.0 - BETA_ONE) * grad
    square_new = BETA_TWO * square + (1.0 - BETA_TWO) * grad * grad
    mean_hat = moment_new / (1.0 - BETA_ONE**STEP)
    power_hat = square_new / (1.0 - BETA_TWO**STEP)
    updated = weight - rate * (mean_hat / (jnp.sqrt(power_hat) + ADAM_EPS) + decay * weight)
    return (updated, moment_new, square_new)


def pick(array, index):
    return lax.dynamic_index_in_dim(array, index, 0, keepdims=False)


def put(array, part, index, dim=0):
    return lax.dynamic_update_slice_in_dim(array, jnp.expand_dims(part, dim), index, dim)


def mirror(number, bits):
    return sum(((number >> i) & 1) << (bits - 1 - i) for i in range(bits))


def after(value, *events):
    return lax.optimization_barrier((value,) + events)[0]


class Grid:
    def __init__(self):
        self.plane = lax.axis_size("place")
        self.bits = self.plane.bit_length() - 1
        self.line = lax.axis_index("line")
        self.place = lax.axis_index("place")
        self.core = lax.axis_index("head")

    def along(self, value, step):
        pairs = [(i, i ^ step) for i in range(LINES)]
        return lax.ppermute(value, "line", pairs)

    def across(self, value):
        return lax.ppermute(value, "head", [(0, 1), (1, 0)])

    def within(self, value, phase):
        pairs = []
        for i in range(self.plane):
            for core in range(2):
                bit = phase if core == 0 else self.bits - 1 - phase
                pairs.append((2 * i + core, 2 * (i ^ (1 << bit)) + core))
        return lax.ppermute(value, ("place", "head"), pairs)

    def place_of(self, mask):
        return self.place ^ jnp.where(self.core == 0, mask, mirror(mask, self.bits))

    def token_gather(self, value):
        near = self.along(value, 1)
        far = self.along(value, 3)
        middle = self.along(far, 1)
        own = jnp.concatenate([value, near, middle, far], axis=0)
        return jnp.concatenate([own, self.across(own)], axis=0)

    def token_reduce(self, own, other):
        mine = own + self.across(other).astype(F32)
        rows = own.shape[0] // LINES
        block = [mine[k * rows : (k + 1) * rows] for k in range(LINES)]
        passed = self.along(block[2].astype(BF16), 1)
        near = self.along(block[1].astype(BF16), 1)
        far = self.along((block[3] + passed.astype(F32)).astype(BF16), 3)
        return block[0] + near.astype(F32) + far.astype(F32)

    def line_swap(self, blocks):
        return lax.all_to_all(blocks, "line", split_axis=0, concat_axis=0, tiled=True)

    def plane_gather(self, own):
        parts = {0: own}
        for phase in range(self.bits):
            for mask in range(1 << phase):
                parts[mask | (1 << phase)] = self.within(parts[mask], phase)
        return parts

    def plane_reduce(self, parts, *events):
        parts = dict(parts)
        for phase in reversed(range(self.bits)):
            for mask in reversed(range(1 << phase)):
                given = parts[mask | (1 << phase)]
                if phase == 0 and events:
                    given = after(given, *events)
                got = self.within(given, phase)
                parts[mask] = parts[mask] + got.astype(F32)
                if mask or phase:
                    parts[mask] = parts[mask].astype(BF16)
        return parts[0]

    def spread(self, own):
        full = jnp.zeros((LINES, self.plane) + own.shape[1:], own.dtype)
        for mask, part in self.plane_gather(own).items():
            full = put(full, part, self.place_of(mask), 1)
        return full.reshape(-1, own.shape[-1])

    def bulk_spread(self, own):
        full = lax.all_gather(own, "place", axis=1, tiled=True)
        return full.reshape(-1, own.shape[-1])

    def bulk_sum(self, terms):
        shaped = terms.reshape(LINES, -1, terms.shape[-1])
        return lax.psum_scatter(shaped, "place", scatter_dimension=1, tiled=True)

    def all_terms(self, terms, *events):
        shaped = terms.reshape(LINES, self.plane, -1, terms.shape[-1])
        parts = {
            mask: lax.dynamic_index_in_dim(shaped, self.place_of(mask), 1, keepdims=False)
            for mask in range(self.plane)
        }
        return self.plane_reduce(parts, *events).astype(BF16)

    def first_half(self, values):
        half = values.shape[0] // 2
        swapped = jnp.concatenate([values[half:], values[:half]])
        return jnp.where(self.core == 0, values, swapped)


TILE = 128


def rows_per_step(local_width):
    return 16 if local_width % 16 == 0 else local_width


def attend_rows(array):
    rows, groups, slots, width = array.shape
    tiles = width // TILE
    shaped = array.reshape(rows, groups, slots, tiles, TILE).transpose(0, 1, 3, 2, 4)
    return shaped.reshape(-1, TILE)


def attend_from_rows(array, shape):
    rows, groups, slots, width = shape
    tiles = width // TILE
    shaped = array.reshape(rows, groups, tiles, slots, TILE).transpose(0, 1, 3, 2, 4)
    return shaped.reshape(shape)


def row_block(rows, height):
    return pl.BlockSpec((rows * height, TILE), lambda i, *_: (i, 0))


def pack_expand(weight):
    local_width, _, width = weight.shape
    rows = rows_per_step(local_width)
    quarter = width // LINES

    def kernel(in_ref, *out_refs):
        for gate, out_ref in enumerate(out_refs):
            for line in range(LINES):
                part = in_ref[:, gate, line * quarter : (line + 1) * quarter]
                out_ref[line] = part.astype(BF16)

    pack = jax.ShapeDtypeStruct((LINES, local_width, quarter), BF16)
    return pl.pallas_call(
        kernel,
        out_shape=[pack] * 2,
        grid=(local_width // rows,),
        in_specs=[pl.BlockSpec((rows, 2, width), lambda i: (i, 0, 0))],
        out_specs=[pl.BlockSpec((LINES, rows, quarter), lambda i: (0, i, 0))] * 2,
        compiler_params=pltpu.CompilerParams(vmem_limit_bytes=32 << 20),
        cost_estimate=pl.CostEstimate(flops=0, bytes_accessed=6 * weight.size, transcendentals=0),
        name="pack_expand",
    )(weight)


def pack_shrink(weight):
    width, local_width = weight.shape
    rows = rows_per_step(local_width)
    quarter = width // LINES

    def kernel(in_ref, out_ref):
        for line in range(LINES):
            out_ref[line] = in_ref[:, line * quarter : (line + 1) * quarter].astype(BF16)

    return pl.pallas_call(
        kernel,
        out_shape=jax.ShapeDtypeStruct((LINES, local_width, quarter), BF16),
        grid=(local_width // rows,),
        in_specs=[pl.BlockSpec((rows, width), lambda i: (i, 0))],
        out_specs=pl.BlockSpec((LINES, rows, quarter), lambda i: (0, i, 0)),
        compiler_params=pltpu.CompilerParams(vmem_limit_bytes=32 << 20),
        cost_estimate=pl.CostEstimate(flops=0, bytes_accessed=6 * weight.size, transcendentals=0),
        name="pack_shrink",
    )(weight.T)


def pack_attend(weight, gains, core):
    local_width, groups, slots, width = weight.shape
    rows = rows_per_step(local_width)
    tiles = width // TILE
    height = groups * slots * tiles
    columns = 2 * width + TILE

    def kernel(core_ref, in_ref, gains_ref, own_ref, other_ref):
        for out_ref, member in ((own_ref, core_ref[0]), (other_ref, 1 - core_ref[0])):
            for group in range(groups):
                for pair in range(2):
                    for tile in range(tiles):
                        first = (group * tiles + tile) * slots + 2 * pair
                        chosen = pl.ds(first + member, rows, stride=height)
                        column = (pair * tiles + tile) * TILE
                        out_ref[group, :, column : column + TILE] = in_ref[chosen, :].astype(BF16)
                out_ref[group, :, 2 * width :] = gains_ref[...].astype(BF16)

    pack = jax.ShapeDtypeStruct((groups, local_width, columns), BF16)
    gain_columns = jnp.pad(gains.T, ((0, 0), (0, TILE - gains.shape[0])))
    return pl.pallas_call(
        kernel,
        out_shape=[pack] * 2,
        grid_spec=pltpu.PrefetchScalarGridSpec(
            num_scalar_prefetch=1,
            grid=(local_width // rows,),
            in_specs=[
                row_block(rows, height),
                pl.BlockSpec((rows, TILE), lambda i, *_: (i, 0)),
            ],
            out_specs=[pl.BlockSpec((groups, rows, columns), lambda i, *_: (0, i, 0))] * 2,
        ),
        compiler_params=pltpu.CompilerParams(vmem_limit_bytes=32 << 20),
        cost_estimate=pl.CostEstimate(flops=0, bytes_accessed=6 * weight.size, transcendentals=0),
        name="pack_attend",
    )(core.reshape(1), attend_rows(weight), gain_columns)


def adam_tile(grad, chosen, in_refs, out_refs):
    weight, moment, square = (ref[chosen] for ref in in_refs)
    updated = adam_step(weight, moment, square, grad, RATE_MATRIX, DECAY)
    for ref, value in zip(out_refs, (grad,) + updated, strict=True):
        ref[chosen] = value


def adam_call(kernel, scalars, grads, grad_specs, states, state_spec, steps, name):
    size = states[0].size
    return pl.pallas_call(
        kernel,
        out_shape=[jax.ShapeDtypeStruct(states[0].shape, F32)] * 4,
        grid_spec=pltpu.PrefetchScalarGridSpec(
            num_scalar_prefetch=len(scalars),
            grid=(steps,),
            in_specs=grad_specs + [state_spec] * 3,
            out_specs=[state_spec] * 4,
        ),
        compiler_params=pltpu.CompilerParams(vmem_limit_bytes=40 << 20),
        cost_estimate=pl.CostEstimate(
            flops=20 * size, bytes_accessed=30 * size, transcendentals=2 * size
        ),
        name=name,
    )(*scalars, *grads, *states)


def adam_expand(weight, moment, square, gate_grad, up_grad):
    local_width, _, width = weight.shape
    rows = rows_per_step(local_width)
    quarter = width // LINES

    def kernel(*refs):
        grad_refs, in_refs, out_refs = refs[:2], refs[2:5], refs[5:]
        for gate, grad_ref in enumerate(grad_refs):
            for line in range(LINES):
                chosen = (slice(None), gate, slice(line * quarter, (line + 1) * quarter))
                adam_tile(grad_ref[line].astype(F32), chosen, in_refs, out_refs)

    return adam_call(
        kernel,
        (),
        [gate_grad, up_grad],
        [pl.BlockSpec((LINES, rows, quarter), lambda i: (0, i, 0))] * 2,
        [weight, moment, square],
        pl.BlockSpec((rows, 2, width), lambda i: (i, 0, 0)),
        local_width // rows,
        "adam_expand",
    )


def adam_attend(weight, moment, square, own, other, core):
    shape = weight.shape
    local_width, groups, slots, width = shape
    rows = rows_per_step(local_width)
    tiles = width // TILE
    height = groups * slots * tiles

    def kernel(core_ref, own_ref, other_ref, *refs):
        in_refs, out_refs = refs[:3], refs[3:]
        for grad_ref, member in ((own_ref, core_ref[0]), (other_ref, 1 - core_ref[0])):
            for group in range(groups):
                for pair in range(2):
                    for tile in range(tiles):
                        first = (group * tiles + tile) * slots + 2 * pair
                        chosen = (pl.ds(first + member, rows, stride=height), slice(None))
                        column = (pair * tiles + tile) * TILE
                        grad = grad_ref[group, :, column : column + TILE].astype(F32)
                        adam_tile(grad, chosen, in_refs, out_refs)

    results = adam_call(
        kernel,
        (core.reshape(1),),
        [own, other],
        [pl.BlockSpec((groups, rows, own.shape[-1]), lambda i, *_: (0, i, 0))] * 2,
        [attend_rows(a) for a in (weight, moment, square)],
        row_block(rows, height),
        local_width // rows,
        "adam_attend",
    )
    return [attend_from_rows(a, shape) for a in results]


def adam_shrink(weight, moment, square, grad):
    width, local_width = weight.shape
    rows = rows_per_step(local_width)
    quarter = width // LINES

    def kernel(grad_ref, *refs):
        for line in range(LINES):
            chosen = (slice(None), slice(line * quarter, (line + 1) * quarter))
            adam_tile(grad_ref[line].astype(F32), chosen, refs[:3], refs[3:])

    results = adam_call(
        kernel,
        (),
        [grad],
        [pl.BlockSpec((LINES, rows, quarter), lambda i: (0, i, 0))],
        [a.T for a in (weight, moment, square)],
        pl.BlockSpec((rows, width), lambda i: (i, 0)),
        local_width // rows,
        "adam_shrink",
    )
    return [a.T for a in results]


GELU_SCALE = 0.7978845608028654
GELU_CUBE = 0.044715


def dot_last(left, right):
    return lax.dot_general(left, right, LAST, preferred_element_type=F32)


def dot_rows(left, right):
    return lax.dot_general(left, right, ROWS, preferred_element_type=F32)


def hidden_step(units):
    return 384 if units % 384 == 0 else units


def whole(shape):
    return pl.BlockSpec(shape, lambda j: (0,) * len(shape), pipeline_mode=pl.Buffered(1))


def columns(rows, step):
    return pl.BlockSpec((rows, step), lambda j: (0, j))


def feed_forward(normed, gate_weight, up_weight, shrink_weight):
    tokens, width = normed.shape
    units = gate_weight.shape[1]
    step = hidden_step(units)
    half = tokens // 2

    def kernel(x_ref, gate_w, up_w, shrink_w, gate_ref, up_ref, own_ref, other_ref, sums):
        both = jnp.dot(
            x_ref[...],
            jnp.concatenate([gate_w[...], up_w[...]], axis=1),
            preferred_element_type=F32,
        )
        gate, up = both[:, :step], both[:, step:]
        gate_ref[...] = gate
        up_ref[...] = up
        bend = jnp.tanh(GELU_SCALE * (gate + GELU_CUBE * gate * gate * gate))
        inner = (0.5 * gate * (1.0 + bend) * up).astype(BF16)
        terms = dot_last(inner, shrink_w[...])
        turn = pl.program_id(0)

        @pl.when(turn == 0)
        def _():
            sums[...] = terms

        @pl.when(turn > 0)
        def _():
            sums[...] += terms

        @pl.when(turn == pl.num_programs(0) - 1)
        def _():
            own_ref[...] = sums[:half, :]
            other_ref[...] = sums[half:, :].astype(BF16)

    size = tokens * units
    return pl.pallas_call(
        kernel,
        out_shape=[
            jax.ShapeDtypeStruct((tokens, units), F32),
            jax.ShapeDtypeStruct((tokens, units), F32),
            jax.ShapeDtypeStruct((half, width), F32),
            jax.ShapeDtypeStruct((half, width), BF16),
        ],
        grid=(units // step,),
        in_specs=[whole((tokens, width))] + [columns(width, step)] * 3,
        out_specs=[columns(tokens, step)] * 2 + [whole((half, width))] * 2,
        scratch_shapes=[pltpu.VMEM((tokens, width), F32)],
        compiler_params=pltpu.CompilerParams(vmem_limit_bytes=48 << 20),
        cost_estimate=pl.CostEstimate(
            flops=6 * size * width, bytes_accessed=6 * units * width, transcendentals=size
        ),
        name="feed_forward",
    )(normed, gate_weight, up_weight, shrink_weight)


def feed_backward(grad_feed, normed, gate, up, gate_weight, up_weight, shrink_weight):
    tokens, width = normed.shape
    units = gate.shape[1]
    step = hidden_step(units)
    half = tokens // 2

    def kernel(
        feed_ref, x_ref, gate_ref, up_ref, gate_w, up_w, shrink_w,
        gate_out, up_out, shrink_out, own_ref, other_ref, sums,
    ):
        grad_inner = jnp.dot(feed_ref[...], shrink_w[...], preferred_element_type=F32)
        gate, up = gate_ref[...], up_ref[...]
        square = gate * gate
        bend = jnp.tanh(GELU_SCALE * (gate + GELU_CUBE * gate * square))
        gelu = 0.5 * gate * (1.0 + bend)
        slope = 0.5 * (1.0 + bend) + 0.5 * gate * (1.0 - bend * bend) * (
            GELU_SCALE * (1.0 + 3.0 * GELU_CUBE * square)
        )
        grad_gate = (grad_inner * up * slope).astype(BF16)
        grad_up = (grad_inner * gelu).astype(BF16)
        grads = jnp.concatenate([grad_gate, grad_up], axis=1)
        weights = jnp.concatenate([gate_w[...], up_w[...]], axis=1)
        terms = dot_last(grads, weights)
        turn = pl.program_id(0)

        @pl.when(turn == 0)
        def _():
            sums[...] = terms

        @pl.when(turn > 0)
        def _():
            sums[...] += terms

        @pl.when(turn == pl.num_programs(0) - 1)
        def _():
            own_ref[...] = sums[:half, :]
            other_ref[...] = sums[half:, :].astype(BF16)

        both = dot_rows(x_ref[...], grads).astype(BF16)
        gate_out[...] = both[:, :step]
        up_out[...] = both[:, step:]
        inner = (gelu * up).astype(BF16)
        shrink_out[...] = dot_rows(feed_ref[...], inner).astype(BF16)

    size = tokens * units
    return pl.pallas_call(
        kernel,
        out_shape=[jax.ShapeDtypeStruct((width, units), BF16)] * 3
        + [
            jax.ShapeDtypeStruct((half, width), F32),
            jax.ShapeDtypeStruct((half, width), BF16),
        ],
        grid=(units // step,),
        in_specs=[whole((tokens, width))] * 2
        + [columns(tokens, step)] * 2
        + [columns(width, step)] * 3,
        out_specs=[columns(width, step)] * 3 + [whole((half, width))] * 2,
        scratch_shapes=[pltpu.VMEM((tokens, width), F32)],
        compiler_params=pltpu.CompilerParams(vmem_limit_bytes=56 << 20),
        cost_estimate=pl.CostEstimate(
            flops=12 * size * width, bytes_accessed=12 * units * width, transcendentals=size
        ),
        name="feed_backward",
    )(grad_feed, normed, gate, up, gate_weight, up_weight, shrink_weight)


def body(
    hidden_in,
    out_cotangent,
    block_table,
    attend_weight,
    attend_moment,
    attend_square,
    output_weight,
    output_moment,
    output_square,
    expand_weight,
    expand_moment,
    expand_square,
    shrink_weight,
    shrink_moment,
    shrink_square,
    gains_weight,
    gains_moment,
    gains_square,
):
    grid = Grid()
    core = grid.core
    half_rows = hidden_in.shape[0] // 2
    local_width, group_count, slot_count, head_width = attend_weight.shape
    score_scale = head_width ** (-0.5)

    table = block_table.reshape(LINES, grid.plane, 2)
    line_table = jnp.take(table, grid.line ^ jnp.arange(LINES), axis=0).transpose(1, 2, 0)
    offsets = jnp.arange(half_rows, dtype=jnp.int32)
    all_spots = (line_table[..., None] * half_rows + offsets).reshape(grid.plane, -1)
    own_spots = grid.first_half(pick(all_spots, grid.place))
    key_spots = all_spots.reshape(-1)
    line_rows = own_spots.shape[0]
    half = line_rows // 2

    own_in = lax.dynamic_slice_in_dim(hidden_in, core * half_rows, half_rows)
    own_out = lax.dynamic_slice_in_dim(out_cotangent, core * half_rows, half_rows)
    far_in = grid.along(own_in, 3)
    near_in = grid.along(own_in, 1)

    def by_group(own, other):
        got = grid.across(other)
        return jnp.where(core == 0, jnp.concatenate([own, got]), jnp.concatenate([got, own]))

    def group_return(blocks):
        halves = blocks.reshape((2, group_count) + blocks.shape[1:])
        return pick(halves, core), grid.across(pick(halves, 1 - core))

    attend_rows_here = grid.line_swap(by_group(*pack_attend(attend_weight, gains_weight, core)))
    middle_in = grid.along(far_in, 1)
    line_in = jnp.concatenate([own_in, near_in, middle_in, far_in], axis=0)
    all_in = jnp.concatenate([line_in, grid.across(line_in)], axis=0)
    attend_and_gains = grid.spread(attend_rows_here)
    attend_full = attend_and_gains[:, : 2 * head_width]
    gain_count = gains_weight.shape[0]
    gains_all = attend_and_gains[:, 2 * head_width :][:, :gain_count].T.astype(F32)

    gate_pack, up_pack = pack_expand(after(expand_weight, far_in))
    gate_rows_here = grid.line_swap(after(gate_pack, attend_rows_here))
    gate_full = grid.bulk_spread(gate_rows_here)
    output_pack = (
        output_weight.astype(BF16)
        .reshape(group_count, 2, head_width, local_width)
        .transpose(1, 0, 3, 2)
    )
    output_pack = by_group(pick(output_pack, core), pick(output_pack, 1 - core))
    output_rows_here = grid.line_swap(after(output_pack, attend_and_gains))

    hidden_line = all_in.astype(F32)
    line_factor = norm_factor(hidden_line)
    normed_line = (hidden_line * line_factor * (1.0 + gains_all[0])).astype(BF16)
    projected = jnp.dot(normed_line, attend_full, preferred_element_type=F32)
    cosine, sine_table = rope_tables(own_spots, head_width)
    pair_pre = projected[:, head_width:]
    pair_b = jnp.where(core == 0, rotate(pair_pre, cosine, sine_table), pair_pre).astype(BF16)
    pair_parts = grid.plane_gather(grid.first_half(pair_b))
    queries_b = rotate(projected[:, :head_width], cosine, sine_table).astype(BF16)
    pair_all = jnp.zeros((grid.plane,) + pair_b.shape, BF16)
    for mask, part in pair_parts.items():
        pair_all = put(pair_all, part, grid.place_of(mask))
    pair_all = pair_all.reshape(-1, head_width)
    pair_other = grid.across(pair_all)

    up_rows_here = grid.line_swap(after(up_pack, pair_parts[1]))
    up_full = grid.bulk_spread(up_rows_here)
    output_full = grid.spread(after(output_rows_here, pair_parts[2]))

    keys_b = jnp.where(core == 0, pair_all, pair_other)
    values_b = jnp.where(core == 0, pair_other, pair_all)
    raw_score = dot_last(queries_b, keys_b)
    bent_score = jnp.tanh(raw_score * score_scale / SOFT_CAP)
    allowed = key_spots[None, :] <= own_spots[:, None]
    exp_score = jnp.where(allowed, jnp.exp(SOFT_CAP * bent_score), 0.0)
    row_total = jnp.sum(exp_score, axis=-1, keepdims=True)
    exp_score_b = exp_score.astype(BF16)
    summed = jnp.dot(exp_score_b, values_b, preferred_element_type=F32)
    mixed_b = (summed / row_total).astype(BF16)

    def halves_last(left, right):
        other = dot_last(left[half:], right).astype(BF16)
        return dot_last(left[:half], right), other

    attend_sum = grid.token_reduce(*halves_last(mixed_b, output_full))

    shrink_pack = pack_shrink(after(shrink_weight, pair_parts[1]))
    shrink_rows_here = grid.line_swap(after(shrink_pack, mixed_b))
    hidden = own_in.astype(F32)
    first_sum = hidden + norm_apply(attend_sum, gains_all[1])
    normed_two_b = norm_apply(first_sum, gains_all[2]).astype(BF16)
    normed_two_line = grid.token_gather(normed_two_b)
    shrink_full = grid.spread(after(shrink_rows_here, normed_two_b))
    gate_act, up_act, *feed_parts = feed_forward(normed_two_line, gate_full, up_full, shrink_full)
    feed_sum = grid.token_reduce(*feed_parts)
    own_hidden_out = (first_sum + norm_apply(feed_sum, gains_all[3])).astype(BF16)

    grad_out = own_out.astype(F32)
    grad_feed, gain_four = norm_back(feed_sum, gains_all[3], grad_out)
    grad_feed_line = grid.token_gather(grad_feed.astype(BF16))
    gate_terms, up_terms, shrink_terms, *grad_two_parts = feed_backward(
        grad_feed_line, normed_two_line, gate_act, up_act, gate_full, up_full, shrink_full
    )
    gate_sums = grid.bulk_sum(gate_terms)
    grad_two = grid.token_reduce(*grad_two_parts)
    up_sums = grid.bulk_sum(up_terms)

    grad_first_norm, gain_three = norm_back(first_sum, gains_all[2], grad_two)
    grad_first = grad_out + grad_first_norm
    grad_attend, gain_two = norm_back(attend_sum, gains_all[1], grad_first)
    grad_attend_line = grid.token_gather(grad_attend.astype(BF16))
    shrink_sums = grid.all_terms(shrink_terms, grad_attend_line)
    grad_mixed = jnp.dot(grad_attend_line, output_full, preferred_element_type=F32)
    gate_back = grid.line_swap(after(gate_sums, grad_mixed))
    grad_summed_b = (grad_mixed / row_total).astype(BF16)
    row_delta = jnp.sum(grad_mixed * summed, axis=-1, keepdims=True) / (row_total * row_total)
    grad_exp = dot_last(grad_summed_b, values_b) - row_delta
    grad_raw_b = (
        exp_score * grad_exp * (1.0 - bent_score * bent_score) * score_scale
    ).astype(BF16)
    grad_query = jnp.dot(grad_raw_b, keys_b, preferred_element_type=F32)
    grad_key = dot_rows(grad_raw_b, queries_b)
    grad_value = dot_rows(exp_score_b, grad_summed_b)
    given = jnp.where(core == 0, grad_value, grad_key).astype(BF16)
    pair_terms = jnp.where(core == 0, grad_key, grad_value) + grid.across(given).astype(F32)
    pair_terms = pair_terms.astype(BF16).reshape(grid.plane, line_rows, head_width)
    pair_grad = grid.plane_reduce(
        {m: pick(pair_terms, grid.place_of(m)) for m in range(grid.plane)}
    )
    pair_grad = grid.first_half(pair_grad)
    output_terms = dot_rows(grad_attend_line, mixed_b).astype(BF16)
    output_sums = grid.all_terms(after(output_terms, pair_grad))
    grad_query_pre = rotate(grad_query, cosine, -sine_table)
    grad_pair_pre = jnp.where(core == 0, rotate(pair_grad, cosine, -sine_table), pair_grad)
    grad_proj_b = jnp.concatenate([grad_query_pre, grad_pair_pre], axis=1).astype(BF16)
    grad_normed_part = dot_last(grad_proj_b, attend_full)
    gain_one = jnp.sum(grad_normed_part * hidden_line * line_factor, axis=0)
    grad_normed = grid.token_reduce(grad_normed_part[:half], grad_normed_part[half:].astype(BF16))
    grad_hidden_norm, _ = norm_back(hidden, gains_all[0], grad_normed)
    own_hidden_grad = grad_first + grad_hidden_norm
    shrink_back = grid.line_swap(after(shrink_sums, pair_grad))

    gain_terms = jnp.stack([gain_one, gain_two, gain_three, gain_four], axis=1)
    gain_terms = jnp.pad(gain_terms, ((0, 0), (2 * head_width, TILE - gain_count)))
    attend_terms = dot_rows(normed_line, jnp.pad(grad_proj_b, ((0, 0), (0, TILE)))) + gain_terms
    attend_line = grid.line_swap(grid.all_terms(attend_terms.astype(BF16)))
    up_back = grid.line_swap(up_sums)
    output_back = group_return(grid.line_swap(output_sums))
    attend_back = group_return(attend_line)
    gain_parts = attend_line[:, :, 2 * head_width : 2 * head_width + gain_count]
    gains_grad = jnp.sum(gain_parts.astype(F32), axis=0).T
    gains_grad = gains_grad + grid.across(gains_grad)

    def both_halves(value):
        other = grid.across(value)
        return jnp.where(
            core == 0, jnp.concatenate([value, other]), jnp.concatenate([other, value])
        )

    hidden_out = both_halves(own_hidden_out)
    hidden_grad = both_halves(own_hidden_grad)

    shrink_new = adam_shrink(shrink_weight, shrink_moment, shrink_square, shrink_back)
    expand_new = adam_expand(expand_weight, expand_moment, expand_square, gate_back, up_back)
    attend_new = adam_attend(
        attend_weight, attend_moment, attend_square, attend_back[0], attend_back[1], core
    )
    output_heads = jnp.where(core == 0, jnp.stack(output_back), jnp.stack(output_back[::-1]))
    output_grad = output_heads.transpose(1, 0, 3, 2).reshape(output_weight.shape).astype(F32)
    output_new = adam_step(
        output_weight, output_moment, output_square, output_grad, RATE_MATRIX, DECAY
    )
    gains_new = adam_step(
        gains_weight, gains_moment, gains_square, gains_grad, RATE_GAIN, 0.0
    )
    return (
        hidden_out,
        hidden_grad,
        *attend_new,
        output_grad,
        *output_new,
        *expand_new,
        *shrink_new,
        gains_grad,
        *gains_new,
    )


def solution(mesh):
    count, cores = mesh.shape["ctx"], mesh.shape["head"]
    devices = mesh.devices.reshape(LINES, count // LINES, cores)
    fine = Mesh(devices, ("line", "place", "head"))
    ctx = ("line", "place")
    tokens = P(ctx, None)
    attend = P(ctx, "head", None, None)
    output = P("head", None, ctx)
    expand = P(ctx, None, "head")
    shrink = P("head", ctx)
    gains = P(None, ctx)
    in_specs = (tokens, tokens, P()) + sum(
        ((spec,) * 3 for spec in (attend, output, expand, shrink, gains)), ()
    )
    out_specs = (tokens, tokens) + sum(
        ((spec,) * 4 for spec in (attend, output, expand, shrink, gains)), ()
    )
    return jax.shard_map(body, mesh=fine, in_specs=in_specs, out_specs=out_specs, check_vma=False)
```

```python
import jax
import jax.numpy as jnp
from jax import lax
from jax.experimental import pallas as pl
from jax.experimental.pallas import tpu as pltpu
from jax.sharding import Mesh
from jax.sharding import PartitionSpec as P

STEP = 10


NORM_EPS = 1e-06
SOFT_CAP = 50.0
ROPE_BASE = 10000.0
RATE_MATRIX = 0.02
RATE_GAIN = 0.1
BETA_ONE = 0.9
BETA_TWO = 0.95
ADAM_EPS = 1e-08
DECAY = 0.1
ROWS = (((0,), (0,)), ((), ()))
LAST = (((1,), (1,)), ((), ()))
LINES = 4
F32 = jnp.float32
BF16 = jnp.bfloat16


def rope_tables(positions, head_width):
    exponent = jnp.arange(head_width // 2, dtype=F32) * (2.0 / head_width)
    frequency = ROPE_BASE ** (-exponent)
    angle = positions.astype(F32)[:, None] * frequency[None, :]
    return (jnp.cos(angle), jnp.sin(angle))


def rotate(values, cosine, sine_table):
    middle = values.shape[-1] // 2
    front_half = values[..., :middle]
    back_half = values[..., middle:]
    return jnp.concatenate(
        [
            front_half * cosine - back_half * sine_table,
            back_half * cosine + front_half * sine_table,
        ],
        axis=-1,
    )


def norm_factor(values):
    return lax.rsqrt(jnp.mean(values * values, axis=-1, keepdims=True) + NORM_EPS)


def norm_apply(values, norm_gain):
    return values * norm_factor(values) * (1.0 + norm_gain)


def norm_back(values, norm_gain, grad_out):
    factor = norm_factor(values)
    weighted = grad_out * (1.0 + norm_gain)
    grad_in = factor * weighted - values * factor * factor * factor * jnp.mean(
        values * weighted, axis=-1, keepdims=True
    )
    grad_gain = jnp.sum(grad_out * values * factor, axis=0)
    return (grad_in, grad_gain)


def adam_step(weight, moment, square, grad, rate, decay):
    moment_new = BETA_ONE * moment + (1.0 - BETA_ONE) * grad
    square_new = BETA_TWO * square + (1.0 - BETA_TWO) * grad * grad
    mean_hat = moment_new / (1.0 - BETA_ONE**STEP)
    power_hat = square_new / (1.0 - BETA_TWO**STEP)
    updated = weight - rate * (mean_hat / (jnp.sqrt(power_hat) + ADAM_EPS) + decay * weight)
    return (updated, moment_new, square_new)


def pick(array, index):
    return lax.dynamic_index_in_dim(array, index, 0, keepdims=False)


def put(array, part, index, dim=0):
    return lax.dynamic_update_slice_in_dim(array, jnp.expand_dims(part, dim), index, dim)


def mirror(number, bits):
    return sum(((number >> i) & 1) << (bits - 1 - i) for i in range(bits))


def after(value, *events):
    return lax.optimization_barrier((value,) + events)[0]


class Grid:
    def __init__(self):
        self.plane = lax.axis_size("place")
        self.bits = self.plane.bit_length() - 1
        self.line = lax.axis_index("line")
        self.place = lax.axis_index("place")
        self.core = lax.axis_index("head")

    def along(self, value, step):
        pairs = [(i, i ^ step) for i in range(LINES)]
        return lax.ppermute(value, "line", pairs)

    def across(self, value):
        return lax.ppermute(value, "head", [(0, 1), (1, 0)])

    def within(self, value, phase):
        pairs = []
        for i in range(self.plane):
            for core in range(2):
                bit = phase if core == 0 else self.bits - 1 - phase
                pairs.append((2 * i + core, 2 * (i ^ (1 << bit)) + core))
        return lax.ppermute(value, ("place", "head"), pairs)

    def place_of(self, mask):
        return self.place ^ jnp.where(self.core == 0, mask, mirror(mask, self.bits))

    def token_gather(self, value, *events):
        near = self.along(value, 1)
        far = self.along(value, 3)
        middle = self.along(far, 1)
        own = jnp.zeros((LINES,) + value.shape, value.dtype)
        for step, part in enumerate((value, near, middle, far)):
            own = put(own, part, self.line ^ step)
        own = own.reshape(-1, value.shape[-1])
        if events:
            own = after(own, *events)
        return jnp.concatenate([own, self.across(own)], axis=0)

    def token_reduce(self, own, other, *events):
        if events:
            other = after(other, *events)
        mine = (own + self.across(other).astype(F32)).reshape(LINES, -1, own.shape[-1])
        block = [pick(mine, self.line ^ step) for step in range(LINES)]
        passed = self.along(block[2].astype(BF16), 1)
        near = self.along(block[1].astype(BF16), 1)
        far = self.along((block[3] + passed.astype(F32)).astype(BF16), 3)
        return block[0] + near.astype(F32) + far.astype(F32)

    def line_swap(self, blocks):
        return lax.all_to_all(blocks, "line", split_axis=0, concat_axis=0, tiled=True)

    def plane_gather(self, own, *events):
        parts = {0: own}
        for phase in range(self.bits):
            for mask in range(1 << phase):
                given = parts[mask]
                if mask and events:
                    given = after(given, *events)
                parts[mask | (1 << phase)] = self.within(given, phase)
        return parts

    def plane_reduce(self, parts, *events):
        parts = dict(parts)
        for phase in reversed(range(self.bits)):
            for mask in reversed(range(1 << phase)):
                given = parts[mask | (1 << phase)]
                if phase == 0 and events:
                    given = after(given, *events)
                got = self.within(given, phase)
                parts[mask] = parts[mask] + got.astype(F32)
                if mask or phase:
                    parts[mask] = parts[mask].astype(BF16)
        return parts[0]

    def spread(self, own, *events):
        return self.assemble(self.plane_gather(own, *events))

    def assemble(self, parts):
        full = jnp.zeros((LINES, self.plane) + parts[0].shape[1:], parts[0].dtype)
        for mask, part in parts.items():
            full = put(full, part, self.place_of(mask), 1)
        return full.reshape(-1, parts[0].shape[-1])

    def bulk_spread(self, own):
        full = lax.all_gather(own, "place", axis=1, tiled=True)
        return full.reshape(-1, own.shape[-1])

    def bulk_sum(self, terms):
        shaped = terms.reshape(LINES, -1, terms.shape[-1])
        return lax.psum_scatter(shaped, "place", scatter_dimension=1, tiled=True)

    def all_terms(self, terms, *events):
        shaped = terms.reshape(LINES, self.plane, -1, terms.shape[-1])
        parts = {
            mask: lax.dynamic_index_in_dim(shaped, self.place_of(mask), 1, keepdims=False)
            for mask in range(self.plane)
        }
        return self.plane_reduce(parts, *events).astype(BF16)

    def first_half(self, values):
        half = values.shape[0] // 2
        swapped = jnp.concatenate([values[half:], values[:half]])
        return jnp.where(self.core == 0, values, swapped)


TILE = 128


def rows_per_step(local_width):
    return 16 if local_width % 16 == 0 else local_width


def attend_rows(array):
    rows, groups, slots, width = array.shape
    tiles = width // TILE
    shaped = array.reshape(rows, groups, slots, tiles, TILE).transpose(0, 1, 3, 2, 4)
    return shaped.reshape(-1, TILE)


def attend_from_rows(array, shape):
    rows, groups, slots, width = shape
    tiles = width // TILE
    shaped = array.reshape(rows, groups, tiles, slots, TILE).transpose(0, 1, 3, 2, 4)
    return shaped.reshape(shape)


def row_block(rows, height):
    return pl.BlockSpec((rows * height, TILE), lambda i, *_: (i, 0))


def pack_expand(weight):
    local_width, _, width = weight.shape
    rows = rows_per_step(local_width)
    quarter = width // LINES

    def kernel(in_ref, *out_refs):
        for gate, out_ref in enumerate(out_refs):
            for line in range(LINES):
                part = in_ref[:, gate, line * quarter : (line + 1) * quarter]
                out_ref[line] = part.astype(BF16)

    pack = jax.ShapeDtypeStruct((LINES, local_width, quarter), BF16)
    return pl.pallas_call(
        kernel,
        out_shape=[pack] * 2,
        grid=(local_width // rows,),
        in_specs=[pl.BlockSpec((rows, 2, width), lambda i: (i, 0, 0))],
        out_specs=[pl.BlockSpec((LINES, rows, quarter), lambda i: (0, i, 0))] * 2,
        compiler_params=pltpu.CompilerParams(vmem_limit_bytes=32 << 20),
        cost_estimate=pl.CostEstimate(flops=0, bytes_accessed=6 * weight.size, transcendentals=0),
        name="pack_expand",
    )(weight)


def pack_shrink(weight):
    width, local_width = weight.shape
    rows = rows_per_step(local_width)
    quarter = width // LINES

    def kernel(in_ref, out_ref):
        for line in range(LINES):
            out_ref[line] = in_ref[:, line * quarter : (line + 1) * quarter].astype(BF16)

    return pl.pallas_call(
        kernel,
        out_shape=jax.ShapeDtypeStruct((LINES, local_width, quarter), BF16),
        grid=(local_width // rows,),
        in_specs=[pl.BlockSpec((rows, width), lambda i: (i, 0))],
        out_specs=pl.BlockSpec((LINES, rows, quarter), lambda i: (0, i, 0)),
        compiler_params=pltpu.CompilerParams(vmem_limit_bytes=32 << 20),
        cost_estimate=pl.CostEstimate(flops=0, bytes_accessed=6 * weight.size, transcendentals=0),
        name="pack_shrink",
    )(weight.T)


def pack_attend(weight, gains, core):
    local_width, groups, slots, width = weight.shape
    rows = rows_per_step(local_width)
    tiles = width // TILE
    height = groups * slots * tiles
    columns = 2 * width + TILE

    def kernel(core_ref, in_ref, gains_ref, own_ref, other_ref):
        for out_ref, member in ((own_ref, core_ref[0]), (other_ref, 1 - core_ref[0])):
            for group in range(groups):
                for pair in range(2):
                    for tile in range(tiles):
                        first = (group * tiles + tile) * slots + 2 * pair
                        chosen = pl.ds(first + member, rows, stride=height)
                        column = (pair * tiles + tile) * TILE
                        out_ref[group, :, column : column + TILE] = in_ref[chosen, :].astype(BF16)
                out_ref[group, :, 2 * width :] = gains_ref[...].astype(BF16)

    pack = jax.ShapeDtypeStruct((groups, local_width, columns), BF16)
    gain_columns = jnp.pad(gains.T, ((0, 0), (0, TILE - gains.shape[0])))
    return pl.pallas_call(
        kernel,
        out_shape=[pack] * 2,
        grid_spec=pltpu.PrefetchScalarGridSpec(
            num_scalar_prefetch=1,
            grid=(local_width // rows,),
            in_specs=[
                row_block(rows, height),
                pl.BlockSpec((rows, TILE), lambda i, *_: (i, 0)),
            ],
            out_specs=[pl.BlockSpec((groups, rows, columns), lambda i, *_: (0, i, 0))] * 2,
        ),
        compiler_params=pltpu.CompilerParams(vmem_limit_bytes=32 << 20),
        cost_estimate=pl.CostEstimate(flops=0, bytes_accessed=6 * weight.size, transcendentals=0),
        name="pack_attend",
    )(core.reshape(1), attend_rows(weight), gain_columns)


def adam_tile(grad, chosen, in_refs, out_refs):
    weight, moment, square = (ref[chosen] for ref in in_refs)
    updated = adam_step(weight, moment, square, grad, RATE_MATRIX, DECAY)
    for ref, value in zip(out_refs, (grad,) + updated, strict=True):
        ref[chosen] = value


def adam_call(kernel, scalars, grads, grad_specs, states, state_spec, steps, name, weight):
    return pl.pallas_call(
        kernel,
        out_shape=[jax.ShapeDtypeStruct(states[0].shape, F32)] * 4,
        grid_spec=pltpu.PrefetchScalarGridSpec(
            num_scalar_prefetch=len(scalars),
            grid=(steps,),
            in_specs=grad_specs + [state_spec] * 3,
            out_specs=[state_spec] * 4,
        ),
        compiler_params=pltpu.CompilerParams(vmem_limit_bytes=40 << 20),
        cost_estimate=waiting(weight),
        name=name,
    )(*scalars, *grads, *states)


def adam_expand(weight, moment, square, grad):
    local_width, _, width = weight.shape
    rows = rows_per_step(local_width)
    quarter = width // LINES

    def kernel(grad_ref, *refs):
        for gate in range(2):
            for line in range(LINES):
                chosen = (slice(None), gate, slice(line * quarter, (line + 1) * quarter))
                grad = grad_ref[line, :, gate * quarter : (gate + 1) * quarter]
                adam_tile(grad.astype(F32), chosen, refs[:3], refs[3:])

    return adam_call(
        kernel,
        (),
        [grad],
        [pl.BlockSpec((LINES, rows, 2 * quarter), lambda i: (0, i, 0))],
        [weight, moment, square],
        pl.BlockSpec((rows, 2, width), lambda i: (i, 0, 0)),
        local_width // rows,
        "adam_expand",
        60,
    )


def adam_attend(weight, moment, square, own, other, core):
    shape = weight.shape
    local_width, groups, slots, width = shape
    rows = rows_per_step(local_width)
    tiles = width // TILE
    height = groups * slots * tiles

    def kernel(core_ref, own_ref, other_ref, *refs):
        in_refs, out_refs = refs[:3], refs[3:]
        for grad_ref, member in ((own_ref, core_ref[0]), (other_ref, 1 - core_ref[0])):
            for group in range(groups):
                for pair in range(2):
                    for tile in range(tiles):
                        first = (group * tiles + tile) * slots + 2 * pair
                        chosen = (pl.ds(first + member, rows, stride=height), slice(None))
                        column = (pair * tiles + tile) * TILE
                        grad = grad_ref[group, :, column : column + TILE].astype(F32)
                        adam_tile(grad, chosen, in_refs, out_refs)

    results = adam_call(
        kernel,
        (core.reshape(1),),
        [own, other],
        [pl.BlockSpec((groups, rows, own.shape[-1]), lambda i, *_: (0, i, 0))] * 2,
        [attend_rows(a) for a in (weight, moment, square)],
        row_block(rows, height),
        local_width // rows,
        "adam_attend",
        10,
    )
    return [attend_from_rows(a, shape) for a in results]


def adam_shrink(weight, moment, square, grad):
    width, local_width = weight.shape
    rows = rows_per_step(local_width)
    quarter = width // LINES

    def kernel(grad_ref, *refs):
        for line in range(LINES):
            chosen = (slice(None), slice(line * quarter, (line + 1) * quarter))
            adam_tile(grad_ref[line].astype(F32), chosen, refs[:3], refs[3:])

    results = adam_call(
        kernel,
        (),
        [grad],
        [pl.BlockSpec((LINES, rows, quarter), lambda i: (0, i, 0))],
        [a.T for a in (weight, moment, square)],
        pl.BlockSpec((rows, width), lambda i: (i, 0)),
        local_width // rows,
        "adam_shrink",
        40,
    )
    return [a.T for a in results]


LINE_WEIGHT = 60
OWN_WEIGHT = 3


def waiting(microseconds):
    return pl.CostEstimate(
        flops=int(microseconds * 1e-6 * PEAK), bytes_accessed=0, transcendentals=0
    )


def plain_norm(values):
    tokens, width = values.shape
    rows = tokens // 2

    def kernel(in_ref, out_ref):
        wide = in_ref[...].astype(F32)
        out_ref[...] = wide * norm_factor(wide)

    block = pl.BlockSpec((rows, width), lambda j: (j, 0))
    return pl.pallas_call(
        kernel,
        out_shape=jax.ShapeDtypeStruct((tokens, width), F32),
        grid=(2,),
        in_specs=[block],
        out_specs=block,
        compiler_params=pltpu.CompilerParams(vmem_limit_bytes=24 << 20),
        cost_estimate=waiting(LINE_WEIGHT),
        name="plain_norm",
    )(values)


def last_grad(values, gain, grad_out, carried):
    def kernel(value_ref, gain_ref, grad_ref, carried_ref, out_ref):
        wide = value_ref[...].astype(F32)
        factor = norm_factor(wide)
        weighted = grad_ref[...] * (1.0 + gain_ref[...])
        mean = jnp.mean(wide * weighted, axis=-1, keepdims=True)
        out_ref[...] = carried_ref[...] + (
            factor * weighted - wide * factor * factor * factor * mean
        )

    return pl.pallas_call(
        kernel,
        out_shape=jax.ShapeDtypeStruct(values.shape, F32),
        compiler_params=pltpu.CompilerParams(vmem_limit_bytes=24 << 20),
        cost_estimate=waiting(OWN_WEIGHT),
        name="last_grad",
    )(values, gain[None], grad_out, carried)


PEAK = 1.15e15
ATTEND_WEIGHT = 30
ATTEND_BACK_WEIGHT = 100


def query_rows(tokens, keys):
    rows = tokens
    while rows > 64 and rows * keys > 1 << 19:
        rows //= 2
    return rows


def scores(queries, keys, query_spots, key_spots):
    raw = dot_last(queries, keys)
    bent = jnp.tanh(raw * (queries.shape[-1] ** (-0.5) / SOFT_CAP))
    return bent, jnp.where(key_spots <= query_spots, jnp.exp(SOFT_CAP * bent), 0.0)


def attend_forward(queries, keys, values, query_spots, key_spots):
    tokens, width = queries.shape
    count = keys.shape[0]
    rows = query_rows(tokens, count)

    def kernel(q_ref, k_ref, v_ref, spot_ref, key_spot_ref, total_ref, summed_ref, mixed_ref):
        _, weight = scores(q_ref[...], k_ref[...], spot_ref[...], key_spot_ref[...])
        total = jnp.sum(weight, axis=-1, keepdims=True)
        summed = jnp.dot(weight.astype(BF16), v_ref[...], preferred_element_type=F32)
        total_ref[...] = total
        summed_ref[...] = summed
        mixed_ref[...] = (summed / total).astype(BF16)

    def block(size):
        return pl.BlockSpec((rows, size), lambda j: (j, 0))

    return pl.pallas_call(
        kernel,
        out_shape=[
            jax.ShapeDtypeStruct((tokens, 1), F32),
            jax.ShapeDtypeStruct((tokens, width), F32),
            jax.ShapeDtypeStruct((tokens, width), BF16),
        ],
        grid=(tokens // rows,),
        in_specs=[block(width)] + [whole((count, width))] * 2 + [block(1), whole((1, count))],
        out_specs=[block(1), block(width), block(width)],
        compiler_params=pltpu.CompilerParams(vmem_limit_bytes=40 << 20),
        cost_estimate=pl.CostEstimate(
            flops=int(ATTEND_WEIGHT * 1e-6 * PEAK), bytes_accessed=0, transcendentals=0
        ),
        name="attend_forward",
    )(queries, keys, values, query_spots[:, None], key_spots[None, :])


def attend_backward(queries, keys, values, query_spots, key_spots, total, summed, grad_mixed, core):
    tokens, width = queries.shape
    count = keys.shape[0]
    rows = query_rows(tokens, count)

    def kernel(
        core_ref, q_ref, k_ref, v_ref, spot_ref, key_spot_ref, total_ref, summed_ref, grad_ref,
        query_out, kept_ref, given_ref, key_sums, value_sums,
    ):
        queries, keys = q_ref[...], k_ref[...]
        bent, weight = scores(queries, keys, spot_ref[...], key_spot_ref[...])
        total, grad_mixed = total_ref[...], grad_ref[...]
        grad_summed = (grad_mixed / total).astype(BF16)
        delta = jnp.sum(grad_mixed * summed_ref[...], axis=-1, keepdims=True) / (total * total)
        grad_weight = dot_last(grad_summed, v_ref[...]) - delta
        scale = width ** (-0.5)
        grad_raw = (weight * grad_weight * (1.0 - bent * bent) * scale).astype(BF16)
        query_out[...] = jnp.dot(grad_raw, keys, preferred_element_type=F32)
        grad_keys = dot_rows(grad_raw, queries)
        grad_values = dot_rows(weight.astype(BF16), grad_summed)
        turn = pl.program_id(0)

        @pl.when(turn == 0)
        def _():
            key_sums[...] = grad_keys
            value_sums[...] = grad_values

        @pl.when(turn > 0)
        def _():
            key_sums[...] += grad_keys
            value_sums[...] += grad_values

        @pl.when(turn == pl.num_programs(0) - 1)
        def _():
            has_keys = core_ref[0] == 0
            kept_ref[...] = jnp.where(has_keys, key_sums[...], value_sums[...])
            given_ref[...] = jnp.where(has_keys, value_sums[...], key_sums[...]).astype(BF16)

    def block(size):
        return pl.BlockSpec((rows, size), lambda j, *_: (j, 0))

    def all_of(shape):
        return pl.BlockSpec(shape, lambda j, *_: (0, 0), pipeline_mode=pl.Buffered(1))

    return pl.pallas_call(
        kernel,
        out_shape=[
            jax.ShapeDtypeStruct((tokens, width), F32),
            jax.ShapeDtypeStruct((count, width), F32),
            jax.ShapeDtypeStruct((count, width), BF16),
        ],
        grid_spec=pltpu.PrefetchScalarGridSpec(
            num_scalar_prefetch=1,
            grid=(tokens // rows,),
            in_specs=[block(width)]
            + [all_of((count, width))] * 2
            + [block(1), all_of((1, count)), block(1), block(width), block(width)],
            out_specs=[block(width)] + [all_of((count, width))] * 2,
            scratch_shapes=[pltpu.VMEM((count, width), F32)] * 2,
        ),
        compiler_params=pltpu.CompilerParams(vmem_limit_bytes=56 << 20),
        cost_estimate=pl.CostEstimate(
            flops=int(ATTEND_BACK_WEIGHT * 1e-6 * PEAK), bytes_accessed=0, transcendentals=0
        ),
        name="attend_backward",
    )(
        core.reshape(1), queries, keys, values, query_spots[:, None], key_spots[None, :],
        total, summed, grad_mixed,
    )


GELU_SCALE = 0.7978845608028654
GELU_CUBE = 0.044715


def dot_last(left, right):
    return lax.dot_general(left, right, LAST, preferred_element_type=F32)


def dot_rows(left, right):
    return lax.dot_general(left, right, ROWS, preferred_element_type=F32)


def hidden_step(units):
    return 384 if units % 384 == 0 else units


def whole(shape):
    return pl.BlockSpec(shape, lambda j: (0,) * len(shape), pipeline_mode=pl.Buffered(1))


def columns(rows, step, first=0):
    return pl.BlockSpec((rows, step), lambda j: (0, first + j))


def gate_and_up(normed, gate_weight, up_shrink):
    tokens, width = normed.shape
    units = gate_weight.shape[1]
    step = hidden_step(units)

    def kernel(x_ref, gate_w, up_w, gate_ref, up_ref, inner_ref):
        weights = jnp.concatenate([gate_w[...], up_w[...]], axis=1)
        both = jnp.dot(x_ref[...], weights, preferred_element_type=F32)
        gate, up = both[:, :step], both[:, step:]
        gate_ref[...] = gate
        up_ref[...] = up
        bend = jnp.tanh(GELU_SCALE * (gate + GELU_CUBE * gate * gate * gate))
        inner_ref[...] = (0.5 * gate * (1.0 + bend) * up).astype(BF16)

    size = tokens * units
    return pl.pallas_call(
        kernel,
        out_shape=[jax.ShapeDtypeStruct((tokens, units), kind) for kind in (F32, F32, BF16)],
        grid=(units // step,),
        in_specs=[whole((tokens, width)), columns(width, step), columns(width, step)],
        out_specs=[columns(tokens, step)] * 3,
        compiler_params=pltpu.CompilerParams(vmem_limit_bytes=32 << 20),
        cost_estimate=pl.CostEstimate(
            flops=4 * size * width, bytes_accessed=4 * units * width, transcendentals=size
        ),
        name="gate_and_up",
    )(normed, gate_weight, up_shrink)


def gate_and_up_back(grad_feed, gate, up, up_shrink):
    tokens, width = grad_feed.shape
    units = gate.shape[1]
    step = hidden_step(units)

    def kernel(feed_ref, gate_ref, up_ref, shrink_w, out_ref):
        grad_inner = jnp.dot(feed_ref[...], shrink_w[...], preferred_element_type=F32)
        gate, up = gate_ref[...], up_ref[...]
        square = gate * gate
        bend = jnp.tanh(GELU_SCALE * (gate + GELU_CUBE * gate * square))
        slope = 0.5 * (1.0 + bend) + 0.5 * gate * (1.0 - bend * bend) * (
            GELU_SCALE * (1.0 + 3.0 * GELU_CUBE * square)
        )
        first = pl.multiple_of(pl.program_id(0) * step, TILE)
        out_ref[:, pl.ds(first, step)] = (grad_inner * up * slope).astype(BF16)
        out_ref[:, pl.ds(units + first, step)] = (
            grad_inner * (0.5 * gate * (1.0 + bend))
        ).astype(BF16)

    size = tokens * units
    return pl.pallas_call(
        kernel,
        out_shape=jax.ShapeDtypeStruct((tokens, 2 * units), BF16),
        grid=(units // step,),
        in_specs=[whole((tokens, width))]
        + [columns(tokens, step)] * 2
        + [columns(width, step, units // step)],
        out_specs=pl.BlockSpec((tokens, 2 * units), lambda j: (0, 0)),
        compiler_params=pltpu.CompilerParams(vmem_limit_bytes=32 << 20),
        cost_estimate=pl.CostEstimate(
            flops=2 * size * width, bytes_accessed=2 * units * width, transcendentals=size
        ),
        name="gate_and_up_back",
    )(grad_feed, gate, up, up_shrink)


def body(
    hidden_in,
    out_cotangent,
    block_table,
    attend_weight,
    attend_moment,
    attend_square,
    output_weight,
    output_moment,
    output_square,
    expand_weight,
    expand_moment,
    expand_square,
    shrink_weight,
    shrink_moment,
    shrink_square,
    gains_weight,
    gains_moment,
    gains_square,
):
    grid = Grid()
    core = grid.core
    half_rows = hidden_in.shape[0] // 2
    local_width, group_count, slot_count, head_width = attend_weight.shape

    line_table = block_table.reshape(LINES, grid.plane, 2).transpose(1, 2, 0)
    offsets = jnp.arange(half_rows, dtype=jnp.int32)
    all_spots = (line_table[..., None] * half_rows + offsets).reshape(grid.plane, -1)
    own_spots = grid.first_half(pick(all_spots, grid.place))
    key_spots = all_spots.reshape(-1)
    line_rows = own_spots.shape[0]
    half = line_rows // 2

    own_in = lax.dynamic_slice_in_dim(hidden_in, core * half_rows, half_rows)
    own_out = lax.dynamic_slice_in_dim(out_cotangent, core * half_rows, half_rows)
    line_in = lax.all_gather(own_in, "line", axis=0, tiled=True)
    all_in = jnp.concatenate([line_in, grid.across(line_in)], axis=0)

    def by_group(own, other):
        got = grid.across(other)
        return jnp.where(core == 0, jnp.concatenate([own, got]), jnp.concatenate([got, own]))

    def group_return(blocks):
        halves = blocks.reshape((2, group_count) + blocks.shape[1:])
        return pick(halves, core), grid.across(pick(halves, 1 - core))

    attend_columns = 2 * head_width + TILE
    output_pack = (
        output_weight.astype(BF16)
        .reshape(group_count, 2, head_width, local_width)
        .transpose(1, 0, 3, 2)
    )
    packs = pack_attend(attend_weight, gains_weight, core)
    packs = [
        jnp.concatenate([pack, pick(output_pack, member)], axis=2)
        for pack, member in zip(packs, (core, 1 - core), strict=True)
    ]
    joined_rows_here = grid.line_swap(by_group(*packs))
    attend_rows_here = joined_rows_here[..., :attend_columns]
    output_rows_here = joined_rows_here[..., attend_columns:]
    gate_pack, up_pack = pack_expand(expand_weight)
    attend_and_gains = grid.spread(attend_rows_here)
    attend_full = attend_and_gains[:, : 2 * head_width]
    gain_count = gains_weight.shape[0]
    gains_all = attend_and_gains[:, 2 * head_width :][:, :gain_count].T.astype(F32)

    gate_rows_here = grid.line_swap(after(gate_pack, joined_rows_here))
    units = gate_rows_here.shape[2]
    gate_full = grid.bulk_spread(gate_rows_here)
    shrink_pack = pack_shrink(after(shrink_weight, attend_rows_here))
    up_shrink_pack = jnp.concatenate([up_pack, shrink_pack], axis=2)

    normed_plain = plain_norm(all_in)
    normed_line = (normed_plain * (1.0 + gains_all[0])).astype(BF16)
    projected = jnp.dot(
        after(normed_line, gate_rows_here), attend_full, preferred_element_type=F32
    )
    up_shrink_rows_here = grid.line_swap(after(up_shrink_pack, gate_rows_here))
    up_shrink_full = grid.bulk_spread(up_shrink_rows_here)
    cosine, sine_table = rope_tables(own_spots, head_width)
    pair_pre = projected[:, head_width:]
    pair_b = jnp.where(core == 0, rotate(pair_pre, cosine, sine_table), pair_pre).astype(BF16)
    pair_parts = grid.plane_gather(grid.first_half(pair_b))
    queries_b = rotate(projected[:, :head_width], cosine, sine_table).astype(BF16)
    pair_all = jnp.zeros((grid.plane,) + pair_b.shape, BF16)
    for mask, part in pair_parts.items():
        pair_all = put(pair_all, part, grid.place_of(mask))
    pair_all = pair_all.reshape(-1, head_width)
    pair_other = grid.across(pair_all)

    output_full = grid.spread(after(output_rows_here, pair_parts[3]))

    keys_b = jnp.where(core == 0, pair_all, pair_other)
    values_b = jnp.where(core == 0, pair_other, pair_all)
    row_total, summed, mixed_b = attend_forward(queries_b, keys_b, values_b, own_spots, key_spots)

    def halves_last(*pairs):
        other = sum(dot_last(left[half:], right) for left, right in pairs).astype(BF16)
        own = sum(dot_last(after(left[:half], other), right) for left, right in pairs)
        return own, other

    attend_sum = grid.token_reduce(*halves_last((after(mixed_b, up_shrink_rows_here), output_full)))

    hidden = own_in.astype(F32)
    first_sum = hidden + norm_apply(attend_sum, gains_all[1])
    normed_two_b = norm_apply(first_sum, gains_all[2]).astype(BF16)
    normed_two_line = grid.token_gather(normed_two_b, gate_full)
    gate_act, up_act, inner_b = gate_and_up(normed_two_line, gate_full, up_shrink_full)
    up_full, shrink_full = up_shrink_full[:, :units], up_shrink_full[:, units:]
    feed_sum = grid.token_reduce(*halves_last((inner_b, shrink_full)))
    own_hidden_out = (first_sum + norm_apply(feed_sum, gains_all[3])).astype(BF16)

    grad_out = own_out.astype(F32)
    grad_feed, gain_four = norm_back(feed_sum, gains_all[3], grad_out)
    grad_feed_line = grid.token_gather(grad_feed.astype(BF16))
    grad_both_b = gate_and_up_back(grad_feed_line, gate_act, up_act, up_shrink_full)
    expand_terms = dot_rows(normed_two_line, grad_both_b).astype(BF16)
    expand_sums = grid.bulk_sum(expand_terms)
    grad_both_b = after(grad_both_b, expand_terms)
    grad_two_parts = halves_last(
        (grad_both_b[:, :units], gate_full), (grad_both_b[:, units:], up_full)
    )
    grad_two = grid.token_reduce(*grad_two_parts)
    shrink_terms = dot_rows(grad_feed_line, after(inner_b, grad_two)).astype(BF16)
    shrink_sums = grid.bulk_sum(shrink_terms)

    grad_first_norm, gain_three = norm_back(first_sum, gains_all[2], grad_two)
    grad_first = grad_out + grad_first_norm
    grad_attend, gain_two = norm_back(attend_sum, gains_all[1], grad_first)
    grad_attend_line = grid.token_gather(grad_attend.astype(BF16))
    grad_mixed = jnp.dot(grad_attend_line, output_full, preferred_element_type=F32)
    grad_query, kept, given = attend_backward(
        queries_b, keys_b, values_b, own_spots, key_spots, row_total, summed, grad_mixed, core
    )
    pair_terms = kept + grid.across(given).astype(F32)
    pair_terms = pair_terms.astype(BF16).reshape(grid.plane, line_rows, head_width)
    pair_grad = grid.plane_reduce(
        {m: pick(pair_terms, grid.place_of(m)) for m in range(grid.plane)}
    )
    pair_grad = grid.first_half(pair_grad)
    output_terms = dot_rows(grad_attend_line, mixed_b).astype(BF16)
    grad_query_pre = rotate(grad_query, cosine, -sine_table)
    grad_pair_pre = jnp.where(core == 0, rotate(pair_grad, cosine, -sine_table), pair_grad)
    grad_proj_b = jnp.concatenate([grad_query_pre, grad_pair_pre], axis=1).astype(BF16)
    own_part, other_part = halves_last((grad_proj_b, attend_full))
    gain_one = jnp.sum(own_part * normed_plain[:half], axis=0) + jnp.sum(
        other_part.astype(F32) * normed_plain[half:], axis=0
    )
    grad_normed = grid.token_reduce(own_part, other_part)
    own_hidden_grad = last_grad(own_in, gains_all[0], grad_normed, grad_first)
    expand_back = grid.line_swap(expand_sums)

    gain_terms = jnp.stack([gain_one, gain_two, gain_three, gain_four], axis=1)
    gain_terms = jnp.pad(gain_terms, ((0, 0), (2 * head_width, TILE - gain_count)))
    attend_terms = dot_rows(normed_line, jnp.pad(grad_proj_b, ((0, 0), (0, TILE)))) + gain_terms
    joined_terms = jnp.concatenate([attend_terms.astype(BF16), output_terms], axis=1)
    joined_sums = grid.bulk_sum(joined_terms)
    shrink_back = grid.line_swap(after(shrink_sums, expand_back))
    joined = grid.line_swap(after(joined_sums, shrink_back))
    attend_line = joined[..., :attend_columns]
    output_back = group_return(joined[..., attend_columns:])
    attend_back = group_return(attend_line)
    gain_parts = attend_line[:, :, 2 * head_width : 2 * head_width + gain_count]
    gains_grad = jnp.sum(gain_parts.astype(F32), axis=0).T
    gains_grad = gains_grad + grid.across(gains_grad)

    def both_halves(value):
        other = grid.across(value)
        return jnp.where(
            core == 0, jnp.concatenate([value, other]), jnp.concatenate([other, value])
        )

    hidden_out = both_halves(own_hidden_out)
    hidden_grad = both_halves(own_hidden_grad)

    shrink_new = adam_shrink(shrink_weight, shrink_moment, shrink_square, shrink_back)
    expand_new = adam_expand(expand_weight, expand_moment, expand_square, expand_back)
    attend_new = adam_attend(
        attend_weight, attend_moment, attend_square, attend_back[0], attend_back[1], core
    )
    output_heads = jnp.where(core == 0, jnp.stack(output_back), jnp.stack(output_back[::-1]))
    output_grad = output_heads.transpose(1, 0, 3, 2).reshape(output_weight.shape).astype(F32)
    output_new = adam_step(
        output_weight, output_moment, output_square, output_grad, RATE_MATRIX, DECAY
    )
    gains_new = adam_step(
        gains_weight, gains_moment, gains_square, gains_grad, RATE_GAIN, 0.0
    )
    return (
        hidden_out,
        hidden_grad,
        *attend_new,
        output_grad,
        *output_new,
        *expand_new,
        *shrink_new,
        gains_grad,
        *gains_new,
    )


def solution(mesh):
    count, cores = mesh.shape["ctx"], mesh.shape["head"]
    devices = mesh.devices.reshape(LINES, count // LINES, cores)
    fine = Mesh(devices, ("line", "place", "head"))
    ctx = ("line", "place")
    tokens = P(ctx, None)
    attend = P(ctx, "head", None, None)
    output = P("head", None, ctx)
    expand = P(ctx, None, "head")
    shrink = P("head", ctx)
    gains = P(None, ctx)
    in_specs = (tokens, tokens, P()) + sum(
        ((spec,) * 3 for spec in (attend, output, expand, shrink, gains)), ()
    )
    out_specs = (tokens, tokens) + sum(
        ((spec,) * 4 for spec in (attend, output, expand, shrink, gains)), ()
    )
    return jax.shard_map(body, mesh=fine, in_specs=in_specs, out_specs=out_specs, check_vma=False)
```

```python
import jax
import jax.numpy as jnp
from jax import lax
from jax.experimental import pallas as pl
from jax.experimental.pallas import tpu as pltpu
from jax.sharding import Mesh
from jax.sharding import PartitionSpec as P

STEP = 10


NORM_EPS = 1e-06
SOFT_CAP = 50.0
ROPE_BASE = 10000.0
RATE_MATRIX = 0.02
RATE_GAIN = 0.1
BETA_ONE = 0.9
BETA_TWO = 0.95
ADAM_EPS = 1e-08
DECAY = 0.1
ROWS = (((0,), (0,)), ((), ()))
LAST = (((1,), (1,)), ((), ()))
LINES = 4
F32 = jnp.float32
BF16 = jnp.bfloat16


def rope_tables(positions, head_width):
    exponent = jnp.arange(head_width // 2, dtype=F32) * (2.0 / head_width)
    frequency = ROPE_BASE ** (-exponent)
    angle = positions.astype(F32)[:, None] * frequency[None, :]
    return (jnp.cos(angle), jnp.sin(angle))


def rotate(values, cosine, sine_table):
    middle = values.shape[-1] // 2
    front_half = values[..., :middle]
    back_half = values[..., middle:]
    return jnp.concatenate(
        [
            front_half * cosine - back_half * sine_table,
            back_half * cosine + front_half * sine_table,
        ],
        axis=-1,
    )


def norm_factor(values):
    return lax.rsqrt(jnp.mean(values * values, axis=-1, keepdims=True) + NORM_EPS)


def norm_apply(values, norm_gain):
    return values * norm_factor(values) * (1.0 + norm_gain)


def norm_back(values, norm_gain, grad_out):
    factor = norm_factor(values)
    weighted = grad_out * (1.0 + norm_gain)
    grad_in = factor * weighted - values * factor * factor * factor * jnp.mean(
        values * weighted, axis=-1, keepdims=True
    )
    grad_gain = jnp.sum(grad_out * values * factor, axis=0)
    return (grad_in, grad_gain)


def adam_step(weight, moment, square, grad, rate, decay):
    moment_new = BETA_ONE * moment + (1.0 - BETA_ONE) * grad
    square_new = BETA_TWO * square + (1.0 - BETA_TWO) * grad * grad
    mean_hat = moment_new / (1.0 - BETA_ONE**STEP)
    power_hat = square_new / (1.0 - BETA_TWO**STEP)
    updated = weight - rate * (mean_hat / (jnp.sqrt(power_hat) + ADAM_EPS) + decay * weight)
    return (updated, moment_new, square_new)


def pick(array, index):
    return lax.dynamic_index_in_dim(array, index, 0, keepdims=False)


def put(array, part, index, dim=0):
    return lax.dynamic_update_slice_in_dim(array, jnp.expand_dims(part, dim), index, dim)


def mirror(number, bits):
    return sum(((number >> i) & 1) << (bits - 1 - i) for i in range(bits))


def after(value, *events):
    return lax.optimization_barrier((value,) + events)[0]


class Grid:
    def __init__(self):
        self.plane = lax.axis_size("place")
        self.bits = self.plane.bit_length() - 1
        self.line = lax.axis_index("line")
        self.place = lax.axis_index("place")
        self.core = lax.axis_index("head")

    def along(self, value, step):
        pairs = [(i, i ^ step) for i in range(LINES)]
        return lax.ppermute(value, "line", pairs)

    def across(self, value):
        return lax.ppermute(value, "head", [(0, 1), (1, 0)])

    def within(self, value, phase):
        pairs = []
        for i in range(self.plane):
            for core in range(2):
                bit = phase if core == 0 else self.bits - 1 - phase
                pairs.append((2 * i + core, 2 * (i ^ (1 << bit)) + core))
        return lax.ppermute(value, ("place", "head"), pairs)

    def place_of(self, mask):
        return self.place ^ jnp.where(self.core == 0, mask, mirror(mask, self.bits))

    def token_gather(self, value, *events):
        near = self.along(value, 1)
        far = self.along(value, 3)
        middle = self.along(far, 1)
        own = jnp.zeros((LINES,) + value.shape, value.dtype)
        for step, part in enumerate((value, near, middle, far)):
            own = put(own, part, self.line ^ step)
        own = own.reshape(-1, value.shape[-1])
        if events:
            own = after(own, *events)
        return jnp.concatenate([own, self.across(own)], axis=0)

    def token_reduce(self, own, other, *events):
        if events:
            other = after(other, *events)
        mine = (own + self.across(other).astype(F32)).reshape(LINES, -1, own.shape[-1])
        block = [pick(mine, self.line ^ step) for step in range(LINES)]
        passed = self.along(block[2].astype(BF16), 1)
        near = self.along(block[1].astype(BF16), 1)
        far = self.along((block[3] + passed.astype(F32)).astype(BF16), 3)
        return block[0] + near.astype(F32) + far.astype(F32)

    def line_swap(self, blocks):
        return lax.all_to_all(blocks, "line", split_axis=0, concat_axis=0, tiled=True)

    def plane_gather(self, own, *events):
        parts = {0: own}
        for phase in range(self.bits):
            for mask in range(1 << phase):
                given = parts[mask]
                if mask and events:
                    given = after(given, *events)
                parts[mask | (1 << phase)] = self.within(given, phase)
        return parts

    def plane_reduce(self, parts, *events):
        parts = dict(parts)
        for phase in reversed(range(self.bits)):
            for mask in reversed(range(1 << phase)):
                given = parts[mask | (1 << phase)]
                if phase == 0 and events:
                    given = after(given, *events)
                got = self.within(given, phase)
                parts[mask] = parts[mask] + got.astype(F32)
                if mask or phase:
                    parts[mask] = parts[mask].astype(BF16)
        return parts[0]

    def spread(self, own, *events):
        return self.assemble(self.plane_gather(own, *events))

    def assemble(self, parts):
        full = jnp.zeros((LINES, self.plane) + parts[0].shape[1:], parts[0].dtype)
        for mask, part in parts.items():
            full = put(full, part, self.place_of(mask), 1)
        return full.reshape(-1, parts[0].shape[-1])

    def bulk_spread(self, own):
        full = lax.all_gather(own, "place", axis=1, tiled=True)
        return full.reshape(-1, own.shape[-1])

    def bulk_sum(self, terms):
        shaped = terms.reshape(LINES, -1, terms.shape[-1])
        return lax.psum_scatter(shaped, "place", scatter_dimension=1, tiled=True)

    def all_terms(self, terms, *events):
        shaped = terms.reshape(LINES, self.plane, -1, terms.shape[-1])
        parts = {
            mask: lax.dynamic_index_in_dim(shaped, self.place_of(mask), 1, keepdims=False)
            for mask in range(self.plane)
        }
        return self.plane_reduce(parts, *events).astype(BF16)

    def first_half(self, values):
        half = values.shape[0] // 2
        swapped = jnp.concatenate([values[half:], values[:half]])
        return jnp.where(self.core == 0, values, swapped)


TILE = 128


def rows_per_step(local_width):
    return 16 if local_width % 16 == 0 else local_width


def attend_rows(array):
    rows, groups, slots, width = array.shape
    tiles = width // TILE
    shaped = array.reshape(rows, groups, slots, tiles, TILE).transpose(0, 1, 3, 2, 4)
    return shaped.reshape(-1, TILE)


def attend_from_rows(array, shape):
    rows, groups, slots, width = shape
    tiles = width // TILE
    shaped = array.reshape(rows, groups, tiles, slots, TILE).transpose(0, 1, 3, 2, 4)
    return shaped.reshape(shape)


def row_block(rows, height):
    return pl.BlockSpec((rows * height, TILE), lambda i, *_: (i, 0))


def pack_expand(weight):
    local_width, _, width = weight.shape
    rows = rows_per_step(local_width)
    quarter = width // LINES

    def kernel(in_ref, *out_refs):
        for gate, out_ref in enumerate(out_refs):
            for line in range(LINES):
                part = in_ref[:, gate, line * quarter : (line + 1) * quarter]
                out_ref[line] = part.astype(BF16)

    pack = jax.ShapeDtypeStruct((LINES, local_width, quarter), BF16)
    return pl.pallas_call(
        kernel,
        out_shape=[pack] * 2,
        grid=(local_width // rows,),
        in_specs=[pl.BlockSpec((rows, 2, width), lambda i: (i, 0, 0))],
        out_specs=[pl.BlockSpec((LINES, rows, quarter), lambda i: (0, i, 0))] * 2,
        compiler_params=pltpu.CompilerParams(vmem_limit_bytes=32 << 20),
        cost_estimate=pl.CostEstimate(flops=0, bytes_accessed=6 * weight.size, transcendentals=0),
        name="pack_expand",
    )(weight)


def pack_shrink(weight):
    width, local_width = weight.shape
    rows = rows_per_step(local_width)
    quarter = width // LINES

    def kernel(in_ref, out_ref):
        for line in range(LINES):
            out_ref[line] = in_ref[:, line * quarter : (line + 1) * quarter].astype(BF16)

    return pl.pallas_call(
        kernel,
        out_shape=jax.ShapeDtypeStruct((LINES, local_width, quarter), BF16),
        grid=(local_width // rows,),
        in_specs=[pl.BlockSpec((rows, width), lambda i: (i, 0))],
        out_specs=pl.BlockSpec((LINES, rows, quarter), lambda i: (0, i, 0)),
        compiler_params=pltpu.CompilerParams(vmem_limit_bytes=32 << 20),
        cost_estimate=pl.CostEstimate(flops=0, bytes_accessed=6 * weight.size, transcendentals=0),
        name="pack_shrink",
    )(weight.T)


def pack_attend(weight, gains, core):
    local_width, groups, slots, width = weight.shape
    rows = rows_per_step(local_width)
    tiles = width // TILE
    height = groups * slots * tiles
    columns = 2 * width + TILE

    def kernel(core_ref, in_ref, gains_ref, own_ref, other_ref):
        for out_ref, member in ((own_ref, core_ref[0]), (other_ref, 1 - core_ref[0])):
            for group in range(groups):
                for pair in range(2):
                    for tile in range(tiles):
                        first = (group * tiles + tile) * slots + 2 * pair
                        chosen = pl.ds(first + member, rows, stride=height)
                        column = (pair * tiles + tile) * TILE
                        out_ref[group, :, column : column + TILE] = in_ref[chosen, :].astype(BF16)
                out_ref[group, :, 2 * width :] = gains_ref[...].astype(BF16)

    pack = jax.ShapeDtypeStruct((groups, local_width, columns), BF16)
    gain_columns = jnp.pad(gains.T, ((0, 0), (0, TILE - gains.shape[0])))
    return pl.pallas_call(
        kernel,
        out_shape=[pack] * 2,
        grid_spec=pltpu.PrefetchScalarGridSpec(
            num_scalar_prefetch=1,
            grid=(local_width // rows,),
            in_specs=[
                row_block(rows, height),
                pl.BlockSpec((rows, TILE), lambda i, *_: (i, 0)),
            ],
            out_specs=[pl.BlockSpec((groups, rows, columns), lambda i, *_: (0, i, 0))] * 2,
        ),
        compiler_params=pltpu.CompilerParams(vmem_limit_bytes=32 << 20),
        cost_estimate=pl.CostEstimate(flops=0, bytes_accessed=6 * weight.size, transcendentals=0),
        name="pack_attend",
    )(core.reshape(1), attend_rows(weight), gain_columns)


def adam_tile(grad, chosen, in_refs, out_refs):
    weight, moment, square = (ref[chosen] for ref in in_refs)
    updated = adam_step(weight, moment, square, grad, RATE_MATRIX, DECAY)
    for ref, value in zip(out_refs, (grad,) + updated, strict=True):
        ref[chosen] = value


def adam_call(kernel, scalars, grads, grad_specs, states, state_spec, steps, name, weight):
    return pl.pallas_call(
        kernel,
        out_shape=[jax.ShapeDtypeStruct(states[0].shape, F32)] * 4,
        grid_spec=pltpu.PrefetchScalarGridSpec(
            num_scalar_prefetch=len(scalars),
            grid=(steps,),
            in_specs=grad_specs + [state_spec] * 3,
            out_specs=[state_spec] * 4,
        ),
        compiler_params=pltpu.CompilerParams(vmem_limit_bytes=40 << 20),
        cost_estimate=waiting(weight),
        name=name,
    )(*scalars, *grads, *states)


def adam_expand(weight, moment, square, grad):
    local_width, _, width = weight.shape
    rows = rows_per_step(local_width)
    quarter = width // LINES

    def kernel(grad_ref, *refs):
        for gate in range(2):
            for line in range(LINES):
                chosen = (slice(None), gate, slice(line * quarter, (line + 1) * quarter))
                grad = grad_ref[line, :, gate * quarter : (gate + 1) * quarter]
                adam_tile(grad.astype(F32), chosen, refs[:3], refs[3:])

    return adam_call(
        kernel,
        (),
        [grad],
        [pl.BlockSpec((LINES, rows, 2 * quarter), lambda i: (0, i, 0))],
        [weight, moment, square],
        pl.BlockSpec((rows, 2, width), lambda i: (i, 0, 0)),
        local_width // rows,
        "adam_expand",
        60,
    )


def adam_attend(weight, moment, square, own, other, core):
    shape = weight.shape
    local_width, groups, slots, width = shape
    rows = rows_per_step(local_width)
    tiles = width // TILE
    height = groups * slots * tiles

    def kernel(core_ref, own_ref, other_ref, *refs):
        in_refs, out_refs = refs[:3], refs[3:]
        for grad_ref, member in ((own_ref, core_ref[0]), (other_ref, 1 - core_ref[0])):
            for group in range(groups):
                for pair in range(2):
                    for tile in range(tiles):
                        first = (group * tiles + tile) * slots + 2 * pair
                        chosen = (pl.ds(first + member, rows, stride=height), slice(None))
                        column = (pair * tiles + tile) * TILE
                        grad = grad_ref[group, :, column : column + TILE].astype(F32)
                        adam_tile(grad, chosen, in_refs, out_refs)

    results = adam_call(
        kernel,
        (core.reshape(1),),
        [own, other],
        [pl.BlockSpec((groups, rows, own.shape[-1]), lambda i, *_: (0, i, 0))] * 2,
        [attend_rows(a) for a in (weight, moment, square)],
        row_block(rows, height),
        local_width // rows,
        "adam_attend",
        10,
    )
    return [attend_from_rows(a, shape) for a in results]


def adam_shrink(weight, moment, square, grad):
    width, local_width = weight.shape
    rows = rows_per_step(local_width)
    quarter = width // LINES

    def kernel(grad_ref, *refs):
        for line in range(LINES):
            chosen = (slice(None), slice(line * quarter, (line + 1) * quarter))
            adam_tile(grad_ref[line].astype(F32), chosen, refs[:3], refs[3:])

    results = adam_call(
        kernel,
        (),
        [grad],
        [pl.BlockSpec((LINES, rows, quarter), lambda i: (0, i, 0))],
        [a.T for a in (weight, moment, square)],
        pl.BlockSpec((rows, width), lambda i: (i, 0)),
        local_width // rows,
        "adam_shrink",
        40,
    )
    return [a.T for a in results]


LINE_WEIGHT = 60
OWN_WEIGHT = 3


def waiting(microseconds):
    return pl.CostEstimate(
        flops=int(microseconds * 1e-6 * PEAK), bytes_accessed=0, transcendentals=0
    )


def plain_norm(values):
    tokens, width = values.shape
    rows = tokens // 2

    def kernel(in_ref, out_ref):
        wide = in_ref[...].astype(F32)
        out_ref[...] = wide * norm_factor(wide)

    block = pl.BlockSpec((rows, width), lambda j: (j, 0))
    return pl.pallas_call(
        kernel,
        out_shape=jax.ShapeDtypeStruct((tokens, width), F32),
        grid=(2,),
        in_specs=[block],
        out_specs=block,
        compiler_params=pltpu.CompilerParams(vmem_limit_bytes=24 << 20),
        cost_estimate=waiting(LINE_WEIGHT),
        name="plain_norm",
    )(values)


def last_grad(values, gain, grad_out, carried):
    def kernel(value_ref, gain_ref, grad_ref, carried_ref, out_ref):
        wide = value_ref[...].astype(F32)
        factor = norm_factor(wide)
        weighted = grad_ref[...] * (1.0 + gain_ref[...])
        mean = jnp.mean(wide * weighted, axis=-1, keepdims=True)
        out_ref[...] = carried_ref[...] + (
            factor * weighted - wide * factor * factor * factor * mean
        )

    return pl.pallas_call(
        kernel,
        out_shape=jax.ShapeDtypeStruct(values.shape, F32),
        compiler_params=pltpu.CompilerParams(vmem_limit_bytes=24 << 20),
        cost_estimate=waiting(OWN_WEIGHT),
        name="last_grad",
    )(values, gain[None], grad_out, carried)


PEAK = 1.15e15
ATTEND_WEIGHT = 45
ATTEND_BACK_WEIGHT = 100


def query_rows(tokens, keys):
    rows = tokens
    while rows > 64 and rows * keys > 1 << 19:
        rows //= 2
    return rows


def scores(queries, keys, query_spots, key_spots):
    raw = dot_last(queries, keys)
    bent = jnp.tanh(raw * (queries.shape[-1] ** (-0.5) / SOFT_CAP))
    return bent, jnp.where(key_spots <= query_spots, jnp.exp(SOFT_CAP * bent), 0.0)


def attend_forward(queries, keys, values, query_spots, key_spots):
    tokens, width = queries.shape
    count = keys.shape[0]
    rows = query_rows(tokens, count)

    def kernel(q_ref, k_ref, v_ref, spot_ref, key_spot_ref, total_ref, summed_ref, mixed_ref):
        _, weight = scores(q_ref[...], k_ref[...], spot_ref[...], key_spot_ref[...])
        total = jnp.sum(weight, axis=-1, keepdims=True)
        summed = jnp.dot(weight.astype(BF16), v_ref[...], preferred_element_type=F32)
        total_ref[...] = total
        summed_ref[...] = summed
        mixed_ref[...] = (summed / total).astype(BF16)

    def block(size):
        return pl.BlockSpec((rows, size), lambda j: (j, 0))

    return pl.pallas_call(
        kernel,
        out_shape=[
            jax.ShapeDtypeStruct((tokens, 1), F32),
            jax.ShapeDtypeStruct((tokens, width), F32),
            jax.ShapeDtypeStruct((tokens, width), BF16),
        ],
        grid=(tokens // rows,),
        in_specs=[block(width)] + [whole((count, width))] * 2 + [block(1), whole((1, count))],
        out_specs=[block(1), block(width), block(width)],
        compiler_params=pltpu.CompilerParams(vmem_limit_bytes=40 << 20),
        cost_estimate=pl.CostEstimate(
            flops=int(ATTEND_WEIGHT * 1e-6 * PEAK), bytes_accessed=0, transcendentals=0
        ),
        name="attend_forward",
    )(queries, keys, values, query_spots[:, None], key_spots[None, :])


def attend_backward(queries, keys, values, query_spots, key_spots, total, summed, grad_mixed, core):
    tokens, width = queries.shape
    count = keys.shape[0]
    rows = query_rows(tokens, count)

    def kernel(
        core_ref, q_ref, k_ref, v_ref, spot_ref, key_spot_ref, total_ref, summed_ref, grad_ref,
        query_out, kept_ref, given_ref, key_sums, value_sums,
    ):
        queries, keys = q_ref[...], k_ref[...]
        bent, weight = scores(queries, keys, spot_ref[...], key_spot_ref[...])
        total, grad_mixed = total_ref[...], grad_ref[...]
        grad_summed = (grad_mixed / total).astype(BF16)
        delta = jnp.sum(grad_mixed * summed_ref[...], axis=-1, keepdims=True) / (total * total)
        grad_weight = dot_last(grad_summed, v_ref[...]) - delta
        scale = width ** (-0.5)
        grad_raw = (weight * grad_weight * (1.0 - bent * bent) * scale).astype(BF16)
        query_out[...] = jnp.dot(grad_raw, keys, preferred_element_type=F32)
        grad_keys = dot_rows(grad_raw, queries)
        grad_values = dot_rows(weight.astype(BF16), grad_summed)
        turn = pl.program_id(0)

        @pl.when(turn == 0)
        def _():
            key_sums[...] = grad_keys
            value_sums[...] = grad_values

        @pl.when(turn > 0)
        def _():
            key_sums[...] += grad_keys
            value_sums[...] += grad_values

        @pl.when(turn == pl.num_programs(0) - 1)
        def _():
            has_keys = core_ref[0] == 0
            kept_ref[...] = jnp.where(has_keys, key_sums[...], value_sums[...])
            given_ref[...] = jnp.where(has_keys, value_sums[...], key_sums[...]).astype(BF16)

    def block(size):
        return pl.BlockSpec((rows, size), lambda j, *_: (j, 0))

    def all_of(shape):
        return pl.BlockSpec(shape, lambda j, *_: (0, 0), pipeline_mode=pl.Buffered(1))

    return pl.pallas_call(
        kernel,
        out_shape=[
            jax.ShapeDtypeStruct((tokens, width), F32),
            jax.ShapeDtypeStruct((count, width), F32),
            jax.ShapeDtypeStruct((count, width), BF16),
        ],
        grid_spec=pltpu.PrefetchScalarGridSpec(
            num_scalar_prefetch=1,
            grid=(tokens // rows,),
            in_specs=[block(width)]
            + [all_of((count, width))] * 2
            + [block(1), all_of((1, count)), block(1), block(width), block(width)],
            out_specs=[block(width)] + [all_of((count, width))] * 2,
            scratch_shapes=[pltpu.VMEM((count, width), F32)] * 2,
        ),
        compiler_params=pltpu.CompilerParams(vmem_limit_bytes=56 << 20),
        cost_estimate=pl.CostEstimate(
            flops=int(ATTEND_BACK_WEIGHT * 1e-6 * PEAK), bytes_accessed=0, transcendentals=0
        ),
        name="attend_backward",
    )(
        core.reshape(1), queries, keys, values, query_spots[:, None], key_spots[None, :],
        total, summed, grad_mixed,
    )


GELU_SCALE = 0.7978845608028654
GELU_CUBE = 0.044715


def dot_last(left, right):
    return lax.dot_general(left, right, LAST, preferred_element_type=F32)


def dot_rows(left, right):
    return lax.dot_general(left, right, ROWS, preferred_element_type=F32)


def hidden_step(units):
    return 384 if units % 384 == 0 else units


def whole(shape):
    return pl.BlockSpec(shape, lambda j: (0,) * len(shape), pipeline_mode=pl.Buffered(1))


def columns(rows, step, first=0):
    return pl.BlockSpec((rows, step), lambda j: (0, first + j))


def gate_and_up(normed, gate_weight, up_shrink):
    tokens, width = normed.shape
    units = gate_weight.shape[1]
    step = hidden_step(units)

    def kernel(x_ref, gate_w, up_w, gate_ref, up_ref, inner_ref):
        weights = jnp.concatenate([gate_w[...], up_w[...]], axis=1)
        both = jnp.dot(x_ref[...], weights, preferred_element_type=F32)
        gate, up = both[:, :step], both[:, step:]
        gate_ref[...] = gate
        up_ref[...] = up
        bend = jnp.tanh(GELU_SCALE * (gate + GELU_CUBE * gate * gate * gate))
        inner_ref[...] = (0.5 * gate * (1.0 + bend) * up).astype(BF16)

    size = tokens * units
    return pl.pallas_call(
        kernel,
        out_shape=[jax.ShapeDtypeStruct((tokens, units), kind) for kind in (F32, F32, BF16)],
        grid=(units // step,),
        in_specs=[whole((tokens, width)), columns(width, step), columns(width, step)],
        out_specs=[columns(tokens, step)] * 3,
        compiler_params=pltpu.CompilerParams(vmem_limit_bytes=32 << 20),
        cost_estimate=pl.CostEstimate(
            flops=4 * size * width, bytes_accessed=4 * units * width, transcendentals=size
        ),
        name="gate_and_up",
    )(normed, gate_weight, up_shrink)


def gate_and_up_back(grad_feed, gate, up, up_shrink):
    tokens, width = grad_feed.shape
    units = gate.shape[1]
    step = hidden_step(units)

    def kernel(feed_ref, gate_ref, up_ref, shrink_w, out_ref):
        grad_inner = jnp.dot(feed_ref[...], shrink_w[...], preferred_element_type=F32)
        gate, up = gate_ref[...], up_ref[...]
        square = gate * gate
        bend = jnp.tanh(GELU_SCALE * (gate + GELU_CUBE * gate * square))
        slope = 0.5 * (1.0 + bend) + 0.5 * gate * (1.0 - bend * bend) * (
            GELU_SCALE * (1.0 + 3.0 * GELU_CUBE * square)
        )
        first = pl.multiple_of(pl.program_id(0) * step, TILE)
        out_ref[:, pl.ds(first, step)] = (grad_inner * up * slope).astype(BF16)
        out_ref[:, pl.ds(units + first, step)] = (
            grad_inner * (0.5 * gate * (1.0 + bend))
        ).astype(BF16)

    size = tokens * units
    return pl.pallas_call(
        kernel,
        out_shape=jax.ShapeDtypeStruct((tokens, 2 * units), BF16),
        grid=(units // step,),
        in_specs=[whole((tokens, width))]
        + [columns(tokens, step)] * 2
        + [columns(width, step, units // step)],
        out_specs=pl.BlockSpec((tokens, 2 * units), lambda j: (0, 0)),
        compiler_params=pltpu.CompilerParams(vmem_limit_bytes=32 << 20),
        cost_estimate=pl.CostEstimate(
            flops=2 * size * width, bytes_accessed=2 * units * width, transcendentals=size
        ),
        name="gate_and_up_back",
    )(grad_feed, gate, up, up_shrink)


def body(
    hidden_in,
    out_cotangent,
    block_table,
    attend_weight,
    attend_moment,
    attend_square,
    output_weight,
    output_moment,
    output_square,
    expand_weight,
    expand_moment,
    expand_square,
    shrink_weight,
    shrink_moment,
    shrink_square,
    gains_weight,
    gains_moment,
    gains_square,
):
    grid = Grid()
    core = grid.core
    half_rows = hidden_in.shape[0] // 2
    local_width, group_count, slot_count, head_width = attend_weight.shape

    line_table = block_table.reshape(LINES, grid.plane, 2).transpose(1, 2, 0)
    offsets = jnp.arange(half_rows, dtype=jnp.int32)
    all_spots = (line_table[..., None] * half_rows + offsets).reshape(grid.plane, -1)
    own_spots = grid.first_half(pick(all_spots, grid.place))
    key_spots = all_spots.reshape(-1)
    line_rows = own_spots.shape[0]
    half = line_rows // 2

    own_in = lax.dynamic_slice_in_dim(hidden_in, core * half_rows, half_rows)
    own_out = lax.dynamic_slice_in_dim(out_cotangent, core * half_rows, half_rows)
    line_in = lax.all_gather(own_in, "line", axis=0, tiled=True)
    all_in = jnp.concatenate([line_in, grid.across(line_in)], axis=0)

    def by_group(own, other):
        got = grid.across(other)
        return jnp.where(core == 0, jnp.concatenate([own, got]), jnp.concatenate([got, own]))

    def group_return(blocks):
        halves = blocks.reshape((2, group_count) + blocks.shape[1:])
        return pick(halves, core), grid.across(pick(halves, 1 - core))

    attend_columns = 2 * head_width + TILE
    output_pack = (
        output_weight.astype(BF16)
        .reshape(group_count, 2, head_width, local_width)
        .transpose(1, 0, 3, 2)
    )
    packs = pack_attend(attend_weight, gains_weight, core)
    packs = [
        jnp.concatenate([pack, pick(output_pack, member)], axis=2)
        for pack, member in zip(packs, (core, 1 - core), strict=True)
    ]
    joined_rows_here = grid.line_swap(by_group(*packs))
    attend_rows_here = joined_rows_here[..., :attend_columns]
    output_rows_here = joined_rows_here[..., attend_columns:]
    gate_pack, up_pack = pack_expand(expand_weight)
    attend_and_gains = grid.spread(attend_rows_here)
    attend_full = attend_and_gains[:, : 2 * head_width]
    gain_count = gains_weight.shape[0]
    gains_all = attend_and_gains[:, 2 * head_width :][:, :gain_count].T.astype(F32)

    gate_rows_here = grid.line_swap(after(gate_pack, joined_rows_here))
    units = gate_rows_here.shape[2]
    gate_full = grid.bulk_spread(gate_rows_here)
    shrink_pack = pack_shrink(after(shrink_weight, attend_rows_here))
    up_shrink_pack = jnp.concatenate([up_pack, shrink_pack], axis=2)

    normed_plain = plain_norm(all_in)
    normed_line = (normed_plain * (1.0 + gains_all[0])).astype(BF16)
    projected = jnp.dot(
        after(normed_line, gate_rows_here), attend_full, preferred_element_type=F32
    )
    up_shrink_rows_here = grid.line_swap(after(up_shrink_pack, gate_rows_here))
    up_shrink_full = grid.bulk_spread(up_shrink_rows_here)
    cosine, sine_table = rope_tables(own_spots, head_width)
    pair_pre = projected[:, head_width:]
    pair_b = jnp.where(core == 0, rotate(pair_pre, cosine, sine_table), pair_pre).astype(BF16)
    pair_parts = grid.plane_gather(grid.first_half(pair_b))
    queries_b = rotate(projected[:, :head_width], cosine, sine_table).astype(BF16)
    pair_all = jnp.zeros((grid.plane,) + pair_b.shape, BF16)
    for mask, part in pair_parts.items():
        pair_all = put(pair_all, part, grid.place_of(mask))
    pair_all = pair_all.reshape(-1, head_width)
    pair_other = grid.across(pair_all)

    output_full = grid.spread(after(output_rows_here, pair_parts[3]))

    keys_b = jnp.where(core == 0, pair_all, pair_other)
    values_b = jnp.where(core == 0, pair_other, pair_all)
    row_total, summed, mixed_b = attend_forward(queries_b, keys_b, values_b, own_spots, key_spots)

    def halves_last(*pairs):
        other = sum(dot_last(left[half:], right) for left, right in pairs).astype(BF16)
        own = sum(dot_last(after(left[:half], other), right) for left, right in pairs)
        return own, other

    attend_sum = grid.token_reduce(*halves_last((after(mixed_b, up_shrink_rows_here), output_full)))

    hidden = own_in.astype(F32)
    first_sum = hidden + norm_apply(attend_sum, gains_all[1])
    normed_two_b = norm_apply(first_sum, gains_all[2]).astype(BF16)
    normed_two_line = grid.token_gather(normed_two_b, gate_full)
    gate_act, up_act, inner_b = gate_and_up(normed_two_line, gate_full, up_shrink_full)
    up_full, shrink_full = up_shrink_full[:, :units], up_shrink_full[:, units:]
    feed_sum = grid.token_reduce(*halves_last((inner_b, shrink_full)))
    own_hidden_out = (first_sum + norm_apply(feed_sum, gains_all[3])).astype(BF16)

    grad_out = own_out.astype(F32)
    grad_feed, gain_four = norm_back(feed_sum, gains_all[3], grad_out)
    grad_feed_line = grid.token_gather(grad_feed.astype(BF16))
    shrink_terms = dot_rows(grad_feed_line, inner_b).astype(BF16)
    shrink_sums = grid.bulk_sum(shrink_terms)
    grad_both_b = gate_and_up_back(after(grad_feed_line, shrink_terms), gate_act, up_act, up_shrink_full)
    expand_terms = dot_rows(normed_two_line, grad_both_b).astype(BF16)
    expand_sums = grid.bulk_sum(expand_terms)
    grad_both_b = after(grad_both_b, expand_terms)
    grad_two_parts = halves_last(
        (grad_both_b[:, :units], gate_full), (grad_both_b[:, units:], up_full)
    )
    grad_two = grid.token_reduce(*grad_two_parts)

    grad_first_norm, gain_three = norm_back(first_sum, gains_all[2], grad_two)
    grad_first = grad_out + grad_first_norm
    grad_attend, gain_two = norm_back(attend_sum, gains_all[1], grad_first)
    grad_attend_line = grid.token_gather(grad_attend.astype(BF16))
    grad_mixed = jnp.dot(grad_attend_line, output_full, preferred_element_type=F32)
    grad_query, kept, given = attend_backward(
        queries_b, keys_b, values_b, own_spots, key_spots, row_total, summed, grad_mixed, core
    )
    pair_terms = kept + grid.across(given).astype(F32)
    pair_terms = pair_terms.astype(BF16).reshape(grid.plane, line_rows, head_width)
    pair_grad = grid.plane_reduce(
        {m: pick(pair_terms, grid.place_of(m)) for m in range(grid.plane)}
    )
    pair_grad = grid.first_half(pair_grad)
    output_terms = dot_rows(grad_attend_line, mixed_b).astype(BF16)
    grad_query_pre = rotate(grad_query, cosine, -sine_table)
    grad_pair_pre = jnp.where(core == 0, rotate(pair_grad, cosine, -sine_table), pair_grad)
    grad_proj_b = jnp.concatenate([grad_query_pre, grad_pair_pre], axis=1).astype(BF16)
    shrink_back = grid.line_swap(after(shrink_sums, grad_attend_line))
    own_part, other_part = halves_last((after(grad_proj_b, shrink_back), attend_full))
    gain_one = jnp.sum(own_part * normed_plain[:half], axis=0) + jnp.sum(
        other_part.astype(F32) * normed_plain[half:], axis=0
    )
    grad_normed = grid.token_reduce(own_part, other_part)
    own_hidden_grad = last_grad(own_in, gains_all[0], grad_normed, grad_first)
    expand_back = grid.line_swap(after(expand_sums, shrink_back))

    gain_terms = jnp.stack([gain_one, gain_two, gain_three, gain_four], axis=1)
    gain_terms = jnp.pad(gain_terms, ((0, 0), (2 * head_width, TILE - gain_count)))
    attend_terms = dot_rows(normed_line, jnp.pad(grad_proj_b, ((0, 0), (0, TILE)))) + gain_terms
    joined_terms = jnp.concatenate([attend_terms.astype(BF16), output_terms], axis=1)
    joined_sums = grid.bulk_sum(joined_terms)
    joined = grid.line_swap(after(joined_sums, expand_back))
    attend_line = joined[..., :attend_columns]
    output_back = group_return(joined[..., attend_columns:])
    attend_back = group_return(attend_line)
    gain_parts = attend_line[:, :, 2 * head_width : 2 * head_width + gain_count]
    gains_grad = jnp.sum(gain_parts.astype(F32), axis=0).T
    gains_grad = gains_grad + grid.across(gains_grad)

    def both_halves(value):
        other = grid.across(value)
        return jnp.where(
            core == 0, jnp.concatenate([value, other]), jnp.concatenate([other, value])
        )

    hidden_out = both_halves(own_hidden_out)
    hidden_grad = both_halves(own_hidden_grad)

    shrink_new = adam_shrink(shrink_weight, shrink_moment, shrink_square, shrink_back)
    expand_new = adam_expand(expand_weight, expand_moment, expand_square, expand_back)
    attend_new = adam_attend(
        attend_weight, attend_moment, attend_square, attend_back[0], attend_back[1], core
    )
    output_heads = jnp.where(core == 0, jnp.stack(output_back), jnp.stack(output_back[::-1]))
    output_grad = output_heads.transpose(1, 0, 3, 2).reshape(output_weight.shape).astype(F32)
    output_new = adam_step(
        output_weight, output_moment, output_square, output_grad, RATE_MATRIX, DECAY
    )
    gains_new = adam_step(
        gains_weight, gains_moment, gains_square, gains_grad, RATE_GAIN, 0.0
    )
    return (
        hidden_out,
        hidden_grad,
        *attend_new,
        output_grad,
        *output_new,
        *expand_new,
        *shrink_new,
        gains_grad,
        *gains_new,
    )


def solution(mesh):
    count, cores = mesh.shape["ctx"], mesh.shape["head"]
    devices = mesh.devices.reshape(LINES, count // LINES, cores)
    fine = Mesh(devices, ("line", "place", "head"))
    ctx = ("line", "place")
    tokens = P(ctx, None)
    attend = P(ctx, "head", None, None)
    output = P("head", None, ctx)
    expand = P(ctx, None, "head")
    shrink = P("head", ctx)
    gains = P(None, ctx)
    in_specs = (tokens, tokens, P()) + sum(
        ((spec,) * 3 for spec in (attend, output, expand, shrink, gains)), ()
    )
    out_specs = (tokens, tokens) + sum(
        ((spec,) * 4 for spec in (attend, output, expand, shrink, gains)), ()
    )
    return jax.shard_map(body, mesh=fine, in_specs=in_specs, out_specs=out_specs, check_vma=False)
```

```python
import jax
import jax.numpy as jnp
from jax import lax
from jax.experimental import pallas as pl
from jax.experimental.pallas import tpu as pltpu
from jax.sharding import Mesh
from jax.sharding import PartitionSpec as P

STEP = 10


NORM_EPS = 1e-06
SOFT_CAP = 50.0
ROPE_BASE = 10000.0
RATE_MATRIX = 0.02
RATE_GAIN = 0.1
BETA_ONE = 0.9
BETA_TWO = 0.95
ADAM_EPS = 1e-08
DECAY = 0.1
ROWS = (((0,), (0,)), ((), ()))
LAST = (((1,), (1,)), ((), ()))
LINES = 4
F32 = jnp.float32
BF16 = jnp.bfloat16


def rope_tables(positions, head_width):
    exponent = jnp.arange(head_width // 2, dtype=F32) * (2.0 / head_width)
    frequency = ROPE_BASE ** (-exponent)
    angle = positions.astype(F32)[:, None] * frequency[None, :]
    return (jnp.cos(angle), jnp.sin(angle))


def rotate(values, cosine, sine_table):
    middle = values.shape[-1] // 2
    front_half = values[..., :middle]
    back_half = values[..., middle:]
    return jnp.concatenate(
        [
            front_half * cosine - back_half * sine_table,
            back_half * cosine + front_half * sine_table,
        ],
        axis=-1,
    )


def norm_factor(values):
    return lax.rsqrt(jnp.mean(values * values, axis=-1, keepdims=True) + NORM_EPS)


def norm_apply(values, norm_gain):
    return values * norm_factor(values) * (1.0 + norm_gain)


def norm_back(values, norm_gain, grad_out):
    factor = norm_factor(values)
    weighted = grad_out * (1.0 + norm_gain)
    grad_in = factor * weighted - values * factor * factor * factor * jnp.mean(
        values * weighted, axis=-1, keepdims=True
    )
    grad_gain = jnp.sum(grad_out * values * factor, axis=0)
    return (grad_in, grad_gain)


def adam_step(weight, moment, square, grad, rate, decay):
    moment_new = BETA_ONE * moment + (1.0 - BETA_ONE) * grad
    square_new = BETA_TWO * square + (1.0 - BETA_TWO) * grad * grad
    mean_hat = moment_new / (1.0 - BETA_ONE**STEP)
    power_hat = square_new / (1.0 - BETA_TWO**STEP)
    updated = weight - rate * (mean_hat / (jnp.sqrt(power_hat) + ADAM_EPS) + decay * weight)
    return (updated, moment_new, square_new)


def pick(array, index):
    return lax.dynamic_index_in_dim(array, index, 0, keepdims=False)


def put(array, part, index, dim=0):
    return lax.dynamic_update_slice_in_dim(array, jnp.expand_dims(part, dim), index, dim)


def mirror(number, bits):
    return sum(((number >> i) & 1) << (bits - 1 - i) for i in range(bits))


def after(value, *events):
    return lax.optimization_barrier((value,) + events)[0]


class Grid:
    def __init__(self):
        self.plane = lax.axis_size("place")
        self.bits = self.plane.bit_length() - 1
        self.line = lax.axis_index("line")
        self.place = lax.axis_index("place")
        self.core = lax.axis_index("head")

    def along(self, value, step):
        pairs = [(i, i ^ step) for i in range(LINES)]
        return lax.ppermute(value, "line", pairs)

    def across(self, value):
        return lax.ppermute(value, "head", [(0, 1), (1, 0)])

    def within(self, value, phase):
        pairs = []
        for i in range(self.plane):
            for core in range(2):
                bit = phase if core == 0 else self.bits - 1 - phase
                pairs.append((2 * i + core, 2 * (i ^ (1 << bit)) + core))
        return lax.ppermute(value, ("place", "head"), pairs)

    def place_of(self, mask):
        return self.place ^ jnp.where(self.core == 0, mask, mirror(mask, self.bits))

    def token_gather(self, value, *events):
        near = self.along(value, 1)
        far = self.along(value, 3)
        middle = self.along(far, 1)
        own = jnp.zeros((LINES,) + value.shape, value.dtype)
        for step, part in enumerate((value, near, middle, far)):
            own = put(own, part, self.line ^ step)
        own = own.reshape(-1, value.shape[-1])
        if events:
            own = after(own, *events)
        return jnp.concatenate([own, self.across(own)], axis=0)

    def token_reduce(self, own, other, *events):
        if events:
            other = after(other, *events)
        mine = (own + self.across(other).astype(F32)).reshape(LINES, -1, own.shape[-1])
        block = [pick(mine, self.line ^ step) for step in range(LINES)]
        passed = self.along(block[2].astype(BF16), 1)
        near = self.along(block[1].astype(BF16), 1)
        far = self.along((block[3] + passed.astype(F32)).astype(BF16), 3)
        return block[0] + near.astype(F32) + far.astype(F32)

    def line_swap(self, blocks):
        return lax.all_to_all(blocks, "line", split_axis=0, concat_axis=0, tiled=True)

    def plane_gather(self, own, *events):
        parts = {0: own}
        for phase in range(self.bits):
            for mask in range(1 << phase):
                given = parts[mask]
                if mask and events:
                    given = after(given, *events)
                parts[mask | (1 << phase)] = self.within(given, phase)
        return parts

    def plane_reduce(self, parts, *events):
        parts = dict(parts)
        for phase in reversed(range(self.bits)):
            for mask in reversed(range(1 << phase)):
                given = parts[mask | (1 << phase)]
                if phase == 0 and events:
                    given = after(given, *events)
                got = self.within(given, phase)
                parts[mask] = parts[mask] + got.astype(F32)
                if mask or phase:
                    parts[mask] = parts[mask].astype(BF16)
        return parts[0]

    def spread(self, own, *events):
        return self.assemble(self.plane_gather(own, *events))

    def assemble(self, parts):
        full = jnp.zeros((LINES, self.plane) + parts[0].shape[1:], parts[0].dtype)
        for mask, part in parts.items():
            full = put(full, part, self.place_of(mask), 1)
        return full.reshape(-1, parts[0].shape[-1])

    def bulk_spread(self, own):
        full = lax.all_gather(own, "place", axis=1, tiled=True)
        return full.reshape(-1, own.shape[-1])

    def bulk_sum(self, terms):
        shaped = terms.reshape(LINES, -1, terms.shape[-1])
        return lax.psum_scatter(shaped, "place", scatter_dimension=1, tiled=True)

    def all_terms(self, terms, *events):
        shaped = terms.reshape(LINES, self.plane, -1, terms.shape[-1])
        parts = {
            mask: lax.dynamic_index_in_dim(shaped, self.place_of(mask), 1, keepdims=False)
            for mask in range(self.plane)
        }
        return self.plane_reduce(parts, *events).astype(BF16)

    def first_half(self, values):
        half = values.shape[0] // 2
        swapped = jnp.concatenate([values[half:], values[:half]])
        return jnp.where(self.core == 0, values, swapped)


TILE = 128


def rows_per_step(local_width):
    return 16 if local_width % 16 == 0 else local_width


def pack_expand(weight):
    local_width, _, width = weight.shape
    rows = rows_per_step(local_width)
    quarter = width // LINES

    def kernel(in_ref, *out_refs):
        for gate, out_ref in enumerate(out_refs):
            for line in range(LINES):
                part = in_ref[:, gate, line * quarter : (line + 1) * quarter]
                out_ref[line] = part.astype(BF16)

    pack = jax.ShapeDtypeStruct((LINES, local_width, quarter), BF16)
    return pl.pallas_call(
        kernel,
        out_shape=[pack] * 2,
        grid=(local_width // rows,),
        in_specs=[pl.BlockSpec((rows, 2, width), lambda i: (i, 0, 0))],
        out_specs=[pl.BlockSpec((LINES, rows, quarter), lambda i: (0, i, 0))] * 2,
        compiler_params=pltpu.CompilerParams(vmem_limit_bytes=32 << 20),
        cost_estimate=pl.CostEstimate(flops=0, bytes_accessed=6 * weight.size, transcendentals=0),
        name="pack_expand",
    )(weight)


def pack_shrink(weight):
    width, local_width = weight.shape
    rows = rows_per_step(local_width)
    quarter = width // LINES

    def kernel(in_ref, out_ref):
        for line in range(LINES):
            out_ref[line] = in_ref[:, line * quarter : (line + 1) * quarter].astype(BF16)

    return pl.pallas_call(
        kernel,
        out_shape=jax.ShapeDtypeStruct((LINES, local_width, quarter), BF16),
        grid=(local_width // rows,),
        in_specs=[pl.BlockSpec((rows, width), lambda i: (i, 0))],
        out_specs=pl.BlockSpec((LINES, rows, quarter), lambda i: (0, i, 0)),
        compiler_params=pltpu.CompilerParams(vmem_limit_bytes=32 << 20),
        cost_estimate=pl.CostEstimate(flops=0, bytes_accessed=6 * weight.size, transcendentals=0),
        name="pack_shrink",
    )(weight.T)


def pack_attend(weight, gains, core):
    local_width, groups, slots, width = weight.shape
    rows = rows_per_step(local_width)
    columns = 2 * width + TILE

    def kernel(core_ref, in_ref, gains_ref, own_ref, other_ref):
        first_core = core_ref[0] == 0
        for group in range(groups):
            for pair in range(2):
                first, second = in_ref[:, group, 2 * pair, :], in_ref[:, group, 2 * pair + 1, :]
                place = slice(pair * width, (pair + 1) * width)
                own_ref[group, :, place] = jnp.where(first_core, first, second).astype(BF16)
                other_ref[group, :, place] = jnp.where(first_core, second, first).astype(BF16)
            own_ref[group, :, 2 * width :] = gains_ref[...].astype(BF16)
            other_ref[group, :, 2 * width :] = gains_ref[...].astype(BF16)

    pack = jax.ShapeDtypeStruct((groups, local_width, columns), BF16)
    gain_columns = jnp.pad(gains.T, ((0, 0), (0, TILE - gains.shape[0])))
    return pl.pallas_call(
        kernel,
        out_shape=[pack] * 2,
        grid_spec=pltpu.PrefetchScalarGridSpec(
            num_scalar_prefetch=1,
            grid=(local_width // rows,),
            in_specs=[
                pl.BlockSpec((rows, groups, slots, width), lambda i, *_: (i, 0, 0, 0)),
                pl.BlockSpec((rows, TILE), lambda i, *_: (i, 0)),
            ],
            out_specs=[pl.BlockSpec((groups, rows, columns), lambda i, *_: (0, i, 0))] * 2,
        ),
        compiler_params=pltpu.CompilerParams(vmem_limit_bytes=32 << 20),
        cost_estimate=pl.CostEstimate(flops=0, bytes_accessed=6 * weight.size, transcendentals=0),
        name="pack_attend",
    )(core.reshape(1), weight, gain_columns)


def adam_tile(grad, chosen, in_refs, out_refs):
    weight, moment, square = (ref[chosen] for ref in in_refs)
    updated = adam_step(weight, moment, square, grad, RATE_MATRIX, DECAY)
    for ref, value in zip(out_refs, (grad,) + updated, strict=True):
        ref[chosen] = value


def adam_call(kernel, scalars, grads, grad_specs, states, state_spec, steps, name, weight):
    return pl.pallas_call(
        kernel,
        out_shape=[jax.ShapeDtypeStruct(states[0].shape, F32)] * 4,
        grid_spec=pltpu.PrefetchScalarGridSpec(
            num_scalar_prefetch=len(scalars),
            grid=(steps,),
            in_specs=grad_specs + [state_spec] * 3,
            out_specs=[state_spec] * 4,
        ),
        compiler_params=pltpu.CompilerParams(vmem_limit_bytes=40 << 20),
        cost_estimate=waiting(weight),
        name=name,
    )(*scalars, *grads, *states)


def adam_expand(weight, moment, square, grad):
    local_width, _, width = weight.shape
    rows = rows_per_step(local_width)
    quarter = width // LINES

    def kernel(grad_ref, *refs):
        for gate in range(2):
            for line in range(LINES):
                chosen = (slice(None), gate, slice(line * quarter, (line + 1) * quarter))
                grad = grad_ref[line, :, gate * quarter : (gate + 1) * quarter]
                adam_tile(grad.astype(F32), chosen, refs[:3], refs[3:])

    return adam_call(
        kernel,
        (),
        [grad],
        [pl.BlockSpec((LINES, rows, 2 * quarter), lambda i: (0, i, 0))],
        [weight, moment, square],
        pl.BlockSpec((rows, 2, width), lambda i: (i, 0, 0)),
        local_width // rows,
        "adam_expand",
        60,
    )


def adam_attend(weight, moment, square, own, other, core):
    local_width, groups, slots, width = weight.shape
    rows = rows_per_step(local_width)

    def kernel(core_ref, own_ref, other_ref, *refs):
        first_core = core_ref[0] == 0
        for group in range(groups):
            for pair in range(2):
                place = slice(pair * width, (pair + 1) * width)
                kept = own_ref[group, :, place].astype(F32)
                came = other_ref[group, :, place].astype(F32)
                for member in range(2):
                    grad = jnp.where(first_core == (member == 0), kept, came)
                    chosen = (slice(None), group, 2 * pair + member, slice(None))
                    adam_tile(grad, chosen, refs[:3], refs[3:])

    return adam_call(
        kernel,
        (core.reshape(1),),
        [own, other],
        [pl.BlockSpec((groups, rows, own.shape[-1]), lambda i, *_: (0, i, 0))] * 2,
        [weight, moment, square],
        pl.BlockSpec((rows, groups, slots, width), lambda i, *_: (i, 0, 0, 0)),
        local_width // rows,
        "adam_attend",
        10,
    )


def adam_shrink(weight, moment, square, grad):
    width, local_width = weight.shape
    rows = rows_per_step(local_width)
    quarter = width // LINES

    def kernel(grad_ref, *refs):
        for line in range(LINES):
            chosen = (slice(None), slice(line * quarter, (line + 1) * quarter))
            adam_tile(grad_ref[line].astype(F32), chosen, refs[:3], refs[3:])

    results = adam_call(
        kernel,
        (),
        [grad],
        [pl.BlockSpec((LINES, rows, quarter), lambda i: (0, i, 0))],
        [a.T for a in (weight, moment, square)],
        pl.BlockSpec((rows, width), lambda i: (i, 0)),
        local_width // rows,
        "adam_shrink",
        40,
    )
    return [a.T for a in results]


LINE_WEIGHT = 60
OWN_WEIGHT = 3


def waiting(microseconds):
    return pl.CostEstimate(
        flops=int(microseconds * 1e-6 * PEAK), bytes_accessed=0, transcendentals=0
    )


def plain_norm(values):
    tokens, width = values.shape
    rows = tokens // 2

    def kernel(in_ref, out_ref):
        wide = in_ref[...].astype(F32)
        out_ref[...] = wide * norm_factor(wide)

    block = pl.BlockSpec((rows, width), lambda j: (j, 0))
    return pl.pallas_call(
        kernel,
        out_shape=jax.ShapeDtypeStruct((tokens, width), F32),
        grid=(2,),
        in_specs=[block],
        out_specs=block,
        compiler_params=pltpu.CompilerParams(vmem_limit_bytes=24 << 20),
        cost_estimate=waiting(LINE_WEIGHT),
        name="plain_norm",
    )(values)


def last_grad(values, gain, grad_out, carried):
    def kernel(value_ref, gain_ref, grad_ref, carried_ref, out_ref):
        wide = value_ref[...].astype(F32)
        factor = norm_factor(wide)
        weighted = grad_ref[...] * (1.0 + gain_ref[...])
        mean = jnp.mean(wide * weighted, axis=-1, keepdims=True)
        out_ref[...] = carried_ref[...] + (
            factor * weighted - wide * factor * factor * factor * mean
        )

    return pl.pallas_call(
        kernel,
        out_shape=jax.ShapeDtypeStruct(values.shape, F32),
        compiler_params=pltpu.CompilerParams(vmem_limit_bytes=24 << 20),
        cost_estimate=waiting(OWN_WEIGHT),
        name="last_grad",
    )(values, gain[None], grad_out, carried)


PEAK = 1.15e15
ATTEND_WEIGHT = 45
ATTEND_BACK_WEIGHT = 100


def query_rows(tokens, keys):
    rows = tokens
    while rows > 64 and rows * keys > 1 << 19:
        rows //= 2
    return rows


def scores(queries, keys, query_spots, key_spots):
    raw = dot_last(queries, keys)
    bent = jnp.tanh(raw * (queries.shape[-1] ** (-0.5) / SOFT_CAP))
    return bent, jnp.where(key_spots <= query_spots, jnp.exp(SOFT_CAP * bent), 0.0)


def attend_forward(queries, keys, values, query_spots, key_spots):
    tokens, width = queries.shape
    count = keys.shape[0]
    rows = query_rows(tokens, count)

    def kernel(q_ref, k_ref, v_ref, spot_ref, key_spot_ref, total_ref, summed_ref, mixed_ref):
        _, weight = scores(q_ref[...], k_ref[...], spot_ref[...], key_spot_ref[...])
        total = jnp.sum(weight, axis=-1, keepdims=True)
        summed = jnp.dot(weight.astype(BF16), v_ref[...], preferred_element_type=F32)
        total_ref[...] = total
        summed_ref[...] = summed
        mixed_ref[...] = (summed / total).astype(BF16)

    def block(size):
        return pl.BlockSpec((rows, size), lambda j: (j, 0))

    return pl.pallas_call(
        kernel,
        out_shape=[
            jax.ShapeDtypeStruct((tokens, 1), F32),
            jax.ShapeDtypeStruct((tokens, width), F32),
            jax.ShapeDtypeStruct((tokens, width), BF16),
        ],
        grid=(tokens // rows,),
        in_specs=[block(width)] + [whole((count, width))] * 2 + [block(1), whole((1, count))],
        out_specs=[block(1), block(width), block(width)],
        compiler_params=pltpu.CompilerParams(vmem_limit_bytes=40 << 20),
        cost_estimate=pl.CostEstimate(
            flops=int(ATTEND_WEIGHT * 1e-6 * PEAK), bytes_accessed=0, transcendentals=0
        ),
        name="attend_forward",
    )(queries, keys, values, query_spots[:, None], key_spots[None, :])


def attend_backward(queries, keys, values, query_spots, key_spots, total, summed, grad_mixed, core):
    tokens, width = queries.shape
    count = keys.shape[0]
    rows = query_rows(tokens, count)

    def kernel(
        core_ref, q_ref, k_ref, v_ref, spot_ref, key_spot_ref, total_ref, summed_ref, grad_ref,
        query_out, kept_ref, given_ref, key_sums, value_sums,
    ):
        queries, keys = q_ref[...], k_ref[...]
        bent, weight = scores(queries, keys, spot_ref[...], key_spot_ref[...])
        total, grad_mixed = total_ref[...], grad_ref[...]
        grad_summed = (grad_mixed / total).astype(BF16)
        delta = jnp.sum(grad_mixed * summed_ref[...], axis=-1, keepdims=True) / (total * total)
        grad_weight = dot_last(grad_summed, v_ref[...]) - delta
        scale = width ** (-0.5)
        grad_raw = (weight * grad_weight * (1.0 - bent * bent) * scale).astype(BF16)
        query_out[...] = jnp.dot(grad_raw, keys, preferred_element_type=F32)
        grad_keys = dot_rows(grad_raw, queries)
        grad_values = dot_rows(weight.astype(BF16), grad_summed)
        turn = pl.program_id(0)

        @pl.when(turn == 0)
        def _():
            key_sums[...] = grad_keys
            value_sums[...] = grad_values

        @pl.when(turn > 0)
        def _():
            key_sums[...] += grad_keys
            value_sums[...] += grad_values

        @pl.when(turn == pl.num_programs(0) - 1)
        def _():
            has_keys = core_ref[0] == 0
            kept_ref[...] = jnp.where(has_keys, key_sums[...], value_sums[...])
            given_ref[...] = jnp.where(has_keys, value_sums[...], key_sums[...]).astype(BF16)

    def block(size):
        return pl.BlockSpec((rows, size), lambda j, *_: (j, 0))

    def all_of(shape):
        return pl.BlockSpec(shape, lambda j, *_: (0, 0), pipeline_mode=pl.Buffered(1))

    return pl.pallas_call(
        kernel,
        out_shape=[
            jax.ShapeDtypeStruct((tokens, width), F32),
            jax.ShapeDtypeStruct((count, width), F32),
            jax.ShapeDtypeStruct((count, width), BF16),
        ],
        grid_spec=pltpu.PrefetchScalarGridSpec(
            num_scalar_prefetch=1,
            grid=(tokens // rows,),
            in_specs=[block(width)]
            + [all_of((count, width))] * 2
            + [block(1), all_of((1, count)), block(1), block(width), block(width)],
            out_specs=[block(width)] + [all_of((count, width))] * 2,
            scratch_shapes=[pltpu.VMEM((count, width), F32)] * 2,
        ),
        compiler_params=pltpu.CompilerParams(vmem_limit_bytes=56 << 20),
        cost_estimate=pl.CostEstimate(
            flops=int(ATTEND_BACK_WEIGHT * 1e-6 * PEAK), bytes_accessed=0, transcendentals=0
        ),
        name="attend_backward",
    )(
        core.reshape(1), queries, keys, values, query_spots[:, None], key_spots[None, :],
        total, summed, grad_mixed,
    )


GELU_SCALE = 0.7978845608028654
GELU_CUBE = 0.044715


def dot_last(left, right):
    return lax.dot_general(left, right, LAST, preferred_element_type=F32)


def dot_rows(left, right):
    return lax.dot_general(left, right, ROWS, preferred_element_type=F32)


def hidden_step(units):
    return 384 if units % 384 == 0 else units


def whole(shape):
    return pl.BlockSpec(shape, lambda j: (0,) * len(shape), pipeline_mode=pl.Buffered(1))


def columns(rows, step, first=0):
    return pl.BlockSpec((rows, step), lambda j: (0, first + j))


def gate_and_up(normed, gate_weight, up_shrink):
    tokens, width = normed.shape
    units = gate_weight.shape[1]
    step = hidden_step(units)

    def kernel(x_ref, gate_w, up_w, gate_ref, up_ref, inner_ref):
        weights = jnp.concatenate([gate_w[...], up_w[...]], axis=1)
        both = jnp.dot(x_ref[...], weights, preferred_element_type=F32)
        gate, up = both[:, :step], both[:, step:]
        gate_ref[...] = gate
        up_ref[...] = up
        bend = jnp.tanh(GELU_SCALE * (gate + GELU_CUBE * gate * gate * gate))
        inner_ref[...] = (0.5 * gate * (1.0 + bend) * up).astype(BF16)

    size = tokens * units
    return pl.pallas_call(
        kernel,
        out_shape=[jax.ShapeDtypeStruct((tokens, units), kind) for kind in (F32, F32, BF16)],
        grid=(units // step,),
        in_specs=[whole((tokens, width)), columns(width, step), columns(width, step)],
        out_specs=[columns(tokens, step)] * 3,
        compiler_params=pltpu.CompilerParams(vmem_limit_bytes=32 << 20),
        cost_estimate=pl.CostEstimate(
            flops=4 * size * width, bytes_accessed=4 * units * width, transcendentals=size
        ),
        name="gate_and_up",
    )(normed, gate_weight, up_shrink)


def gate_and_up_back(grad_feed, gate, up, up_shrink):
    tokens, width = grad_feed.shape
    units = gate.shape[1]
    step = hidden_step(units)

    def kernel(feed_ref, gate_ref, up_ref, shrink_w, out_ref):
        grad_inner = jnp.dot(feed_ref[...], shrink_w[...], preferred_element_type=F32)
        gate, up = gate_ref[...], up_ref[...]
        square = gate * gate
        bend = jnp.tanh(GELU_SCALE * (gate + GELU_CUBE * gate * square))
        slope = 0.5 * (1.0 + bend) + 0.5 * gate * (1.0 - bend * bend) * (
            GELU_SCALE * (1.0 + 3.0 * GELU_CUBE * square)
        )
        first = pl.multiple_of(pl.program_id(0) * step, TILE)
        out_ref[:, pl.ds(first, step)] = (grad_inner * up * slope).astype(BF16)
        out_ref[:, pl.ds(units + first, step)] = (
            grad_inner * (0.5 * gate * (1.0 + bend))
        ).astype(BF16)

    size = tokens * units
    return pl.pallas_call(
        kernel,
        out_shape=jax.ShapeDtypeStruct((tokens, 2 * units), BF16),
        grid=(units // step,),
        in_specs=[whole((tokens, width))]
        + [columns(tokens, step)] * 2
        + [columns(width, step, units // step)],
        out_specs=pl.BlockSpec((tokens, 2 * units), lambda j: (0, 0)),
        compiler_params=pltpu.CompilerParams(vmem_limit_bytes=32 << 20),
        cost_estimate=pl.CostEstimate(
            flops=2 * size * width, bytes_accessed=2 * units * width, transcendentals=size
        ),
        name="gate_and_up_back",
    )(grad_feed, gate, up, up_shrink)


def body(
    hidden_in,
    out_cotangent,
    block_table,
    attend_weight,
    attend_moment,
    attend_square,
    output_weight,
    output_moment,
    output_square,
    expand_weight,
    expand_moment,
    expand_square,
    shrink_weight,
    shrink_moment,
    shrink_square,
    gains_weight,
    gains_moment,
    gains_square,
):
    grid = Grid()
    core = grid.core
    half_rows = hidden_in.shape[0] // 2
    local_width, group_count, slot_count, head_width = attend_weight.shape

    line_table = block_table.reshape(LINES, grid.plane, 2).transpose(1, 2, 0)
    offsets = jnp.arange(half_rows, dtype=jnp.int32)
    all_spots = (line_table[..., None] * half_rows + offsets).reshape(grid.plane, -1)
    own_spots = grid.first_half(pick(all_spots, grid.place))
    key_spots = all_spots.reshape(-1)
    line_rows = own_spots.shape[0]
    half = line_rows // 2

    own_in = lax.dynamic_slice_in_dim(hidden_in, core * half_rows, half_rows)
    own_out = lax.dynamic_slice_in_dim(out_cotangent, core * half_rows, half_rows)
    line_in = lax.all_gather(own_in, "line", axis=0, tiled=True)
    all_in = jnp.concatenate([line_in, grid.across(line_in)], axis=0)

    def by_group(own, other):
        got = grid.across(other)
        return jnp.where(core == 0, jnp.concatenate([own, got]), jnp.concatenate([got, own]))

    def group_return(blocks):
        halves = blocks.reshape((2, group_count) + blocks.shape[1:])
        return pick(halves, core), grid.across(pick(halves, 1 - core))

    attend_columns = 2 * head_width + TILE
    output_pack = (
        output_weight.astype(BF16)
        .reshape(group_count, 2, head_width, local_width)
        .transpose(1, 0, 3, 2)
    )
    packs = pack_attend(attend_weight, gains_weight, core)
    packs = [
        jnp.concatenate([pack, pick(output_pack, member)], axis=2)
        for pack, member in zip(packs, (core, 1 - core), strict=True)
    ]
    joined_rows_here = grid.line_swap(by_group(*packs))
    attend_rows_here = joined_rows_here[..., :attend_columns]
    output_rows_here = joined_rows_here[..., attend_columns:]
    gate_pack, up_pack = pack_expand(expand_weight)
    attend_and_gains = grid.spread(attend_rows_here)
    attend_full = attend_and_gains[:, : 2 * head_width]
    gain_count = gains_weight.shape[0]
    gains_all = attend_and_gains[:, 2 * head_width :][:, :gain_count].T.astype(F32)

    gate_rows_here = grid.line_swap(after(gate_pack, joined_rows_here))
    units = gate_rows_here.shape[2]
    gate_full = grid.bulk_spread(gate_rows_here)
    shrink_pack = pack_shrink(after(shrink_weight, attend_rows_here))
    up_shrink_pack = jnp.concatenate([up_pack, shrink_pack], axis=2)

    normed_plain = plain_norm(all_in)
    normed_line = (normed_plain * (1.0 + gains_all[0])).astype(BF16)
    projected = jnp.dot(
        after(normed_line, gate_rows_here), attend_full, preferred_element_type=F32
    )
    up_shrink_rows_here = grid.line_swap(after(up_shrink_pack, gate_rows_here))
    up_shrink_full = grid.bulk_spread(up_shrink_rows_here)
    cosine, sine_table = rope_tables(own_spots, head_width)
    pair_pre = projected[:, head_width:]
    pair_b = jnp.where(core == 0, rotate(pair_pre, cosine, sine_table), pair_pre).astype(BF16)
    pair_parts = grid.plane_gather(grid.first_half(pair_b))
    queries_b = rotate(projected[:, :head_width], cosine, sine_table).astype(BF16)
    pair_all = jnp.zeros((grid.plane,) + pair_b.shape, BF16)
    for mask, part in pair_parts.items():
        pair_all = put(pair_all, part, grid.place_of(mask))
    pair_all = pair_all.reshape(-1, head_width)
    pair_other = grid.across(pair_all)

    output_full = grid.spread(after(output_rows_here, pair_parts[3]))

    keys_b = jnp.where(core == 0, pair_all, pair_other)
    values_b = jnp.where(core == 0, pair_other, pair_all)
    row_total, summed, mixed_b = attend_forward(queries_b, keys_b, values_b, own_spots, key_spots)

    def halves_last(*pairs):
        other = sum(dot_last(left[half:], right) for left, right in pairs).astype(BF16)
        own = sum(dot_last(after(left[:half], other), right) for left, right in pairs)
        return own, other

    attend_sum = grid.token_reduce(*halves_last((after(mixed_b, up_shrink_rows_here), output_full)))

    hidden = own_in.astype(F32)
    first_sum = hidden + norm_apply(attend_sum, gains_all[1])
    normed_two_b = norm_apply(first_sum, gains_all[2]).astype(BF16)
    normed_two_line = grid.token_gather(normed_two_b, gate_full)
    gate_act, up_act, inner_b = gate_and_up(normed_two_line, gate_full, up_shrink_full)
    up_full, shrink_full = up_shrink_full[:, :units], up_shrink_full[:, units:]
    feed_sum = grid.token_reduce(*halves_last((inner_b, shrink_full)))
    own_hidden_out = (first_sum + norm_apply(feed_sum, gains_all[3])).astype(BF16)

    grad_out = own_out.astype(F32)
    grad_feed, gain_four = norm_back(feed_sum, gains_all[3], grad_out)
    grad_feed_line = grid.token_gather(grad_feed.astype(BF16))
    shrink_terms = dot_rows(grad_feed_line, inner_b).astype(BF16)
    shrink_sums = grid.bulk_sum(shrink_terms)
    grad_both_b = gate_and_up_back(after(grad_feed_line, shrink_terms), gate_act, up_act, up_shrink_full)
    expand_terms = dot_rows(normed_two_line, grad_both_b).astype(BF16)
    expand_sums = grid.bulk_sum(expand_terms)
    grad_both_b = after(grad_both_b, expand_terms)
    grad_two_parts = halves_last(
        (grad_both_b[:, :units], gate_full), (grad_both_b[:, units:], up_full)
    )
    grad_two = grid.token_reduce(*grad_two_parts)

    grad_first_norm, gain_three = norm_back(first_sum, gains_all[2], grad_two)
    grad_first = grad_out + grad_first_norm
    grad_attend, gain_two = norm_back(attend_sum, gains_all[1], grad_first)
    grad_attend_line = grid.token_gather(grad_attend.astype(BF16))
    grad_mixed = jnp.dot(grad_attend_line, output_full, preferred_element_type=F32)
    grad_query, kept, given = attend_backward(
        queries_b, keys_b, values_b, own_spots, key_spots, row_total, summed, grad_mixed, core
    )
    pair_terms = kept + grid.across(given).astype(F32)
    pair_terms = pair_terms.astype(BF16).reshape(grid.plane, line_rows, head_width)
    pair_grad = grid.plane_reduce(
        {m: pick(pair_terms, grid.place_of(m)) for m in range(grid.plane)}
    )
    pair_grad = grid.first_half(pair_grad)
    output_terms = dot_rows(grad_attend_line, mixed_b).astype(BF16)
    grad_query_pre = rotate(grad_query, cosine, -sine_table)
    grad_pair_pre = jnp.where(core == 0, rotate(pair_grad, cosine, -sine_table), pair_grad)
    grad_proj_b = jnp.concatenate([grad_query_pre, grad_pair_pre], axis=1).astype(BF16)
    shrink_back = grid.line_swap(after(shrink_sums, grad_attend_line))
    own_part, other_part = halves_last((after(grad_proj_b, shrink_back), attend_full))
    gain_one = jnp.sum(own_part * normed_plain[:half], axis=0) + jnp.sum(
        other_part.astype(F32) * normed_plain[half:], axis=0
    )
    grad_normed = grid.token_reduce(own_part, other_part)
    own_hidden_grad = last_grad(own_in, gains_all[0], grad_normed, grad_first)
    expand_back = grid.line_swap(after(expand_sums, shrink_back))

    gain_terms = jnp.stack([gain_one, gain_two, gain_three, gain_four], axis=1)
    gain_terms = jnp.pad(gain_terms, ((0, 0), (2 * head_width, TILE - gain_count)))
    attend_terms = dot_rows(normed_line, jnp.pad(grad_proj_b, ((0, 0), (0, TILE)))) + gain_terms
    joined_terms = jnp.concatenate([attend_terms.astype(BF16), output_terms], axis=1)
    joined_sums = grid.bulk_sum(joined_terms)
    joined = grid.line_swap(after(joined_sums, expand_back))
    attend_line = joined[..., :attend_columns]
    output_back = group_return(joined[..., attend_columns:])
    attend_back = group_return(attend_line)
    gain_parts = attend_line[:, :, 2 * head_width : 2 * head_width + gain_count]
    gains_grad = jnp.sum(gain_parts.astype(F32), axis=0).T
    gains_grad = gains_grad + grid.across(gains_grad)

    def both_halves(value):
        other = grid.across(value)
        return jnp.where(
            core == 0, jnp.concatenate([value, other]), jnp.concatenate([other, value])
        )

    hidden_out = both_halves(own_hidden_out)
    hidden_grad = both_halves(own_hidden_grad)

    shrink_new = adam_shrink(shrink_weight, shrink_moment, shrink_square, shrink_back)
    expand_new = adam_expand(expand_weight, expand_moment, expand_square, expand_back)
    attend_new = adam_attend(
        attend_weight, attend_moment, attend_square, attend_back[0], attend_back[1], core
    )
    output_heads = jnp.where(core == 0, jnp.stack(output_back), jnp.stack(output_back[::-1]))
    output_grad = output_heads.transpose(1, 0, 3, 2).reshape(output_weight.shape).astype(F32)
    output_new = adam_step(
        output_weight, output_moment, output_square, output_grad, RATE_MATRIX, DECAY
    )
    gains_new = adam_step(
        gains_weight, gains_moment, gains_square, gains_grad, RATE_GAIN, 0.0
    )
    return (
        hidden_out,
        hidden_grad,
        *attend_new,
        output_grad,
        *output_new,
        *expand_new,
        *shrink_new,
        gains_grad,
        *gains_new,
    )


def solution(mesh):
    count, cores = mesh.shape["ctx"], mesh.shape["head"]
    devices = mesh.devices.reshape(LINES, count // LINES, cores)
    fine = Mesh(devices, ("line", "place", "head"))
    ctx = ("line", "place")
    tokens = P(ctx, None)
    attend = P(ctx, "head", None, None)
    output = P("head", None, ctx)
    expand = P(ctx, None, "head")
    shrink = P("head", ctx)
    gains = P(None, ctx)
    in_specs = (tokens, tokens, P()) + sum(
        ((spec,) * 3 for spec in (attend, output, expand, shrink, gains)), ()
    )
    out_specs = (tokens, tokens) + sum(
        ((spec,) * 4 for spec in (attend, output, expand, shrink, gains)), ()
    )
    return jax.shard_map(body, mesh=fine, in_specs=in_specs, out_specs=out_specs, check_vma=False)
```

```python
import jax
import jax.numpy as jnp
from jax import lax
from jax.experimental import pallas as pl
from jax.experimental.pallas import tpu as pltpu
from jax.sharding import Mesh
from jax.sharding import PartitionSpec as P

STEP = 10


NORM_EPS = 1e-06
SOFT_CAP = 50.0
ROPE_BASE = 10000.0
RATE_MATRIX = 0.02
RATE_GAIN = 0.1
BETA_ONE = 0.9
BETA_TWO = 0.95
ADAM_EPS = 1e-08
DECAY = 0.1
ROWS = (((0,), (0,)), ((), ()))
LAST = (((1,), (1,)), ((), ()))
LINES = 4
F32 = jnp.float32
BF16 = jnp.bfloat16


def rope_tables(positions, head_width):
    exponent = jnp.arange(head_width // 2, dtype=F32) * (2.0 / head_width)
    frequency = ROPE_BASE ** (-exponent)
    angle = positions.astype(F32)[:, None] * frequency[None, :]
    return (jnp.cos(angle), jnp.sin(angle))


def rotate(values, cosine, sine_table):
    middle = values.shape[-1] // 2
    front_half = values[..., :middle]
    back_half = values[..., middle:]
    return jnp.concatenate(
        [
            front_half * cosine - back_half * sine_table,
            back_half * cosine + front_half * sine_table,
        ],
        axis=-1,
    )


def norm_factor(values):
    return lax.rsqrt(jnp.mean(values * values, axis=-1, keepdims=True) + NORM_EPS)


def norm_apply(values, norm_gain):
    return values * norm_factor(values) * (1.0 + norm_gain)


def norm_back(values, norm_gain, grad_out):
    factor = norm_factor(values)
    weighted = grad_out * (1.0 + norm_gain)
    grad_in = factor * weighted - values * factor * factor * factor * jnp.mean(
        values * weighted, axis=-1, keepdims=True
    )
    grad_gain = jnp.sum(grad_out * values * factor, axis=0)
    return (grad_in, grad_gain)


def adam_step(weight, moment, square, grad, rate, decay):
    moment_new = BETA_ONE * moment + (1.0 - BETA_ONE) * grad
    square_new = BETA_TWO * square + (1.0 - BETA_TWO) * grad * grad
    mean_hat = moment_new / (1.0 - BETA_ONE**STEP)
    power_hat = square_new / (1.0 - BETA_TWO**STEP)
    updated = weight - rate * (mean_hat / (jnp.sqrt(power_hat) + ADAM_EPS) + decay * weight)
    return (updated, moment_new, square_new)


def pick(array, index):
    return lax.dynamic_index_in_dim(array, index, 0, keepdims=False)


def put(array, part, index, dim=0):
    return lax.dynamic_update_slice_in_dim(array, jnp.expand_dims(part, dim), index, dim)


def mirror(number, bits):
    return sum(((number >> i) & 1) << (bits - 1 - i) for i in range(bits))


def after(value, *events):
    return lax.optimization_barrier((value,) + events)[0]


class Grid:
    def __init__(self):
        self.plane = lax.axis_size("place")
        self.bits = self.plane.bit_length() - 1
        self.line = lax.axis_index("line")
        self.place = lax.axis_index("place")
        self.core = lax.axis_index("head")

    def along(self, value, step):
        pairs = [(i, i ^ step) for i in range(LINES)]
        return lax.ppermute(value, "line", pairs)

    def across(self, value):
        return lax.ppermute(value, "head", [(0, 1), (1, 0)])

    def within(self, value, phase):
        pairs = []
        for i in range(self.plane):
            for core in range(2):
                bit = phase if core == 0 else self.bits - 1 - phase
                pairs.append((2 * i + core, 2 * (i ^ (1 << bit)) + core))
        return lax.ppermute(value, ("place", "head"), pairs)

    def place_of(self, mask):
        return self.place ^ jnp.where(self.core == 0, mask, mirror(mask, self.bits))

    def token_gather(self, value, *events):
        near = self.along(value, 1)
        far = self.along(value, 3)
        middle = self.along(far, 1)
        own = jnp.zeros((LINES,) + value.shape, value.dtype)
        for step, part in enumerate((value, near, middle, far)):
            own = put(own, part, self.line ^ step)
        own = own.reshape(-1, value.shape[-1])
        if events:
            own = after(own, *events)
        return jnp.concatenate([own, self.across(own)], axis=0)

    def token_reduce(self, own, other, *events):
        if events:
            other = after(other, *events)
        mine = (own + self.across(other).astype(F32)).reshape(LINES, -1, own.shape[-1])
        block = [pick(mine, self.line ^ step) for step in range(LINES)]
        passed = self.along(block[2].astype(BF16), 1)
        near = self.along(block[1].astype(BF16), 1)
        far = self.along((block[3] + passed.astype(F32)).astype(BF16), 3)
        return block[0] + near.astype(F32) + far.astype(F32)

    def line_swap(self, blocks):
        return lax.all_to_all(blocks, "line", split_axis=0, concat_axis=0, tiled=True)

    def plane_gather(self, own, *events):
        parts = {0: own}
        for phase in range(self.bits):
            for mask in range(1 << phase):
                given = parts[mask]
                if mask and events:
                    given = after(given, *events)
                parts[mask | (1 << phase)] = self.within(given, phase)
        return parts

    def plane_reduce(self, parts, *events):
        parts = dict(parts)
        for phase in reversed(range(self.bits)):
            for mask in reversed(range(1 << phase)):
                given = parts[mask | (1 << phase)]
                if phase == 0 and events:
                    given = after(given, *events)
                got = self.within(given, phase)
                parts[mask] = parts[mask] + got.astype(F32)
                if mask or phase:
                    parts[mask] = parts[mask].astype(BF16)
        return parts[0]

    def spread(self, own, *events):
        return self.assemble(self.plane_gather(own, *events))

    def assemble(self, parts):
        full = jnp.zeros((LINES, self.plane) + parts[0].shape[1:], parts[0].dtype)
        for mask, part in parts.items():
            full = put(full, part, self.place_of(mask), 1)
        return full.reshape(-1, parts[0].shape[-1])

    def bulk_spread(self, own):
        full = lax.all_gather(own, "place", axis=1, tiled=True)
        return full.reshape(-1, own.shape[-1])

    def bulk_sum(self, terms):
        shaped = terms.reshape(LINES, -1, terms.shape[-1])
        return lax.psum_scatter(shaped, "place", scatter_dimension=1, tiled=True)

    def all_terms(self, terms, *events):
        shaped = terms.reshape(LINES, self.plane, -1, terms.shape[-1])
        parts = {
            mask: lax.dynamic_index_in_dim(shaped, self.place_of(mask), 1, keepdims=False)
            for mask in range(self.plane)
        }
        return self.plane_reduce(parts, *events).astype(BF16)

    def first_half(self, values):
        half = values.shape[0] // 2
        swapped = jnp.concatenate([values[half:], values[:half]])
        return jnp.where(self.core == 0, values, swapped)


TILE = 128


def rows_per_step(local_width):
    return 16 if local_width % 16 == 0 else local_width


def attend_rows(array):
    rows, groups, slots, width = array.shape
    tiles = width // TILE
    shaped = array.reshape(rows, groups, slots, tiles, TILE).transpose(0, 1, 3, 2, 4)
    return shaped.reshape(-1, TILE)


def attend_from_rows(array, shape):
    rows, groups, slots, width = shape
    tiles = width // TILE
    shaped = array.reshape(rows, groups, tiles, slots, TILE).transpose(0, 1, 3, 2, 4)
    return shaped.reshape(shape)


def row_block(rows, height):
    return pl.BlockSpec((rows * height, TILE), lambda i, *_: (i, 0))


def pack_expand(weight):
    local_width, _, width = weight.shape
    rows = rows_per_step(local_width)
    quarter = width // LINES

    def kernel(in_ref, *out_refs):
        for gate, out_ref in enumerate(out_refs):
            for line in range(LINES):
                part = in_ref[:, gate, line * quarter : (line + 1) * quarter]
                out_ref[line] = part.astype(BF16)

    pack = jax.ShapeDtypeStruct((LINES, local_width, quarter), BF16)
    return pl.pallas_call(
        kernel,
        out_shape=[pack] * 2,
        grid=(local_width // rows,),
        in_specs=[pl.BlockSpec((rows, 2, width), lambda i: (i, 0, 0))],
        out_specs=[pl.BlockSpec((LINES, rows, quarter), lambda i: (0, i, 0))] * 2,
        compiler_params=pltpu.CompilerParams(vmem_limit_bytes=32 << 20),
        cost_estimate=pl.CostEstimate(flops=0, bytes_accessed=6 * weight.size, transcendentals=0),
        name="pack_expand",
    )(weight)


def pack_shrink(weight):
    width, local_width = weight.shape
    rows = rows_per_step(local_width)
    quarter = width // LINES

    def kernel(in_ref, out_ref):
        for line in range(LINES):
            out_ref[line] = in_ref[:, line * quarter : (line + 1) * quarter].astype(BF16)

    return pl.pallas_call(
        kernel,
        out_shape=jax.ShapeDtypeStruct((LINES, local_width, quarter), BF16),
        grid=(local_width // rows,),
        in_specs=[pl.BlockSpec((rows, width), lambda i: (i, 0))],
        out_specs=pl.BlockSpec((LINES, rows, quarter), lambda i: (0, i, 0)),
        compiler_params=pltpu.CompilerParams(vmem_limit_bytes=32 << 20),
        cost_estimate=pl.CostEstimate(flops=0, bytes_accessed=6 * weight.size, transcendentals=0),
        name="pack_shrink",
    )(weight.T)


def pack_attend(weight, gains, core):
    local_width, groups, slots, width = weight.shape
    rows = rows_per_step(local_width)
    tiles = width // TILE
    height = groups * slots * tiles
    columns = 2 * width + TILE

    def kernel(core_ref, in_ref, gains_ref, own_ref, other_ref):
        for out_ref, member in ((own_ref, core_ref[0]), (other_ref, 1 - core_ref[0])):
            for group in range(groups):
                for pair in range(2):
                    for tile in range(tiles):
                        first = (group * tiles + tile) * slots + 2 * pair
                        chosen = pl.ds(first + member, rows, stride=height)
                        column = (pair * tiles + tile) * TILE
                        out_ref[group, :, column : column + TILE] = in_ref[chosen, :].astype(BF16)
                out_ref[group, :, 2 * width :] = gains_ref[...].astype(BF16)

    pack = jax.ShapeDtypeStruct((groups, local_width, columns), BF16)
    gain_columns = jnp.pad(gains.T, ((0, 0), (0, TILE - gains.shape[0])))
    return pl.pallas_call(
        kernel,
        out_shape=[pack] * 2,
        grid_spec=pltpu.PrefetchScalarGridSpec(
            num_scalar_prefetch=1,
            grid=(local_width // rows,),
            in_specs=[
                row_block(rows, height),
                pl.BlockSpec((rows, TILE), lambda i, *_: (i, 0)),
            ],
            out_specs=[pl.BlockSpec((groups, rows, columns), lambda i, *_: (0, i, 0))] * 2,
        ),
        compiler_params=pltpu.CompilerParams(vmem_limit_bytes=32 << 20),
        cost_estimate=pl.CostEstimate(flops=0, bytes_accessed=6 * weight.size, transcendentals=0),
        name="pack_attend",
    )(core.reshape(1), attend_rows(weight), gain_columns)


def adam_tile(grad, chosen, in_refs, out_refs):
    weight, moment, square = (ref[chosen] for ref in in_refs)
    updated = adam_step(weight, moment, square, grad, RATE_MATRIX, DECAY)
    for ref, value in zip(out_refs, (grad,) + updated, strict=True):
        ref[chosen] = value


def adam_call(kernel, scalars, grads, grad_specs, states, state_spec, steps, name, weight):
    return pl.pallas_call(
        kernel,
        out_shape=[jax.ShapeDtypeStruct(states[0].shape, F32)] * 4,
        grid_spec=pltpu.PrefetchScalarGridSpec(
            num_scalar_prefetch=len(scalars),
            grid=(steps,),
            in_specs=grad_specs + [state_spec] * 3,
            out_specs=[state_spec] * 4,
        ),
        compiler_params=pltpu.CompilerParams(vmem_limit_bytes=40 << 20),
        cost_estimate=waiting(weight),
        name=name,
    )(*scalars, *grads, *states)


def adam_expand(weight, moment, square, grad):
    local_width, _, width = weight.shape
    rows = rows_per_step(local_width)
    quarter = width // LINES

    def kernel(grad_ref, *refs):
        for gate in range(2):
            for line in range(LINES):
                chosen = (slice(None), gate, slice(line * quarter, (line + 1) * quarter))
                grad = grad_ref[line, :, gate * quarter : (gate + 1) * quarter]
                adam_tile(grad.astype(F32), chosen, refs[:3], refs[3:])

    return adam_call(
        kernel,
        (),
        [grad],
        [pl.BlockSpec((LINES, rows, 2 * quarter), lambda i: (0, i, 0))],
        [weight, moment, square],
        pl.BlockSpec((rows, 2, width), lambda i: (i, 0, 0)),
        local_width // rows,
        "adam_expand",
        60,
    )


def adam_attend(weight, moment, square, own, other, core):
    shape = weight.shape
    local_width, groups, slots, width = shape
    rows = rows_per_step(local_width)
    tiles = width // TILE
    height = groups * slots * tiles

    def kernel(core_ref, own_ref, other_ref, *refs):
        in_refs, out_refs = refs[:3], refs[3:]
        for grad_ref, member in ((own_ref, core_ref[0]), (other_ref, 1 - core_ref[0])):
            for group in range(groups):
                for pair in range(2):
                    for tile in range(tiles):
                        first = (group * tiles + tile) * slots + 2 * pair
                        chosen = (pl.ds(first + member, rows, stride=height), slice(None))
                        column = (pair * tiles + tile) * TILE
                        grad = grad_ref[group, :, column : column + TILE].astype(F32)
                        adam_tile(grad, chosen, in_refs, out_refs)

    results = adam_call(
        kernel,
        (core.reshape(1),),
        [own, other],
        [pl.BlockSpec((groups, rows, own.shape[-1]), lambda i, *_: (0, i, 0))] * 2,
        [attend_rows(a) for a in (weight, moment, square)],
        row_block(rows, height),
        local_width // rows,
        "adam_attend",
        10,
    )
    return [attend_from_rows(a, shape) for a in results]


def adam_shrink(weight, moment, square, grad):
    width, local_width = weight.shape
    rows = rows_per_step(local_width)
    quarter = width // LINES

    def kernel(grad_ref, *refs):
        for line in range(LINES):
            chosen = (slice(None), slice(line * quarter, (line + 1) * quarter))
            adam_tile(grad_ref[line].astype(F32), chosen, refs[:3], refs[3:])

    results = adam_call(
        kernel,
        (),
        [grad],
        [pl.BlockSpec((LINES, rows, quarter), lambda i: (0, i, 0))],
        [a.T for a in (weight, moment, square)],
        pl.BlockSpec((rows, width), lambda i: (i, 0)),
        local_width // rows,
        "adam_shrink",
        40,
    )
    return [a.T for a in results]


LINE_WEIGHT = 90
OWN_WEIGHT = 3


def waiting(microseconds):
    return pl.CostEstimate(
        flops=int(microseconds * 1e-6 * PEAK), bytes_accessed=0, transcendentals=0
    )


def plain_norm(values):
    tokens, width = values.shape
    rows = tokens // 2

    def kernel(in_ref, out_ref):
        wide = in_ref[...].astype(F32)
        out_ref[...] = wide * norm_factor(wide)

    block = pl.BlockSpec((rows, width), lambda j: (j, 0))
    return pl.pallas_call(
        kernel,
        out_shape=jax.ShapeDtypeStruct((tokens, width), F32),
        grid=(2,),
        in_specs=[block],
        out_specs=block,
        compiler_params=pltpu.CompilerParams(vmem_limit_bytes=24 << 20),
        cost_estimate=waiting(LINE_WEIGHT),
        name="plain_norm",
    )(values)


def last_grad(values, gain, grad_out, carried):
    def kernel(value_ref, gain_ref, grad_ref, carried_ref, out_ref):
        wide = value_ref[...].astype(F32)
        factor = norm_factor(wide)
        weighted = grad_ref[...] * (1.0 + gain_ref[...])
        mean = jnp.mean(wide * weighted, axis=-1, keepdims=True)
        out_ref[...] = carried_ref[...] + (
            factor * weighted - wide * factor * factor * factor * mean
        )

    return pl.pallas_call(
        kernel,
        out_shape=jax.ShapeDtypeStruct(values.shape, F32),
        compiler_params=pltpu.CompilerParams(vmem_limit_bytes=24 << 20),
        cost_estimate=waiting(OWN_WEIGHT),
        name="last_grad",
    )(values, gain[None], grad_out, carried)


PEAK = 1.15e15
ATTEND_WEIGHT = 45
ATTEND_BACK_WEIGHT = 100


def query_rows(tokens, keys):
    rows = tokens
    while rows > 64 and rows * keys > 1 << 19:
        rows //= 2
    return rows


def scores(queries, keys, query_spots, key_spots):
    raw = dot_last(queries, keys)
    bent = jnp.tanh(raw * (queries.shape[-1] ** (-0.5) / SOFT_CAP))
    return bent, jnp.where(key_spots <= query_spots, jnp.exp(SOFT_CAP * bent), 0.0)


def attend_forward(queries, keys, values, query_spots, key_spots):
    tokens, width = queries.shape
    count = keys.shape[0]
    rows = query_rows(tokens, count)

    def kernel(q_ref, k_ref, v_ref, spot_ref, key_spot_ref, total_ref, summed_ref, mixed_ref):
        _, weight = scores(q_ref[...], k_ref[...], spot_ref[...], key_spot_ref[...])
        total = jnp.sum(weight, axis=-1, keepdims=True)
        summed = jnp.dot(weight.astype(BF16), v_ref[...], preferred_element_type=F32)
        total_ref[...] = total
        summed_ref[...] = summed
        mixed_ref[...] = (summed / total).astype(BF16)

    def block(size):
        return pl.BlockSpec((rows, size), lambda j: (j, 0))

    return pl.pallas_call(
        kernel,
        out_shape=[
            jax.ShapeDtypeStruct((tokens, 1), F32),
            jax.ShapeDtypeStruct((tokens, width), F32),
            jax.ShapeDtypeStruct((tokens, width), BF16),
        ],
        grid=(tokens // rows,),
        in_specs=[block(width)] + [whole((count, width))] * 2 + [block(1), whole((1, count))],
        out_specs=[block(1), block(width), block(width)],
        compiler_params=pltpu.CompilerParams(vmem_limit_bytes=40 << 20),
        cost_estimate=pl.CostEstimate(
            flops=int(ATTEND_WEIGHT * 1e-6 * PEAK), bytes_accessed=0, transcendentals=0
        ),
        name="attend_forward",
    )(queries, keys, values, query_spots[:, None], key_spots[None, :])


def attend_backward(queries, keys, values, query_spots, key_spots, total, summed, grad_mixed, core):
    tokens, width = queries.shape
    count = keys.shape[0]
    rows = query_rows(tokens, count)

    def kernel(
        core_ref, q_ref, k_ref, v_ref, spot_ref, key_spot_ref, total_ref, summed_ref, grad_ref,
        query_out, kept_ref, given_ref, key_sums, value_sums,
    ):
        queries, keys = q_ref[...], k_ref[...]
        bent, weight = scores(queries, keys, spot_ref[...], key_spot_ref[...])
        total, grad_mixed = total_ref[...], grad_ref[...]
        grad_summed = (grad_mixed / total).astype(BF16)
        delta = jnp.sum(grad_mixed * summed_ref[...], axis=-1, keepdims=True) / (total * total)
        grad_weight = dot_last(grad_summed, v_ref[...]) - delta
        scale = width ** (-0.5)
        grad_raw = (weight * grad_weight * (1.0 - bent * bent) * scale).astype(BF16)
        query_out[...] = jnp.dot(grad_raw, keys, preferred_element_type=F32)
        grad_keys = dot_rows(grad_raw, queries)
        grad_values = dot_rows(weight.astype(BF16), grad_summed)
        turn = pl.program_id(0)

        @pl.when(turn == 0)
        def _():
            key_sums[...] = grad_keys
            value_sums[...] = grad_values

        @pl.when(turn > 0)
        def _():
            key_sums[...] += grad_keys
            value_sums[...] += grad_values

        @pl.when(turn == pl.num_programs(0) - 1)
        def _():
            has_keys = core_ref[0] == 0
            kept_ref[...] = jnp.where(has_keys, key_sums[...], value_sums[...])
            given_ref[...] = jnp.where(has_keys, value_sums[...], key_sums[...]).astype(BF16)

    def block(size):
        return pl.BlockSpec((rows, size), lambda j, *_: (j, 0))

    def all_of(shape):
        return pl.BlockSpec(shape, lambda j, *_: (0, 0), pipeline_mode=pl.Buffered(1))

    return pl.pallas_call(
        kernel,
        out_shape=[
            jax.ShapeDtypeStruct((tokens, width), F32),
            jax.ShapeDtypeStruct((count, width), F32),
            jax.ShapeDtypeStruct((count, width), BF16),
        ],
        grid_spec=pltpu.PrefetchScalarGridSpec(
            num_scalar_prefetch=1,
            grid=(tokens // rows,),
            in_specs=[block(width)]
            + [all_of((count, width))] * 2
            + [block(1), all_of((1, count)), block(1), block(width), block(width)],
            out_specs=[block(width)] + [all_of((count, width))] * 2,
            scratch_shapes=[pltpu.VMEM((count, width), F32)] * 2,
        ),
        compiler_params=pltpu.CompilerParams(vmem_limit_bytes=56 << 20),
        cost_estimate=pl.CostEstimate(
            flops=int(ATTEND_BACK_WEIGHT * 1e-6 * PEAK), bytes_accessed=0, transcendentals=0
        ),
        name="attend_backward",
    )(
        core.reshape(1), queries, keys, values, query_spots[:, None], key_spots[None, :],
        total, summed, grad_mixed,
    )


GELU_SCALE = 0.7978845608028654
GELU_CUBE = 0.044715


def dot_last(left, right):
    return lax.dot_general(left, right, LAST, preferred_element_type=F32)


def dot_rows(left, right):
    return lax.dot_general(left, right, ROWS, preferred_element_type=F32)


def hidden_step(units):
    return 384 if units % 384 == 0 else units


def whole(shape):
    return pl.BlockSpec(shape, lambda j: (0,) * len(shape), pipeline_mode=pl.Buffered(1))


def columns(rows, step, first=0):
    return pl.BlockSpec((rows, step), lambda j: (0, first + j))


def gate_and_up(normed, gate_weight, up_shrink):
    tokens, width = normed.shape
    units = gate_weight.shape[1]
    step = hidden_step(units)

    def kernel(x_ref, gate_w, up_w, gate_ref, up_ref, inner_ref):
        weights = jnp.concatenate([gate_w[...], up_w[...]], axis=1)
        both = jnp.dot(x_ref[...], weights, preferred_element_type=F32)
        gate, up = both[:, :step], both[:, step:]
        gate_ref[...] = gate
        up_ref[...] = up
        bend = jnp.tanh(GELU_SCALE * (gate + GELU_CUBE * gate * gate * gate))
        inner_ref[...] = (0.5 * gate * (1.0 + bend) * up).astype(BF16)

    size = tokens * units
    return pl.pallas_call(
        kernel,
        out_shape=[jax.ShapeDtypeStruct((tokens, units), kind) for kind in (F32, F32, BF16)],
        grid=(units // step,),
        in_specs=[whole((tokens, width)), columns(width, step), columns(width, step)],
        out_specs=[columns(tokens, step)] * 3,
        compiler_params=pltpu.CompilerParams(vmem_limit_bytes=32 << 20),
        cost_estimate=pl.CostEstimate(
            flops=4 * size * width, bytes_accessed=4 * units * width, transcendentals=size
        ),
        name="gate_and_up",
    )(normed, gate_weight, up_shrink)


def gate_and_up_back(grad_feed, gate, up, up_shrink):
    tokens, width = grad_feed.shape
    units = gate.shape[1]
    step = hidden_step(units)

    def kernel(feed_ref, gate_ref, up_ref, shrink_w, out_ref):
        grad_inner = jnp.dot(feed_ref[...], shrink_w[...], preferred_element_type=F32)
        gate, up = gate_ref[...], up_ref[...]
        square = gate * gate
        bend = jnp.tanh(GELU_SCALE * (gate + GELU_CUBE * gate * square))
        slope = 0.5 * (1.0 + bend) + 0.5 * gate * (1.0 - bend * bend) * (
            GELU_SCALE * (1.0 + 3.0 * GELU_CUBE * square)
        )
        first = pl.multiple_of(pl.program_id(0) * step, TILE)
        out_ref[:, pl.ds(first, step)] = (grad_inner * up * slope).astype(BF16)
        out_ref[:, pl.ds(units + first, step)] = (
            grad_inner * (0.5 * gate * (1.0 + bend))
        ).astype(BF16)

    size = tokens * units
    return pl.pallas_call(
        kernel,
        out_shape=jax.ShapeDtypeStruct((tokens, 2 * units), BF16),
        grid=(units // step,),
        in_specs=[whole((tokens, width))]
        + [columns(tokens, step)] * 2
        + [columns(width, step, units // step)],
        out_specs=pl.BlockSpec((tokens, 2 * units), lambda j: (0, 0)),
        compiler_params=pltpu.CompilerParams(vmem_limit_bytes=32 << 20),
        cost_estimate=pl.CostEstimate(
            flops=2 * size * width, bytes_accessed=2 * units * width, transcendentals=size
        ),
        name="gate_and_up_back",
    )(grad_feed, gate, up, up_shrink)


def body(
    hidden_in,
    out_cotangent,
    block_table,
    attend_weight,
    attend_moment,
    attend_square,
    output_weight,
    output_moment,
    output_square,
    expand_weight,
    expand_moment,
    expand_square,
    shrink_weight,
    shrink_moment,
    shrink_square,
    gains_weight,
    gains_moment,
    gains_square,
):
    grid = Grid()
    core = grid.core
    half_rows = hidden_in.shape[0] // 2
    local_width, group_count, slot_count, head_width = attend_weight.shape

    line_table = block_table.reshape(LINES, grid.plane, 2).transpose(1, 2, 0)
    offsets = jnp.arange(half_rows, dtype=jnp.int32)
    all_spots = (line_table[..., None] * half_rows + offsets).reshape(grid.plane, -1)
    own_spots = grid.first_half(pick(all_spots, grid.place))
    key_spots = all_spots.reshape(-1)
    line_rows = own_spots.shape[0]
    half = line_rows // 2

    own_in = lax.dynamic_slice_in_dim(hidden_in, core * half_rows, half_rows)
    own_out = lax.dynamic_slice_in_dim(out_cotangent, core * half_rows, half_rows)
    line_in = lax.all_gather(own_in, "line", axis=0, tiled=True)
    all_in = jnp.concatenate([line_in, grid.across(line_in)], axis=0)

    def by_group(own, other):
        got = grid.across(other)
        return jnp.where(core == 0, jnp.concatenate([own, got]), jnp.concatenate([got, own]))

    def group_return(blocks):
        halves = blocks.reshape((2, group_count) + blocks.shape[1:])
        return pick(halves, core), grid.across(pick(halves, 1 - core))

    attend_columns = 2 * head_width + TILE
    output_pack = (
        output_weight.astype(BF16)
        .reshape(group_count, 2, head_width, local_width)
        .transpose(1, 0, 3, 2)
    )
    packs = pack_attend(attend_weight, gains_weight, core)
    packs = [
        jnp.concatenate([pack, pick(output_pack, member)], axis=2)
        for pack, member in zip(packs, (core, 1 - core), strict=True)
    ]
    joined_rows_here = grid.line_swap(by_group(*packs))
    attend_rows_here = joined_rows_here[..., :attend_columns]
    output_rows_here = joined_rows_here[..., attend_columns:]
    gate_pack, up_pack = pack_expand(expand_weight)
    attend_and_gains = grid.spread(attend_rows_here)
    attend_full = attend_and_gains[:, : 2 * head_width]
    gain_count = gains_weight.shape[0]
    gains_all = attend_and_gains[:, 2 * head_width :][:, :gain_count].T.astype(F32)

    gate_rows_here = grid.line_swap(after(gate_pack, joined_rows_here))
    units = gate_rows_here.shape[2]
    gate_full = grid.bulk_spread(gate_rows_here)
    shrink_pack = pack_shrink(after(shrink_weight, attend_rows_here))
    up_shrink_pack = jnp.concatenate([up_pack, shrink_pack], axis=2)

    normed_plain = plain_norm(all_in)
    normed_line = (normed_plain * (1.0 + gains_all[0])).astype(BF16)
    projected = jnp.dot(
        after(normed_line, gate_rows_here), attend_full, preferred_element_type=F32
    )
    up_shrink_rows_here = grid.line_swap(after(up_shrink_pack, gate_rows_here))
    up_shrink_full = grid.bulk_spread(up_shrink_rows_here)
    cosine, sine_table = rope_tables(own_spots, head_width)
    pair_pre = projected[:, head_width:]
    pair_b = jnp.where(core == 0, rotate(pair_pre, cosine, sine_table), pair_pre).astype(BF16)
    pair_parts = grid.plane_gather(grid.first_half(pair_b))
    queries_b = rotate(projected[:, :head_width], cosine, sine_table).astype(BF16)
    pair_all = jnp.zeros((grid.plane,) + pair_b.shape, BF16)
    for mask, part in pair_parts.items():
        pair_all = put(pair_all, part, grid.place_of(mask))
    pair_all = pair_all.reshape(-1, head_width)
    pair_other = grid.across(pair_all)

    output_full = grid.spread(after(output_rows_here, pair_parts[3]))

    keys_b = jnp.where(core == 0, pair_all, pair_other)
    values_b = jnp.where(core == 0, pair_other, pair_all)
    row_total, summed, mixed_b = attend_forward(queries_b, keys_b, values_b, own_spots, key_spots)

    def halves_last(*pairs):
        other = sum(dot_last(left[half:], right) for left, right in pairs).astype(BF16)
        own = sum(dot_last(after(left[:half], other), right) for left, right in pairs)
        return own, other

    attend_sum = grid.token_reduce(*halves_last((after(mixed_b, up_shrink_rows_here), output_full)))

    hidden = own_in.astype(F32)
    first_sum = hidden + norm_apply(attend_sum, gains_all[1])
    normed_two_b = norm_apply(first_sum, gains_all[2]).astype(BF16)
    normed_two_line = grid.token_gather(normed_two_b, gate_full)
    gate_act, up_act, inner_b = gate_and_up(normed_two_line, gate_full, up_shrink_full)
    up_full, shrink_full = up_shrink_full[:, :units], up_shrink_full[:, units:]
    feed_sum = grid.token_reduce(*halves_last((inner_b, shrink_full)))
    own_hidden_out = (first_sum + norm_apply(feed_sum, gains_all[3])).astype(BF16)

    grad_out = own_out.astype(F32)
    grad_feed, gain_four = norm_back(feed_sum, gains_all[3], grad_out)
    grad_feed_line = grid.token_gather(grad_feed.astype(BF16))
    shrink_terms = dot_rows(grad_feed_line, inner_b).astype(BF16)
    shrink_sums = grid.bulk_sum(shrink_terms)
    grad_both_b = gate_and_up_back(after(grad_feed_line, shrink_terms), gate_act, up_act, up_shrink_full)
    expand_terms = dot_rows(normed_two_line, grad_both_b).astype(BF16)
    expand_sums = grid.bulk_sum(expand_terms)
    grad_both_b = after(grad_both_b, expand_terms)
    grad_two_parts = halves_last(
        (grad_both_b[:, :units], gate_full), (grad_both_b[:, units:], up_full)
    )
    grad_two = grid.token_reduce(*grad_two_parts)

    grad_first_norm, gain_three = norm_back(first_sum, gains_all[2], grad_two)
    grad_first = grad_out + grad_first_norm
    grad_attend, gain_two = norm_back(attend_sum, gains_all[1], grad_first)
    grad_attend_line = grid.token_gather(grad_attend.astype(BF16))
    grad_mixed = jnp.dot(grad_attend_line, output_full, preferred_element_type=F32)
    grad_query, kept, given = attend_backward(
        queries_b, keys_b, values_b, own_spots, key_spots, row_total, summed, grad_mixed, core
    )
    pair_terms = kept + grid.across(given).astype(F32)
    pair_terms = pair_terms.astype(BF16).reshape(grid.plane, line_rows, head_width)
    pair_grad = grid.plane_reduce(
        {m: pick(pair_terms, grid.place_of(m)) for m in range(grid.plane)}
    )
    pair_grad = grid.first_half(pair_grad)
    output_terms = dot_rows(grad_attend_line, mixed_b).astype(BF16)
    grad_query_pre = rotate(grad_query, cosine, -sine_table)
    grad_pair_pre = jnp.where(core == 0, rotate(pair_grad, cosine, -sine_table), pair_grad)
    grad_proj_b = jnp.concatenate([grad_query_pre, grad_pair_pre], axis=1).astype(BF16)
    shrink_back = grid.line_swap(shrink_sums)
    own_part, other_part = halves_last((after(grad_proj_b, shrink_back), attend_full))
    gain_one = jnp.sum(own_part * normed_plain[:half], axis=0) + jnp.sum(
        other_part.astype(F32) * normed_plain[half:], axis=0
    )
    grad_normed = grid.token_reduce(own_part, other_part)
    own_hidden_grad = last_grad(own_in, gains_all[0], grad_normed, grad_first)
    expand_back = grid.line_swap(after(expand_sums, shrink_back))

    gain_terms = jnp.stack([gain_one, gain_two, gain_three, gain_four], axis=1)
    gain_terms = jnp.pad(gain_terms, ((0, 0), (2 * head_width, TILE - gain_count)))
    attend_terms = dot_rows(normed_line, jnp.pad(grad_proj_b, ((0, 0), (0, TILE)))) + gain_terms
    joined_terms = jnp.concatenate([attend_terms.astype(BF16), output_terms], axis=1)
    joined_sums = grid.bulk_sum(joined_terms)
    joined = grid.line_swap(after(joined_sums, expand_back))
    attend_line = joined[..., :attend_columns]
    output_back = group_return(joined[..., attend_columns:])
    attend_back = group_return(attend_line)
    gain_parts = attend_line[:, :, 2 * head_width : 2 * head_width + gain_count]
    gains_grad = jnp.sum(gain_parts.astype(F32), axis=0).T
    gains_grad = gains_grad + grid.across(gains_grad)

    def both_halves(value):
        other = grid.across(value)
        return jnp.where(
            core == 0, jnp.concatenate([value, other]), jnp.concatenate([other, value])
        )

    hidden_out = both_halves(own_hidden_out)
    hidden_grad = both_halves(own_hidden_grad)

    shrink_new = adam_shrink(shrink_weight, shrink_moment, shrink_square, shrink_back)
    expand_new = adam_expand(expand_weight, expand_moment, expand_square, expand_back)
    attend_new = adam_attend(
        attend_weight, attend_moment, attend_square, attend_back[0], attend_back[1], core
    )
    output_heads = jnp.where(core == 0, jnp.stack(output_back), jnp.stack(output_back[::-1]))
    output_grad = output_heads.transpose(1, 0, 3, 2).reshape(output_weight.shape).astype(F32)
    output_new = adam_step(
        output_weight, output_moment, output_square, output_grad, RATE_MATRIX, DECAY
    )
    gains_new = adam_step(
        gains_weight, gains_moment, gains_square, gains_grad, RATE_GAIN, 0.0
    )
    return (
        hidden_out,
        hidden_grad,
        *attend_new,
        output_grad,
        *output_new,
        *expand_new,
        *shrink_new,
        gains_grad,
        *gains_new,
    )


def solution(mesh):
    count, cores = mesh.shape["ctx"], mesh.shape["head"]
    devices = mesh.devices.reshape(LINES, count // LINES, cores)
    fine = Mesh(devices, ("line", "place", "head"))
    ctx = ("line", "place")
    tokens = P(ctx, None)
    attend = P(ctx, "head", None, None)
    output = P("head", None, ctx)
    expand = P(ctx, None, "head")
    shrink = P("head", ctx)
    gains = P(None, ctx)
    in_specs = (tokens, tokens, P()) + sum(
        ((spec,) * 3 for spec in (attend, output, expand, shrink, gains)), ()
    )
    out_specs = (tokens, tokens) + sum(
        ((spec,) * 4 for spec in (attend, output, expand, shrink, gains)), ()
    )
    return jax.shard_map(body, mesh=fine, in_specs=in_specs, out_specs=out_specs, check_vma=False)
```
